128 devices in a mesh: gx: 8 (over y, core), gy: 16 (over x, z).
Axes of the slice: x: 4, y: 4, z: 4, core: 2. Of those that a mesh axis runs over, the one named last changes fastest.
Arguments:
- control: float32 [3, 512, 2048], P(None, 'gy', 'gx'), may hold values from -2 to 2
- perts: float32 [16, 3, 512, 2048], P(None, None, 'gy', 'gx'), may hold values from -2.8 to 2.8
Outputs:
- basis: float32 [16, 3, 512, 2048], P(None, None, 'gy', 'gx')
- rfactor: float32 [16, 16], replicated
The draws below stay inside these ranges and needn't reach their ends.
All inputs are finite; a program needn't handle non-finite values.
Results may differ from the reference program's by a relative error of at most 0.0003.
Values sent between devices are 32-bit elements; how exact they have to be, the bound alone decides.
A program may use at most 64 MiB of HBM per device.

```python
import math
import jax
import jax.numpy as jnp
from jax import lax

MEMBERS = 16
STEPS = 2
NY = 512
NX = 2048


def draw_perts(key, part):
    keys = jax.random.split(jax.random.fold_in(key, 17), 4)
    exponent = jax.random.uniform(keys[3], (MEMBERS, 1, 1, 1), jnp.float32, 0.0, 1.0)
    scales = 0.05 * jnp.power(10.0, exponent)
    weight_matrix = jax.random.uniform(keys[2], (MEMBERS, 1, 1, 1), jnp.float32, -1.0, 1.0)
    noise = jnp.clip(jax.random.normal(keys[0], (MEMBERS, 3, NY, NX), jnp.float32), -4.0, 4.0)
    common = jnp.clip(jax.random.normal(keys[1], (1, 3, NY, NX), jnp.float32), -4.0, 4.0)
    field = 0.6 * noise + 0.8 * weight_matrix * common
    return (scales * field).astype(jnp.float32)


def steps_of(stream_key, shape, pieces, least, largest):
    def one(axis_at, blocks):
        steps = jax.random.uniform(jax.random.fold_in(jax.random.fold_in(stream_key, 6), axis_at), (blocks,), jnp.float32, least / len(pieces), largest / len(pieces))
        return jnp.repeat(jnp.exp(steps), shape[axis_at] // blocks).reshape((-1,) + (1,) * (len(shape) - axis_at - 1))

    gain = one(*pieces[0])
    for cut in pieces[1:]:
        gain = gain * one(*cut)
    return gain


def centred(rng, dims, deviation, reach, shards=(), kind=jnp.bfloat16):
    array = jax.random.normal(rng, dims, jnp.float32) * deviation
    if len(shards) > 0:
        array = steps_of(rng, dims, shards, -0.22, 0.18) * array
    return jnp.clip(array, min=-reach, max=reach).astype(kind)


def setup_inputs(seed: int = 0) -> dict:
    streams_of = jax.random.split(jax.random.key(seed), 3)
    return {
        "control": centred(streams_of[0], (3, NY, NX), 0.5, 2.0, ((1, 16), (2, 8)), jnp.float32),
        "perts": draw_perts(jax.random.fold_in(streams_of[2], 71), 0),
    }


mean_depth = 4.0
gravity = 1.0
coriolis_mid = 0.5
time_step = 0.1
two_pi = 2.0 * math.pi

def slope_x(field):
    return (8.0 * (jnp.roll(field, -1, -1) - jnp.roll(field, 1, -1)) - (jnp.roll(field, -2, -1) - jnp.roll(field, 2, -1))) / 12.0

def slope_y(field):
    return (8.0 * (jnp.roll(field, -1, -2) - jnp.roll(field, 1, -2)) - (jnp.roll(field, -2, -2) - jnp.roll(field, 2, -2))) / 12.0

def tendency(model_state, coriolis_parameter):
    height, east_wind, north_wind = (model_state[0], model_state[1], model_state[2])
    depth = mean_depth + height
    change_h = -(slope_x(depth * east_wind) + slope_y(depth * north_wind))
    change_e = -(east_wind * slope_x(east_wind) + north_wind * slope_y(east_wind)) + coriolis_parameter * north_wind - gravity * slope_x(height)
    change_n = -(east_wind * slope_x(north_wind) + north_wind * slope_y(north_wind)) - coriolis_parameter * east_wind - gravity * slope_y(height)
    return jnp.stack([change_h, change_e, change_n], 0)

def prediction_state(model_state, coriolis_parameter):
    for step in range(STEPS):
        first = tendency(model_state, coriolis_parameter)
        middle = model_state + time_step * first
        second = tendency(middle, coriolis_parameter)
        model_state = model_state + 0.5 * time_step * (first + second)
    return model_state

def reference(control, perts):
    rows = jnp.arange(NY).astype(jnp.float32)
    coriolis_parameter = (coriolis_mid * (1.0 + 0.5 * jnp.sin(two_pi * rows / float(NY))))[:, None]
    control_prediction = prediction_state(control, coriolis_parameter)

    def member(perturbation_field):
        return prediction_state(control + perturbation_field, coriolis_parameter) - control_prediction
    bred = lax.map(member, perts)
    flat = bred.reshape(MEMBERS, -1)
    gram = jnp.dot(flat, flat.T, precision=lax.Precision.HIGHEST)
    lower = jnp.linalg.cholesky(gram)
    solved = jax.scipy.linalg.solve_triangular(lower, flat, lower=True)
    domain_length = 3 * NY * NX
    basis = (math.sqrt(domain_length) * solved).reshape(perts.shape)
    rfactor = lower.T / math.sqrt(domain_length)
    return (basis, rfactor)
```

```python
import functools
import math

import jax
import jax.numpy as jnp
from jax import lax
from jax.experimental import pallas as pl
from jax.experimental.pallas import tpu as pltpu
from jax.sharding import PartitionSpec as P

MESH = pl.DeviceIdType.MESH
HALO = 8
STEPS = 2
MEAN_DEPTH = 4.0
TIME_STEP = 0.1
HIGHEST = lax.Precision.HIGHEST


def slope(minus2, minus1, plus1, plus2):
    return (plus1 - minus1) - 0.125 * (plus2 - minus2)


def kernel(
    nx_dev, ny_dev, members, rows, cols,
    ctrl_hbm, perts_hbm, basis_ref, rfac_ref,
    st, pk, halo, nat, now, mid, cini, cfin, cor, fin, red1, red2,
    in_sem, y_send, y_recv, x_send, x_recv, r1_send, r1_recv, r2_send, r2_recv,
):
    gx, gy = lax.axis_index("gx"), lax.axis_index("gy")
    ext = rows + 2 * HALO
    tall = ext // 8
    states = members + 1
    lane = lax.broadcasted_iota(jnp.int32, (8, 128), 1)
    sub = lax.broadcasted_iota(jnp.int32, (8, 128), 0)
    left, right = lax.rem(gx + nx_dev - 1, nx_dev), lax.rem(gx + 1, nx_dev)
    up, down = lax.rem(gy + ny_dev - 1, ny_dev), lax.rem(gy + 1, ny_dev)

    def own_copy(k):
        source = ctrl_hbm if k == 0 else perts_hbm.at[pl.ds((k - 1) * 4, 4)]
        target = st.at[0] if k == 0 else st.at[pl.ds((k - 1) * 4 + 1, 4)]
        if k == 0:
            return pltpu.make_async_copy(source, target.at[:, pl.ds(HALO, rows), :], in_sem.at[k])
        return pltpu.make_async_copy(source, target.at[:, :, pl.ds(HALO, rows), :], in_sem.at[k])

    for k in range(members // 4 + 1):
        own_copy(k).start()

    barrier = pltpu.get_barrier_semaphore()
    greeted = []
    for d in range(1, nx_dev):
        greeted.append((lax.rem(gx + d, nx_dev), gy))
    for d in range(1, ny_dev):
        greeted.append((gx, lax.rem(gy + d, ny_dev)))
    for a in (left, right):
        for b in (up, down):
            greeted.append((a, b))
    for peer in greeted:
        pl.semaphore_signal(barrier, inc=1, device_id=peer, device_id_type=MESH)

    grid_rows = rows * ny_dev
    for t in range(tall):
        row = lax.rem(gy * rows - HALO + tall * sub + t + grid_rows, grid_rows).astype(jnp.float32)
        cor[t] = 0.5 * (1.0 + 0.5 * jnp.sin(2.0 * math.pi * row / float(grid_rows)))
    cini[...] = jnp.zeros_like(cini)
    cfin[...] = jnp.zeros_like(cfin)

    pl.semaphore_wait(barrier, len(greeted))

    def y_copies(k, field_ref):
        return (
            pltpu.make_async_remote_copy(
                field_ref.at[:, pl.ds(0, HALO), :],
                st.at[k, :, pl.ds(HALO + rows, HALO), :],
                y_send.at[0, k], y_recv.at[0, k], device_id=(gx, up), device_id_type=MESH),
            pltpu.make_async_remote_copy(
                field_ref.at[:, pl.ds(rows - HALO, HALO), :],
                st.at[k, :, pl.ds(0, HALO), :],
                y_send.at[1, k], y_recv.at[1, k], device_id=(gx, down), device_id_type=MESH),
        )

    for copy in y_copies(0, ctrl_hbm):
        copy.start()

    @pl.loop(0, members)
    def _(m):
        for copy in y_copies(m + 1, perts_hbm.at[m]):
            copy.start()

    for k in range(members // 4 + 1):
        own_copy(k).wait()

    wide = lax.broadcasted_iota(jnp.int32, (rows, 128), 1) // 8

    @pl.loop(0, 3)
    def _(f):
        first = jnp.zeros((rows, 128), jnp.float32)
        last = jnp.zeros((rows, 128), jnp.float32)
        for m in range(members):
            head = st[m + 1, f, HALO : HALO + rows, 0:128]
            tail = st[m + 1, f, HALO : HALO + rows, cols - 128 : cols]
            first = jnp.where(wide == m, pltpu.roll(head, (8 * m) % 128, 1), first)
            last = jnp.where(wide == m, pltpu.roll(tail, (8 * m + 8) % 128, 1), last)
        pk[0, 0, f] = first
        pk[1, 0, f] = last
        pk[0, 1, f] = st[0, f, HALO : HALO + rows, 0:128]
        pk[1, 1, f] = pltpu.roll(st[0, f, HALO : HALO + rows, cols - 128 : cols], 8, 1)

    def x_copies():
        out = []
        for side, x_to in ((0, left), (1, right)):
            for place, (start, count, to, y_to) in enumerate(
                ((0, rows, HALO, gy), (0, HALO, HALO + rows, up), (rows - HALO, HALO, 0, down))
            ):
                out.append(
                    pltpu.make_async_remote_copy(
                        pk.at[side, :, :, pl.ds(start, count), :],
                        halo.at[side, :, :, pl.ds(to, count), :],
                        x_send.at[side, place], x_recv.at[side, place],
                        device_id=(x_to, y_to), device_id_type=MESH)
                )
        return out

    sent = x_copies()
    for copy in sent:
        copy.start()
    for copy in sent:
        copy.wait()

    def shifted(planes, d):
        turned = [pltpu.roll(p, (-d) % 128, 1) for p in planes]
        n = len(planes)
        if d > 0:
            return [jnp.where(lane < 128 - d, turned[i], turned[(i + 1) % n]) for i in range(n)]
        return [jnp.where(lane >= -d, turned[i], turned[(i - 1) % n]) for i in range(n)]

    def slope_x(planes):
        return [slope(*z) for z in zip(shifted(planes, -2), shifted(planes, -1), shifted(planes, 1), shifted(planes, 2))]

    def put(ref, f, t, i, value):
        ref[f, t + 2, i] = value
        if t < 2:
            ref[f, t + 2 + tall, i] = pltpu.roll(value, 7, 0)
        if t >= tall - 2:
            ref[f, t + 2 - tall, i] = pltpu.roll(value, 1, 0)

    def put_state(ref, t, i, h, e, n):
        put(ref, 0, t, i, h)
        put(ref, 1, t, i, e)
        put(ref, 2, t, i, n)
        put(ref, 3, t, i, (MEAN_DEPTH + h) * n)

    def changes(ref, t):
        h = [ref[0, t + 2, i] for i in range(3)]
        e = [ref[1, t + 2, i] for i in range(3)]
        n = [ref[2, t + 2, i] for i in range(3)]
        de = [(MEAN_DEPTH + a) * b for a, b in zip(h, e)]
        hx, ex, nx, dex = slope_x(h), slope_x(e), slope_x(n), slope_x(de)
        c = cor[t]
        out = []
        for i in range(3):
            hy, ey, ny, dny = (slope(ref[f, t, i], ref[f, t + 1, i], ref[f, t + 3, i], ref[f, t + 4, i]) for f in range(4))
            out.append((
                h[i], e[i], n[i],
                dex[i] + dny,
                e[i] * ex[i] + n[i] * ey + hx[i],
                e[i] * nx[i] + n[i] * ny + hy,
                c * n[i], c * e[i],
            ))
        return out

    full, half = TIME_STEP * (2.0 / 3.0), 0.5 * TIME_STEP * (2.0 / 3.0)

    @pl.loop(0, states)
    def _(k):
        m = jnp.maximum(k - 1, 0)
        tile = jnp.where(k == 0, 1, 0)
        for copy in y_copies(k, ctrl_hbm):
            copy.wait_recv()
        to_right = lax.rem(128 - 8 * m, 128)
        to_left = lax.rem(128 + 120 - 8 * m, 128)
        for f in range(3):
            for i in range(2):
                nat[f, i] = st[k, f, :, 128 * i : 128 * (i + 1)]
        for t in range(tall):
            pick = pl.ds(t, 8, stride=tall)
            planes = []
            for f in range(3):
                after = pltpu.roll(halo[0, tile, f, pick, :], to_right, 1)
                before = pltpu.roll(halo[1, tile, f, pick, :], to_left, 1)
                planes.append((
                    cini[f, t, 0] + nat[f, 0, pick, :],
                    cini[f, t, 1] + nat[f, 1, pick, :],
                    cini[f, t, 2] + jnp.where(lane < 64, after, before),
                ))
            for i in range(3):
                put_state(now, t, i, planes[0][i], planes[1][i], planes[2][i])

        @pl.when(k == 0)
        def _():
            for f in range(3):
                cini[f] = now[f, 2 : 2 + tall]

        @pl.loop(0, STEPS)
        def _(step):
            for t in range(tall):
                for i, (h, e, n, th, te, tn, cn, ce) in enumerate(changes(now, t)):
                    put_state(mid, t, i, h - full * th, e - full * te + TIME_STEP * cn, n - full * tn - TIME_STEP * ce)
            for t in range(tall):
                for i, (h, e, n, th, te, tn, cn, ce) in enumerate(changes(mid, t)):
                    put_state(
                        now, t, i,
                        0.5 * (now[0, t + 2, i] + h) - half * th,
                        0.5 * (now[1, t + 2, i] + e) - half * te + (0.5 * TIME_STEP) * cn,
                        0.5 * (now[2, t + 2, i] + n) - half * tn - (0.5 * TIME_STEP) * ce,
                    )

        for f in range(3):
            for t in range(tall):
                for i in range(2):
                    fin[k, f, i, pl.ds(t, 8, stride=tall), :] = now[f, t + 2, i] - cfin[f, t, i]

        @pl.when(k == 0)
        def _():
            for f in range(3):
                for i in range(2):
                    cfin[f, :, i] = now[f, 2 : 2 + tall, i]

    @pl.loop(0, states)
    def _(k):
        for copy in y_copies(k, ctrl_hbm):
            copy.wait_send()

    block = 8 * members

    def piece(f, r):
        both = [fin[1:, f, i, pl.ds(pl.multiple_of(HALO + 8 * r, 8), 8), :].reshape(block, 128) for i in range(2)]
        return jnp.concatenate(both, axis=1)

    def add_piece(j, total):
        x = piece(j // (rows // 8), lax.rem(j, rows // 8))
        return total + lax.dot_general(x, x, (((1,), (1,)), ((), ())), precision=HIGHEST, preferred_element_type=jnp.float32)

    pieces = 3 * rows // 8
    total = lax.fori_loop(0, pieces, add_piece, jnp.zeros((block, block), jnp.float32))
    r_id = lax.broadcasted_iota(jnp.int32, (block, block), 0)
    c_id = lax.broadcasted_iota(jnp.int32, (block, block), 1)
    same = lax.rem(r_id, 8) == lax.rem(c_id, 8)
    total = jnp.where(same, total, 0.0)
    total = jnp.sum(total.reshape(members, 8, block), axis=1)
    g_id = lax.broadcasted_iota(jnp.int32, (block, 128), 0) // 8
    l_id = lax.broadcasted_iota(jnp.int32, (block, 128), 1)
    gather = jnp.where(g_id == l_id, 1.0, 0.0)
    gram = jnp.dot(total, gather, precision=HIGHEST, preferred_element_type=jnp.float32)

    def all_sum(value, buf, me, count, peer_of, send, recv):
        buf[me] = value
        copies = []
        for d in range(1, count):
            copies.append(
                pltpu.make_async_remote_copy(
                    buf.at[me], buf.at[me], send.at[d], recv.at[d],
                    device_id=peer_of(lax.rem(me + d, count)), device_id_type=MESH)
            )
        for copy in copies:
            copy.start()
        for copy in copies:
            copy.wait_recv()
        out = buf[0]
        for d in range(1, count):
            out = out + buf[d]
        return out, copies

    packed = jnp.where(lane < members, gram[0:8], pltpu.roll(gram[8:16], members, 1))
    packed, sent1 = all_sum(packed, red1, gx, nx_dev, lambda i: (i, gy), r1_send, r1_recv)
    packed, sent2 = all_sum(packed, red2, gy, ny_dev, lambda i: (gx, i), r2_send, r2_recv)
    for copy in sent1 + sent2:
        copy.wait_send()
    gram = jnp.concatenate([packed, pltpu.roll(packed, 128 - members, 1)], axis=0)

    row_id = lax.broadcasted_iota(jnp.int32, (members, 128), 0)
    col_id = lax.broadcasted_iota(jnp.int32, (members, 128), 1)
    work = jnp.where(col_id < members, gram, jnp.where(col_id - members == row_id, 1.0, 0.0))
    for k in range(members):
        column = jnp.sum(jnp.where(col_id == k, work, 0.0), axis=1, keepdims=True)
        pivot = jnp.sqrt(column[k : k + 1])
        row = work[k : k + 1] / pivot
        factor = column / pivot
        work = jnp.where(row_id > k, work - factor * row, jnp.where(row_id == k, row, work))
    length = float(3 * grid_rows * cols * nx_dev)
    rfac_ref[...] = jnp.where(row_id <= col_id, work * (1.0 / math.sqrt(length)), 0.0)[:, :members]

    inverse = pltpu.roll(work, 128 - members, 1) * math.sqrt(length)
    s_id = lax.broadcasted_iota(jnp.int32, (128, block), 0)
    e_id = lax.broadcasted_iota(jnp.int32, (128, block), 1) // 8
    spread = jnp.where(s_id == e_id, 1.0, 0.0)
    big = jnp.dot(inverse, spread, precision=HIGHEST, preferred_element_type=jnp.float32)
    big = jnp.broadcast_to(big[:, None, :], (members, 8, block)).reshape(block, block)
    big = jnp.where(same & (r_id // 8 >= c_id // 8), big, 0.0)

    @pl.loop(0, pieces)
    def _(j):
        f, r = j // (rows // 8), lax.rem(j, rows // 8)
        y = jnp.dot(big, piece(f, r), precision=HIGHEST, preferred_element_type=jnp.float32)
        basis_ref[:, f, pl.ds(pl.multiple_of(8 * r, 8), 8), :] = y.reshape(members, 8, cols)


def body(control, perts):
    nx_dev, ny_dev = lax.axis_size("gx"), lax.axis_size("gy")
    members, _, rows, cols = perts.shape
    states, ext = members + 1, rows + 2 * HALO
    tall = ext // 8
    f32 = jnp.float32
    dma = pltpu.SemaphoreType.DMA
    return pl.pallas_call(
        functools.partial(kernel, nx_dev, ny_dev, members, rows, cols),
        out_shape=(
            jax.ShapeDtypeStruct(perts.shape, f32),
            jax.ShapeDtypeStruct((members, members), f32),
        ),
        in_specs=[pl.BlockSpec(memory_space=pl.ANY)] * 2,
        out_specs=[pl.BlockSpec(memory_space=pltpu.VMEM)] * 2,
        scratch_shapes=[
            pltpu.VMEM((states, 3, ext, cols), f32),
            pltpu.VMEM((2, 2, 3, rows, 128), f32),
            pltpu.VMEM((2, 2, 3, ext, 128), f32),
            pltpu.VMEM((3, 2, ext, 128), f32),
            pltpu.VMEM((4, tall + 4, 3, 8, 128), f32),
            pltpu.VMEM((4, tall + 4, 3, 8, 128), f32),
            pltpu.VMEM((3, tall, 3, 8, 128), f32),
            pltpu.VMEM((3, tall, 2, 8, 128), f32),
            pltpu.VMEM((tall, 8, 128), f32),
            pltpu.VMEM((states, 3, 2, ext, 128), f32),
            pltpu.VMEM((nx_dev, 8, 128), f32),
            pltpu.VMEM((ny_dev, 8, 128), f32),
            dma((members // 4 + 1,)),
            dma((2, states)),
            dma((2, states)),
            dma((2, 3)),
            dma((2, 3)),
            dma((nx_dev,)),
            dma((nx_dev,)),
            dma((ny_dev,)),
            dma((ny_dev,)),
        ],
        compiler_params=pltpu.CompilerParams(
            collective_id=0, has_side_effects=True, vmem_limit_bytes=40 * 1024 * 1024
        ),
    )(control, perts)


def solution(mesh):
    in_specs = (P(None, "gy", "gx"), P(None, None, "gy", "gx"))
    out_specs = (P(None, None, "gy", "gx"), P())
    return jax.shard_map(body, mesh=mesh, in_specs=in_specs, out_specs=out_specs, check_vma=False)
```

```python
import functools
import math

import jax
import jax.numpy as jnp
from jax import lax
from jax.experimental import pallas as pl
from jax.experimental.pallas import tpu as pltpu
from jax.sharding import PartitionSpec as P

MESH = pl.DeviceIdType.MESH
HALO = 8
STEPS = 2
MEAN_DEPTH = 4.0
TIME_STEP = 0.1
SCALE = TIME_STEP * (2.0 / 3.0)
HIGHEST = lax.Precision.HIGHEST


def kernel(
    nx_dev, ny_dev, members, rows, cols,
    ctrl_hbm, perts_hbm, basis_ref, rfac_ref,
    st, pk, halo, nat, band, now, mid, cini, cfin, cor, fin, parts, red1, red2,
    in_sem, y_send, y_recv, x_send, x_recv, r1_send, r1_recv, r2_send, r2_recv,
):
    gx, gy = lax.axis_index("gx"), lax.axis_index("gy")
    ext = rows + 2 * HALO
    tall = ext // 8
    pairs = members // 2 + 1
    lane = lax.broadcasted_iota(jnp.int32, (8, 128), 1)
    sub = lax.broadcasted_iota(jnp.int32, (8, 128), 0)
    left, right = lax.rem(gx + nx_dev - 1, nx_dev), lax.rem(gx + 1, nx_dev)
    up, down = lax.rem(gy + ny_dev - 1, ny_dev), lax.rem(gy + 1, ny_dev)

    def own_copy(k):
        source = ctrl_hbm if k == 0 else perts_hbm.at[pl.ds((k - 1) * 4, 4)]
        target = st.at[0] if k == 0 else st.at[pl.ds((k - 1) * 4 + 1, 4)]
        if k == 0:
            return pltpu.make_async_copy(source, target.at[:, pl.ds(HALO, rows), :], in_sem.at[k])
        return pltpu.make_async_copy(source, target.at[:, :, pl.ds(HALO, rows), :], in_sem.at[k])

    for k in range(members // 4 + 1):
        own_copy(k).start()

    barrier = pltpu.get_barrier_semaphore()
    greeted = []
    for d in range(1, nx_dev):
        greeted.append((lax.rem(gx + d, nx_dev), gy))
    for d in range(1, ny_dev):
        greeted.append((gx, lax.rem(gy + d, ny_dev)))
    for a in (left, right):
        for b in (up, down):
            greeted.append((a, b))
    for peer in greeted:
        pl.semaphore_signal(barrier, inc=1, device_id=peer, device_id_type=MESH)

    grid_rows = rows * ny_dev
    for t in range(tall):
        row = lax.rem(gy * rows - HALO + tall * sub + t + grid_rows, grid_rows).astype(jnp.float32)
        cor[t] = TIME_STEP * 0.5 * (1.0 + 0.5 * jnp.sin(2.0 * math.pi * row / float(grid_rows)))
    cini[...] = jnp.zeros_like(cini)
    cfin[...] = jnp.zeros_like(cfin)

    for k in range(members // 4 + 1):
        own_copy(k).wait()

    wide = lax.broadcasted_iota(jnp.int32, (rows, 128), 1) // 8

    @pl.loop(0, 3)
    def _(f):
        first = jnp.zeros((rows, 128), jnp.float32)
        last = jnp.zeros((rows, 128), jnp.float32)
        for m in range(members):
            head = st[m + 1, f, HALO : HALO + rows, 0:128]
            tail = st[m + 1, f, HALO : HALO + rows, cols - 128 : cols]
            both = pltpu.roll(jnp.where(wide < 8, head, tail), (8 * m) % 128, 1)
            first = jnp.where(wide == m, both, first)
            last = jnp.where(wide == (m + 15) % 16, both, last)
        pk[0, 0, f] = first
        pk[1, 0, f] = last
        pk[0, 1, f] = st[0, f, HALO : HALO + rows, 0:128]
        pk[1, 1, f] = st[0, f, HALO : HALO + rows, cols - 128 : cols]

    def x_copies():
        out = []
        for side, x_to in ((0, left), (1, right)):
            for place, (start, count, to, y_to) in enumerate(
                ((0, rows, HALO, gy), (0, HALO, HALO + rows, up), (rows - HALO, HALO, 0, down))
            ):
                out.append(
                    pltpu.make_async_remote_copy(
                        pk.at[side, :, :, pl.ds(start, count), :],
                        halo.at[side, :, :, pl.ds(to, count), :],
                        x_send.at[side, place], x_recv.at[side, place],
                        device_id=(x_to, y_to), device_id_type=MESH)
                )
        return out

    pl.semaphore_wait(barrier, len(greeted))
    for copy in x_copies():
        copy.start()

    def y_copies(p, field_ref, st_ref):
        lead = (slice(None),) * (len(field_ref.shape) - 2)
        return [
            pltpu.make_async_remote_copy(
                field_ref.at[lead + (pl.ds(start, HALO),)],
                st_ref.at[lead + (pl.ds(to, HALO),)],
                y_send.at[way, p], y_recv.at[way, p], device_id=(gx, y_to), device_id_type=MESH)
            for way, (start, to, y_to) in enumerate(((0, HALO + rows, up), (rows - HALO, 0, down)))
        ]

    def control_y():
        return y_copies(0, ctrl_hbm, st.at[0])

    def pair_y(p):
        return y_copies(p, perts_hbm.at[pl.ds(2 * p - 2, 2)], st.at[pl.ds(2 * p - 1, 2)])

    for copy in control_y():
        copy.start()

    @pl.loop(1, pairs)
    def _(p):
        for copy in pair_y(p):
            copy.start()

    for copy in x_copies():
        copy.wait()

    k_id = lax.rem(lax.broadcasted_iota(jnp.int32, (256, 128), 0), 128)
    ahead = lax.rem(k_id - lax.broadcasted_iota(jnp.int32, (256, 128), 1) + 128, 128)
    weights = jnp.where(ahead == 1, 1.0, jnp.where(ahead == 127, -1.0, 0.0))
    weights = jnp.where(ahead == 2, -0.125, jnp.where(ahead == 126, 0.125, weights))
    band[...] = weights.astype(jnp.bfloat16)

    def put(ref, f, i, t, value):
        ref[f, i, t + 2] = value
        if t < 2:
            ref[f, i, t + 2 + tall] = pltpu.roll(value, 7, 0)
        if t >= tall - 2:
            ref[f, i, t + 2 - tall] = pltpu.roll(value, 1, 0)

    def put_state(ref, i, t, h, e, n):
        put(ref, 0, i, t, h)
        put(ref, 1, i, t, e)
        put(ref, 2, i, t, n)
        put(ref, 3, i, t, (SCALE * SCALE * MEAN_DEPTH + h) * n)

    def slopes_x(ref, i):
        h, e, n = (ref[f, i, 2 : 2 + tall].reshape(ext, 128) for f in range(3))
        z = jnp.concatenate([h, e, n, (SCALE * SCALE * MEAN_DEPTH + h) * e], axis=0)
        top = z.astype(jnp.bfloat16)
        rest = (z - top.astype(jnp.float32)).astype(jnp.bfloat16)
        out = jnp.dot(jnp.concatenate([top, rest], axis=1), band[...], preferred_element_type=jnp.float32)
        return out.reshape(4, tall, 8, 128)

    def slope_y(ref, f, i, t):
        return (ref[f, i, t + 3] - ref[f, i, t + 1]) - 0.125 * (ref[f, i, t + 4] - ref[f, i, t])

    def forward(ref, i, t, along):
        h, e, n = ref[0, i, t + 2], ref[1, i, t + 2], ref[2, i, t + 2]
        c = cor[t]
        new_h = h - along[3, t] - slope_y(ref, 3, i, t)
        new_e = e - (e * along[1, t] + n * slope_y(ref, 1, i, t) + along[0, t]) + c * n
        new_n = n - (e * along[2, t] + n * slope_y(ref, 2, i, t) + slope_y(ref, 0, i, t)) - c * e
        return new_h, new_e, new_n

    @pl.loop(0, pairs)
    def _(p):
        @pl.when(p == 0)
        def _():
            for copy in control_y():
                copy.wait_recv()

        @pl.when(p > 0)
        def _():
            for copy in pair_y(p):
                copy.wait_recv()

        slot = jnp.where(p == 0, 1, 0)
        first = jnp.maximum(2 * p - 1, 0)
        for s, k in enumerate((first, 2 * p)):
            for f in range(3):
                for i in range(2):
                    nat[s, f, i] = st[k, f, :, 128 * i : 128 * (i + 1)]
        places = (jnp.maximum(first - 1, 0), jnp.maximum(2 * p - 1, 0))
        for f in range(3):
            scale = SCALE * SCALE if f == 0 else SCALE
            for t in range(tall):
                pick = pl.ds(t, 8, stride=tall)
                after, before = halo[0, slot, f, pick, :], halo[1, slot, f, pick, :]
                rings, middle = [], []
                for s, m in enumerate(places):
                    low, high = nat[s, f, 0, pick, :], nat[s, f, 1, pick, :]
                    beyond = pltpu.roll(jnp.where(lane // 8 == m, after, before), lax.rem(128 - 8 * m, 128), 1)
                    rings.append(jnp.where(lane < 120, low, beyond))
                    rings.append(jnp.where(lane < 8, beyond, high))
                    middle.append(jnp.where(lane < 64, high, low))
                apart = pltpu.roll(middle[1], 64, 1)
                rings.append(jnp.where((lane < 32) | (lane >= 96), middle[0], apart))
                for i in range(5):
                    now[f, i, t + 2] = cini[f, i, t] + scale * rings[i]

        @pl.when(p == 0)
        def _():
            for f in range(3):
                cini[f] = now[f, :, 2 : 2 + tall]

        for i in range(5):
            for t in range(tall):
                put_state(now, i, t, now[0, i, t + 2], now[1, i, t + 2], now[2, i, t + 2])

        @pl.loop(0, STEPS)
        def _(step):
            for i in range(5):
                along = slopes_x(now, i)
                for t in range(tall):
                    put_state(mid, i, t, *forward(now, i, t, along))
            for i in range(5):
                along = slopes_x(mid, i)
                for t in range(tall):
                    new = forward(mid, i, t, along)
                    put_state(now, i, t, *(0.5 * (now[f, i, t + 2] + new[f]) for f in range(3)))

        for f in range(3):
            scale = 1.0 / (SCALE * SCALE) if f == 0 else 1.0 / SCALE
            for t in range(tall):
                z = [scale * (now[f, i, t + 2] - cfin[f, i, t]) for i in range(5)]
                pick = pl.ds(t, 8, stride=tall)
                for s, k in enumerate((first, 2 * p)):
                    both = z[4] if s == 0 else pltpu.roll(z[4], 64, 1)
                    fin[k, f, 0, pick, :] = jnp.where(lane < 112, z[2 * s], both)
                    fin[k, f, 1, pick, :] = jnp.where(lane < 16, both, z[2 * s + 1])

        @pl.when(p == 0)
        def _():
            for f in range(3):
                cfin[f] = now[f, :, 2 : 2 + tall]

    for copy in control_y():
        copy.wait_send()

    @pl.loop(1, pairs)
    def _(p):
        for copy in pair_y(p):
            copy.wait_send()

    block = 8 * members

    def piece(f, r):
        both = [fin[1:, f, i, pl.ds(pl.multiple_of(HALO + 8 * r, 8), 8), :].reshape(block, 128) for i in range(2)]
        return jnp.concatenate(both, axis=1)

    def add_piece(j, total):
        x = piece(j // (rows // 8), lax.rem(j, rows // 8))
        top = x.astype(jnp.bfloat16)
        rest = (x - top.astype(jnp.float32)).astype(jnp.bfloat16)
        x = jnp.concatenate([top, rest], axis=0)
        parts[j] = x
        return total + lax.dot_general(x, x, (((1,), (1,)), ((), ())), preferred_element_type=jnp.float32)

    pieces = 3 * rows // 8
    total = lax.fori_loop(0, pieces, add_piece, jnp.zeros((2 * block, 2 * block), jnp.float32))
    total = total[:block] + total[block:]
    total = total[:, :block] + total[:, block:]
    r_id = lax.broadcasted_iota(jnp.int32, (block, block), 0)
    c_id = lax.broadcasted_iota(jnp.int32, (block, block), 1)
    same = lax.rem(r_id, 8) == lax.rem(c_id, 8)
    total = jnp.where(same, total, 0.0)
    total = jnp.sum(total.reshape(members, 8, block), axis=1)
    g_id = lax.broadcasted_iota(jnp.int32, (block, 128), 0) // 8
    l_id = lax.broadcasted_iota(jnp.int32, (block, 128), 1)
    gather = jnp.where(g_id == l_id, 1.0, 0.0)
    gram = jnp.dot(total, gather, precision=HIGHEST, preferred_element_type=jnp.float32)

    def all_sum(value, buf, me, count, peer_of, send, recv):
        buf[me] = value
        copies = []
        for d in range(1, count):
            copies.append(
                pltpu.make_async_remote_copy(
                    buf.at[me], buf.at[me], send.at[d], recv.at[d],
                    device_id=peer_of(lax.rem(me + d, count)), device_id_type=MESH)
            )
        for copy in copies:
            copy.start()
        for copy in copies:
            copy.wait_recv()
        out = buf[0]
        for d in range(1, count):
            out = out + buf[d]
        return out, copies

    packed = jnp.where(lane < members, gram[0:8], pltpu.roll(gram[8:16], members, 1))
    packed, sent1 = all_sum(packed, red1, gx, nx_dev, lambda i: (i, gy), r1_send, r1_recv)
    packed, sent2 = all_sum(packed, red2, gy, ny_dev, lambda i: (gx, i), r2_send, r2_recv)
    for copy in sent1 + sent2:
        copy.wait_send()
    gram = jnp.concatenate([packed, pltpu.roll(packed, 128 - members, 1)], axis=0)

    row_id = lax.broadcasted_iota(jnp.int32, (members, 128), 0)
    col_id = lax.broadcasted_iota(jnp.int32, (members, 128), 1)
    work = jnp.where(col_id < members, gram, jnp.where(col_id - members == row_id, 1.0, 0.0))
    for k in range(members):
        column = jnp.sum(jnp.where(col_id == k, work, 0.0), axis=1, keepdims=True)
        pivot = jnp.sqrt(column[k : k + 1])
        row = work[k : k + 1] / pivot
        factor = column / pivot
        work = jnp.where(row_id > k, work - factor * row, jnp.where(row_id == k, row, work))
    length = float(3 * grid_rows * cols * nx_dev)
    rfac_ref[...] = jnp.where(row_id <= col_id, work * (1.0 / math.sqrt(length)), 0.0)[:, :members]

    inverse = pltpu.roll(work, 128 - members, 1) * math.sqrt(length)
    s_id = lax.broadcasted_iota(jnp.int32, (128, block), 0)
    e_id = lax.broadcasted_iota(jnp.int32, (128, block), 1) // 8
    spread = jnp.where(s_id == e_id, 1.0, 0.0)
    big = jnp.dot(inverse, spread, precision=HIGHEST, preferred_element_type=jnp.float32)
    big = jnp.broadcast_to(big[:, None, :], (members, 8, block)).reshape(block, block)
    big = jnp.where(same & (r_id // 8 >= c_id // 8), big, 0.0)

    top = big.astype(jnp.bfloat16)
    rest = (big - top.astype(jnp.float32)).astype(jnp.bfloat16)
    big = jnp.concatenate([jnp.concatenate([top, top], axis=1), jnp.concatenate([rest, rest], axis=1)], axis=0)

    @pl.loop(0, pieces)
    def _(j):
        f, r = j // (rows // 8), lax.rem(j, rows // 8)
        y = jnp.dot(big, parts[j], preferred_element_type=jnp.float32)
        y = y[:block] + y[block:]
        basis_ref[:, f, pl.ds(pl.multiple_of(8 * r, 8), 8), :] = y.reshape(members, 8, cols)


def body(control, perts):
    nx_dev, ny_dev = lax.axis_size("gx"), lax.axis_size("gy")
    members, _, rows, cols = perts.shape
    states, ext = members + 1, rows + 2 * HALO
    tall = ext // 8
    f32 = jnp.float32
    dma = pltpu.SemaphoreType.DMA
    return pl.pallas_call(
        functools.partial(kernel, nx_dev, ny_dev, members, rows, cols),
        out_shape=(
            jax.ShapeDtypeStruct(perts.shape, f32),
            jax.ShapeDtypeStruct((members, members), f32),
        ),
        in_specs=[pl.BlockSpec(memory_space=pl.ANY)] * 2,
        out_specs=[pl.BlockSpec(memory_space=pltpu.VMEM)] * 2,
        scratch_shapes=[
            pltpu.VMEM((states, 3, ext, cols), f32),
            pltpu.VMEM((2, 2, 3, rows, 128), f32),
            pltpu.VMEM((2, 2, 3, ext, 128), f32),
            pltpu.VMEM((2, 3, 2, ext, 128), f32),
            pltpu.VMEM((256, 128), jnp.bfloat16),
            pltpu.VMEM((4, 5, tall + 4, 8, 128), f32),
            pltpu.VMEM((4, 5, tall + 4, 8, 128), f32),
            pltpu.VMEM((3, 5, tall, 8, 128), f32),
            pltpu.VMEM((3, 5, tall, 8, 128), f32),
            pltpu.VMEM((tall, 8, 128), f32),
            pltpu.VMEM((states, 3, 2, ext, 128), f32),
            pltpu.VMEM((3 * rows // 8, 16 * members, cols), jnp.bfloat16),
            pltpu.VMEM((nx_dev, 8, 128), f32),
            pltpu.VMEM((ny_dev, 8, 128), f32),
            dma((members // 4 + 1,)),
            dma((2, members // 2 + 1)),
            dma((2, members // 2 + 1)),
            dma((2, 3)),
            dma((2, 3)),
            dma((nx_dev,)),
            dma((nx_dev,)),
            dma((ny_dev,)),
            dma((ny_dev,)),
        ],
        compiler_params=pltpu.CompilerParams(
            collective_id=0, has_side_effects=True, vmem_limit_bytes=60 * 1024 * 1024
        ),
    )(control, perts)


def solution(mesh):
    in_specs = (P(None, "gy", "gx"), P(None, None, "gy", "gx"))
    out_specs = (P(None, None, "gy", "gx"), P())
    return jax.shard_map(body, mesh=mesh, in_specs=in_specs, out_specs=out_specs, check_vma=False)
```

```python
import functools
import math

import jax
import jax.numpy as jnp
from jax import lax
from jax.experimental import pallas as pl
from jax.experimental.pallas import tpu as pltpu
from jax.sharding import PartitionSpec as P

MESH = pl.DeviceIdType.MESH
HALO = 8
STEPS = 2
MEAN_DEPTH = 4.0
TIME_STEP = 0.1
SCALE = TIME_STEP * (2.0 / 3.0)


def kernel(
    nx_dev, ny_dev, members, rows, cols,
    ctrl_hbm, perts_hbm, fin, factor_ref,
    st, pk, halo, nat, band, now, mid, cini, cfin, cor, parts, red1, red2,
    in_sem, y_send, y_recv, x_send, x_recv, r1_send, r1_recv, r2_send, r2_recv,
):
    gx, gy = lax.axis_index("gx"), lax.axis_index("gy")
    ext = rows + 2 * HALO
    tall = ext // 8
    pairs = members // 2 + 1
    lane = lax.broadcasted_iota(jnp.int32, (8, 128), 1)
    sub = lax.broadcasted_iota(jnp.int32, (8, 128), 0)
    left, right = lax.rem(gx + nx_dev - 1, nx_dev), lax.rem(gx + 1, nx_dev)
    up, down = lax.rem(gy + ny_dev - 1, ny_dev), lax.rem(gy + 1, ny_dev)

    def own_copy(k):
        source = ctrl_hbm if k == 0 else perts_hbm.at[pl.ds((k - 1) * 4, 4)]
        target = st.at[0] if k == 0 else st.at[pl.ds((k - 1) * 4 + 1, 4)]
        if k == 0:
            return pltpu.make_async_copy(source, target.at[:, pl.ds(HALO, rows), :], in_sem.at[k])
        return pltpu.make_async_copy(source, target.at[:, :, pl.ds(HALO, rows), :], in_sem.at[k])

    for k in range(members // 4 + 1):
        own_copy(k).start()

    barrier = pltpu.get_barrier_semaphore()
    greeted = []
    for d in range(1, nx_dev):
        greeted.append((lax.rem(gx + d, nx_dev), gy))
    for d in range(1, ny_dev):
        greeted.append((gx, lax.rem(gy + d, ny_dev)))
    for a in (left, right):
        for b in (up, down):
            greeted.append((a, b))
    for peer in greeted:
        pl.semaphore_signal(barrier, inc=1, device_id=peer, device_id_type=MESH)

    grid_rows = rows * ny_dev
    for t in range(tall):
        row = lax.rem(gy * rows - HALO + tall * sub + t + grid_rows, grid_rows).astype(jnp.float32)
        cor[t] = TIME_STEP * 0.5 * (1.0 + 0.5 * jnp.sin(2.0 * math.pi * row / float(grid_rows)))
    for f in range(3):
        cini[f] = jnp.full(cini.shape[1:], SCALE * SCALE * MEAN_DEPTH if f == 0 else 0.0, jnp.float32)
    cfin[...] = jnp.zeros_like(cfin)

    for k in range(members // 4 + 1):
        own_copy(k).wait()

    wide = lax.broadcasted_iota(jnp.int32, (rows, 128), 1) // 8

    @pl.loop(0, 3)
    def _(f):
        first = jnp.zeros((rows, 128), jnp.float32)
        last = jnp.zeros((rows, 128), jnp.float32)
        for m in range(members):
            head = st[m + 1, f, HALO : HALO + rows, 0:128]
            tail = st[m + 1, f, HALO : HALO + rows, cols - 128 : cols]
            both = pltpu.roll(jnp.where(wide < 8, head, tail), (8 * m) % 128, 1)
            first = jnp.where(wide == m, both, first)
            last = jnp.where(wide == (m + 15) % 16, both, last)
        pk[0, 0, f] = first
        pk[1, 0, f] = last
        pk[0, 1, f] = st[0, f, HALO : HALO + rows, 0:128]
        pk[1, 1, f] = st[0, f, HALO : HALO + rows, cols - 128 : cols]

    def x_copies():
        out = []
        for side, x_to in ((0, left), (1, right)):
            for place, (start, count, to, y_to) in enumerate(
                ((0, rows, HALO, gy), (0, HALO, HALO + rows, up), (rows - HALO, HALO, 0, down))
            ):
                out.append(
                    pltpu.make_async_remote_copy(
                        pk.at[side, :, :, pl.ds(start, count), :],
                        halo.at[side, :, :, pl.ds(to, count), :],
                        x_send.at[side, place], x_recv.at[side, place],
                        device_id=(x_to, y_to), device_id_type=MESH)
                )
        return out

    pl.semaphore_wait(barrier, len(greeted))
    for copy in x_copies():
        copy.start()

    def y_copies(p, field_ref, st_ref):
        lead = (slice(None),) * (len(field_ref.shape) - 2)
        return [
            pltpu.make_async_remote_copy(
                field_ref.at[lead + (pl.ds(start, HALO),)],
                st_ref.at[lead + (pl.ds(to, HALO),)],
                y_send.at[way, p], y_recv.at[way, p], device_id=(gx, y_to), device_id_type=MESH)
            for way, (start, to, y_to) in enumerate(((0, HALO + rows, up), (rows - HALO, 0, down)))
        ]

    def control_y():
        return y_copies(0, ctrl_hbm, st.at[0])

    def pair_y(p):
        return y_copies(p, perts_hbm.at[pl.ds(2 * p - 2, 2)], st.at[pl.ds(2 * p - 1, 2)])

    for copy in control_y():
        copy.start()

    @pl.loop(1, pairs)
    def _(p):
        for copy in pair_y(p):
            copy.start()

    for copy in x_copies():
        copy.wait_recv()

    k_id = lax.rem(lax.broadcasted_iota(jnp.int32, (256, 128), 0), 128)
    ahead = lax.rem(k_id - lax.broadcasted_iota(jnp.int32, (256, 128), 1) + 128, 128)
    weights = jnp.where(ahead == 1, 1.0, jnp.where(ahead == 127, -1.0, 0.0))
    weights = jnp.where(ahead == 2, -0.125, jnp.where(ahead == 126, 0.125, weights))
    band[...] = weights.astype(jnp.bfloat16)

    def put(ref, f, i, t, value):
        ref[f, i, t + 2] = value
        if t < 2:
            ref[f, i, t + 2 + tall] = pltpu.roll(value, 7, 0)
        if t >= tall - 2:
            ref[f, i, t + 2 - tall] = pltpu.roll(value, 1, 0)

    def put_state(ref, i, t, h, e, n):
        put(ref, 0, i, t, h)
        put(ref, 1, i, t, e)
        put(ref, 2, i, t, n)
        put(ref, 3, i, t, h * n)

    def slopes_x(ref, i):
        h, e, n = (ref[f, i, 2 : 2 + tall].reshape(ext, 128) for f in range(3))
        z = jnp.concatenate([h, e, n, h * e], axis=0)
        top = z.astype(jnp.bfloat16)
        rest = (z - top.astype(jnp.float32)).astype(jnp.bfloat16)
        out = jnp.dot(jnp.concatenate([top, rest], axis=1), band[...], preferred_element_type=jnp.float32)
        return out.reshape(4, tall, 8, 128)

    def slope_y(ref, f, i, t):
        return (ref[f, i, t + 3] - ref[f, i, t + 1]) - 0.125 * (ref[f, i, t + 4] - ref[f, i, t])

    def forward(ref, i, t, along):
        h, e, n = ref[0, i, t + 2], ref[1, i, t + 2], ref[2, i, t + 2]
        c = cor[t]
        new_h = h - along[3, t] - slope_y(ref, 3, i, t)
        new_e = e - (e * along[1, t] + n * slope_y(ref, 1, i, t) + along[0, t]) + c * n
        new_n = n - (e * along[2, t] + n * slope_y(ref, 2, i, t) + slope_y(ref, 0, i, t)) - c * e
        return new_h, new_e, new_n

    @pl.loop(0, pairs)
    def _(p):
        @pl.when(p == 0)
        def _():
            for copy in control_y():
                copy.wait_recv()

        @pl.when(p > 0)
        def _():
            for copy in pair_y(p):
                copy.wait_recv()

        slot = jnp.where(p == 0, 1, 0)
        first = jnp.maximum(2 * p - 1, 0)
        for s, k in enumerate((first, 2 * p)):
            for f in range(3):
                for i in range(2):
                    nat[s, f, i] = st[k, f, :, 128 * i : 128 * (i + 1)]
        places = (jnp.maximum(first - 1, 0), jnp.maximum(2 * p - 1, 0))
        for f in range(3):
            scale = SCALE * SCALE if f == 0 else SCALE
            for t in range(tall):
                pick = pl.ds(t, 8, stride=tall)
                after, before = halo[0, slot, f, pick, :], halo[1, slot, f, pick, :]
                rings, middle = [], []
                for s, m in enumerate(places):
                    low, high = nat[s, f, 0, pick, :], nat[s, f, 1, pick, :]
                    beyond = pltpu.roll(jnp.where(lane // 8 == m, after, before), lax.rem(128 - 8 * m, 128), 1)
                    rings.append(jnp.where(lane < 120, low, beyond))
                    rings.append(jnp.where(lane < 8, beyond, high))
                    middle.append(jnp.where(lane < 64, high, low))
                apart = pltpu.roll(middle[1], 64, 1)
                rings.append(jnp.where((lane < 32) | (lane >= 96), middle[0], apart))
                for i in range(5):
                    now[f, i, t + 2] = cini[f, i, t] + scale * rings[i]

        @pl.when(p == 0)
        def _():
            for f in range(3):
                cini[f] = now[f, :, 2 : 2 + tall]

        for i in range(5):
            for t in range(tall):
                put_state(now, i, t, now[0, i, t + 2], now[1, i, t + 2], now[2, i, t + 2])

        @pl.loop(0, STEPS)
        def _(step):
            for i in range(5):
                along = slopes_x(now, i)
                for t in range(tall):
                    put_state(mid, i, t, *forward(now, i, t, along))
            for i in range(5):
                along = slopes_x(mid, i)
                for t in range(tall):
                    new = forward(mid, i, t, along)
                    put_state(now, i, t, *(0.5 * (now[f, i, t + 2] + new[f]) for f in range(3)))

        for f in range(3):
            scale = 1.0 / (SCALE * SCALE) if f == 0 else 1.0 / SCALE
            for t in range(tall):
                z = [scale * (now[f, i, t + 2] - cfin[f, i, t]) for i in range(5)]
                pick = pl.ds(t, 8, stride=tall)
                for s, k in enumerate((first, 2 * p)):
                    both = z[4] if s == 0 else pltpu.roll(z[4], 64, 1)
                    fin[k, f, 0, pick, :] = jnp.where(lane < 112, z[2 * s], both)
                    fin[k, f, 1, pick, :] = jnp.where(lane < 16, both, z[2 * s + 1])

        @pl.when(p == 0)
        def _():
            for f in range(3):
                cfin[f] = now[f, :, 2 : 2 + tall]

    for copy in x_copies() + control_y():
        copy.wait_send()

    @pl.loop(1, pairs)
    def _(p):
        for copy in pair_y(p):
            copy.wait_send()

    @pl.loop(0, members // 4)
    def _(a):
        @pl.loop(0, a + 1)
        def _(b):
            total = [[None] * 4 for _ in range(4)]
            for f in range(3):
                for i in range(2):
                    x = [fin[1 + 4 * a + u, f, i, HALO : HALO + rows, :] for u in range(4)]
                    y = [fin[1 + 4 * b + u, f, i, HALO : HALO + rows, :] for u in range(4)]
                    for u in range(4):
                        for v in range(4):
                            z = jnp.sum((x[u] * y[v]).reshape(rows // 8, 8, 128), axis=0)
                            total[u][v] = z if total[u][v] is None else total[u][v] + z
            for u in range(4):
                for v in range(4):
                    parts[4 * a + u, 4 * b + v] = total[u][v]
                    parts[4 * b + v, 4 * a + u] = total[u][v]

    row_id = lax.broadcasted_iota(jnp.int32, (members, 128), 0)
    col_id = lax.broadcasted_iota(jnp.int32, (members, 128), 1)
    gram = jnp.zeros((members, 128), jnp.float32)
    for m in range(members):
        sums = jnp.sum(jnp.sum(parts[m], axis=1), axis=1, keepdims=True)
        gram = jnp.where(col_id == m, sums, gram)

    def all_sum(value, buf, me, count, peer_of, send, recv):
        buf[me] = value
        copies = []
        for d in range(1, count):
            copies.append(
                pltpu.make_async_remote_copy(
                    buf.at[me], buf.at[me], send.at[d], recv.at[d],
                    device_id=peer_of(lax.rem(me + d, count)), device_id_type=MESH)
            )
        for copy in copies:
            copy.start()
        for copy in copies:
            copy.wait_recv()
        out = buf[0]
        for d in range(1, count):
            out = out + buf[d]
        return out, copies

    packed = jnp.where(lane < members, gram[0:8], pltpu.roll(gram[8:16], members, 1))
    packed, sent1 = all_sum(packed, red1, gx, nx_dev, lambda i: (i, gy), r1_send, r1_recv)
    packed, sent2 = all_sum(packed, red2, gy, ny_dev, lambda i: (gx, i), r2_send, r2_recv)
    for copy in sent1 + sent2:
        copy.wait_send()
    gram = jnp.concatenate([packed, pltpu.roll(packed, 128 - members, 1)], axis=0)

    work = jnp.where(col_id < members, gram, jnp.where(col_id - members == row_id, 1.0, 0.0))
    pivots = jnp.ones((members, 1), jnp.float32)
    for k in range(members):
        column = work[:, k : k + 1]
        pivot = column[k : k + 1]
        work = work - jnp.where(row_id > k, column, 0.0) * (work[k : k + 1] * (1.0 / pivot))
        pivots = jnp.where(row_id[:, :1] == k, pivot, pivots)
    factor_ref[...] = work / jnp.sqrt(pivots)


def apply_kernel(length, members, rows, bred, factor, basis_hbm, rfac_hbm, table, out, rout, sem):
    row_id = lax.broadcasted_iota(jnp.int32, (members, members), 0)
    col_id = lax.broadcasted_iota(jnp.int32, (members, members), 1)
    rout[...] = jnp.where(row_id <= col_id, factor[:, :members] * (1.0 / math.sqrt(length)), 0.0)
    small = pltpu.make_async_copy(rout, rfac_hbm, sem.at[3])
    small.start()
    for j in range(members):
        column = factor[:, members + j : members + j + 1] * math.sqrt(length)
        table[j] = jnp.broadcast_to(column, (members, 128))
    copies = []
    for f in range(3):
        for i in range(2):
            x = [bred[1 + j, f, i, HALO : HALO + rows, :] for j in range(members)]
            for m in range(members):
                total = table[0, m : m + 1, :] * x[0]
                for j in range(1, m + 1):
                    total = total + table[j, m : m + 1, :] * x[j]
                out[m, f, :, 128 * i : 128 * (i + 1)] = total
        copies.append(pltpu.make_async_copy(out.at[:, pl.ds(f, 1)], basis_hbm.at[:, pl.ds(f, 1)], sem.at[f]))
        copies[-1].start()
    for copy in copies + [small]:
        copy.wait()


def body(control, perts):
    nx_dev, ny_dev = lax.axis_size("gx"), lax.axis_size("gy")
    members, _, rows, cols = perts.shape
    states, ext = members + 1, rows + 2 * HALO
    tall = ext // 8
    f32 = jnp.float32
    dma = pltpu.SemaphoreType.DMA
    vmem, hbm = pl.BlockSpec(memory_space=pltpu.VMEM), pl.BlockSpec(memory_space=pltpu.HBM)
    bred, factor = pl.pallas_call(
        functools.partial(kernel, nx_dev, ny_dev, members, rows, cols),
        out_shape=(
            jax.ShapeDtypeStruct((states, 3, 2, ext, 128), f32),
            jax.ShapeDtypeStruct((members, 128), f32),
        ),
        in_specs=[hbm] * 2,
        out_specs=[vmem] * 2,
        scratch_shapes=[
            pltpu.VMEM((states, 3, ext, cols), f32),
            pltpu.VMEM((2, 2, 3, rows, 128), f32),
            pltpu.VMEM((2, 2, 3, ext, 128), f32),
            pltpu.VMEM((2, 3, 2, ext, 128), f32),
            pltpu.VMEM((256, 128), jnp.bfloat16),
            pltpu.VMEM((4, 5, tall + 4, 8, 128), f32),
            pltpu.VMEM((4, 5, tall + 4, 8, 128), f32),
            pltpu.VMEM((3, 5, tall, 8, 128), f32),
            pltpu.VMEM((3, 5, tall, 8, 128), f32),
            pltpu.VMEM((tall, 8, 128), f32),
            pltpu.VMEM((members, members, 8, 128), f32),
            pltpu.VMEM((nx_dev, 8, 128), f32),
            pltpu.VMEM((ny_dev, 8, 128), f32),
            dma((members // 4 + 1,)),
            dma((2, members // 2 + 1)),
            dma((2, members // 2 + 1)),
            dma((2, 3)),
            dma((2, 3)),
            dma((nx_dev,)),
            dma((nx_dev,)),
            dma((ny_dev,)),
            dma((ny_dev,)),
        ],
        compiler_params=pltpu.CompilerParams(
            collective_id=0, has_side_effects=True, vmem_limit_bytes=24 * 1024 * 1024
        ),
    )(control, perts)
    length = float(3 * rows * ny_dev * cols * nx_dev)
    return pl.pallas_call(
        functools.partial(apply_kernel, length, members, rows),
        out_shape=(
            jax.ShapeDtypeStruct(perts.shape, f32),
            jax.ShapeDtypeStruct((members, members), f32),
        ),
        in_specs=[vmem] * 2,
        out_specs=[hbm] * 2,
        scratch_shapes=[
            pltpu.VMEM((members, members, 128), f32),
            pltpu.VMEM((members, 3, rows, cols), f32),
            pltpu.VMEM((members, members), f32),
            dma((4,)),
        ],
        compiler_params=pltpu.CompilerParams(vmem_limit_bytes=24 * 1024 * 1024),
    )(bred, factor)


def solution(mesh):
    in_specs = (P(None, "gy", "gx"), P(None, None, "gy", "gx"))
    out_specs = (P(None, None, "gy", "gx"), P())
    return jax.shard_map(body, mesh=mesh, in_specs=in_specs, out_specs=out_specs, check_vma=False)
```

```python
import functools
import math

import jax
import jax.numpy as jnp
from jax import lax
from jax.experimental import pallas as pl
from jax.experimental.pallas import tpu as pltpu
from jax.sharding import PartitionSpec as P

MESH = pl.DeviceIdType.MESH
HALO = 8
STEPS = 2
MEAN_DEPTH = 4.0
TIME_STEP = 0.1
SCALE = TIME_STEP * (2.0 / 3.0)


def kernel(
    nx_dev, ny_dev, members, rows, cols,
    ctrl_hbm, perts_hbm, bred_hbm, factor_ref,
    st, pk, halo, band, now, mid, cini, cfin, cor, fin, parts, red1, red2,
    in_sem, out_sem, y_send, y_recv, x_send, x_recv, r1_send, r1_recv, r2_send, r2_recv,
):
    gx, gy = lax.axis_index("gx"), lax.axis_index("gy")
    ext = rows + 2 * HALO
    pairs = members // 2 + 1
    lane = lax.broadcasted_iota(jnp.int32, (8, 128), 1)
    left, right = lax.rem(gx + nx_dev - 1, nx_dev), lax.rem(gx + 1, nx_dev)
    up, down = lax.rem(gy + ny_dev - 1, ny_dev), lax.rem(gy + 1, ny_dev)

    def own_copy(k):
        source = ctrl_hbm if k == 0 else perts_hbm.at[pl.ds((k - 1) * 4, 4)]
        target = st.at[0] if k == 0 else st.at[pl.ds((k - 1) * 4 + 1, 4)]
        if k == 0:
            return pltpu.make_async_copy(source, target.at[:, pl.ds(HALO, rows), :], in_sem.at[k])
        return pltpu.make_async_copy(source, target.at[:, :, pl.ds(HALO, rows), :], in_sem.at[k])

    barrier = pltpu.get_barrier_semaphore()
    greeted = [(a, b) for a in (left, right) for b in (gy, up, down)] + [(gx, up), (gx, down)]
    greeted += [(lax.rem(gx + d, nx_dev), gy) for d in range(2, nx_dev - 1)]
    greeted += [(gx, lax.rem(gy + d, ny_dev)) for d in range(2, ny_dev - 1)]
    for peer in greeted[:8]:
        pl.semaphore_signal(barrier, inc=1, device_id=peer, device_id_type=MESH)
    for k in range(members // 4 + 1):
        own_copy(k).start()
    for peer in greeted[8:]:
        pl.semaphore_signal(barrier, inc=1, device_id=peer, device_id_type=MESH)

    grid_rows = rows * ny_dev
    row = gy * rows - HALO + grid_rows + lax.broadcasted_iota(jnp.int32, (ext, 128), 0)
    row = lax.rem(row, grid_rows).astype(jnp.float32)
    cor[...] = TIME_STEP * 0.5 * (1.0 + 0.5 * jnp.sin(2.0 * math.pi * row / float(grid_rows)))
    for f in range(3):
        cini[f] = jnp.full(cini.shape[1:], SCALE * SCALE * MEAN_DEPTH if f == 0 else 0.0, jnp.float32)
    cfin[...] = jnp.zeros_like(cfin)

    for k in range(members // 4 + 1):
        own_copy(k).wait()

    wide = lax.broadcasted_iota(jnp.int32, (rows, 128), 1) // 8

    @pl.loop(0, 3)
    def _(f):
        first = jnp.zeros((rows, 128), jnp.float32)
        last = jnp.zeros((rows, 128), jnp.float32)
        for m in range(members):
            head = st[m + 1, f, HALO : HALO + rows, 0:128]
            tail = st[m + 1, f, HALO : HALO + rows, cols - 128 : cols]
            both = pltpu.roll(jnp.where(wide < 8, head, tail), (8 * m) % 128, 1)
            first = jnp.where(wide == m, both, first)
            last = jnp.where(wide == (m + 15) % 16, both, last)
        pk[0, 0, f] = first
        pk[1, 0, f] = last
        pk[0, 1, f] = st[0, f, HALO : HALO + rows, 0:128]
        pk[1, 1, f] = st[0, f, HALO : HALO + rows, cols - 128 : cols]

    def x_copies():
        out = []
        for side, x_to in ((0, left), (1, right)):
            for place, (start, count, to, y_to) in enumerate(
                ((0, rows, HALO, gy), (0, HALO, HALO + rows, up), (rows - HALO, HALO, 0, down))
            ):
                out.append(
                    pltpu.make_async_remote_copy(
                        pk.at[side, :, :, pl.ds(start, count), :],
                        halo.at[side, :, :, pl.ds(to, count), :],
                        x_send.at[side, place], x_recv.at[side, place],
                        device_id=(x_to, y_to), device_id_type=MESH)
                )
        return out

    pl.semaphore_wait(barrier, len(greeted))
    for copy in x_copies():
        copy.start()

    def y_copies(p, field_ref, st_ref):
        lead = (slice(None),) * (len(field_ref.shape) - 2)
        return [
            pltpu.make_async_remote_copy(
                field_ref.at[lead + (pl.ds(start, HALO),)],
                st_ref.at[lead + (pl.ds(to, HALO),)],
                y_send.at[way, p], y_recv.at[way, p], device_id=(gx, y_to), device_id_type=MESH)
            for way, (start, to, y_to) in enumerate(((0, HALO + rows, up), (rows - HALO, 0, down)))
        ]

    def control_y():
        return y_copies(0, ctrl_hbm, st.at[0])

    def pair_y(p):
        return y_copies(p, perts_hbm.at[pl.ds(2 * p - 2, 2)], st.at[pl.ds(2 * p - 1, 2)])

    for copy in control_y():
        copy.start()

    @pl.loop(1, pairs)
    def _(p):
        for copy in pair_y(p):
            copy.start()

    for copy in x_copies():
        copy.wait_recv()

    k_id = lax.rem(lax.broadcasted_iota(jnp.int32, (256, 128), 0), 128)
    ahead = lax.rem(k_id - lax.broadcasted_iota(jnp.int32, (256, 128), 1) + 128, 128)
    weights = jnp.where(ahead == 1, 1.0, jnp.where(ahead == 127, -1.0, 0.0))
    weights = jnp.where(ahead == 2, -0.125, jnp.where(ahead == 126, 0.125, weights))
    band[...] = weights.astype(jnp.bfloat16)

    def put_state(ref, i, at, h, e, n):
        for f, z in enumerate((h, e, n, h * n)):
            ref[f, i, at : at + 8] = z

    def slopes_x(ref, i, starts):
        h, e, n = ([ref[f, i, at : at + 8] for at in starts] for f in range(3))
        z = jnp.concatenate(h + e + n + [u * v for u, v in zip(h, e)], axis=0)
        top = z.astype(jnp.bfloat16)
        rest = (z - top.astype(jnp.float32)).astype(jnp.bfloat16)
        out = jnp.dot(jnp.concatenate([top, rest], axis=1), band[...], preferred_element_type=jnp.float32)
        return out.reshape(4, len(starts), 8, 128)

    def slope_y(ref, f, i, at):
        z = [ref[f, i, at + d : at + d + 8] for d in (-2, -1, 1, 2)]
        return (z[2] - z[1]) - 0.125 * (z[3] - z[0])

    def forward(ref, i, at, along):
        h, e, n = (ref[f, i, at : at + 8] for f in range(3))
        c = cor[at : at + 8]
        new_h = h - along[3] - slope_y(ref, 3, i, at)
        new_e = e - (e * along[1] + n * (slope_y(ref, 1, i, at) - c) + along[0])
        new_n = n - (e * (along[2] + c) + n * slope_y(ref, 2, i, at) + slope_y(ref, 0, i, at))
        return new_h, new_e, new_n

    def bred_out(p):
        return pltpu.make_async_copy(fin.at[pl.ds(2 * p - 1, 2)], bred_hbm.at[pl.ds(2 * p - 2, 2)], out_sem.at[p])

    inner = [list(range(2 * w, ext - 2 * w - 7, 8)) for w in (1, 2, 2, 4)]
    inner[0].append(ext - 10)

    @pl.loop(0, pairs)
    def _(p):
        @pl.when(p == 0)
        def _():
            for copy in control_y():
                copy.wait_recv()

        @pl.when(p > 0)
        def _():
            for copy in pair_y(p):
                copy.wait_recv()

        slot = jnp.where(p == 0, 1, 0)
        first = jnp.maximum(2 * p - 1, 0)
        places = (jnp.maximum(first - 1, 0), jnp.maximum(2 * p - 1, 0))
        for f in range(3):
            scale = SCALE * SCALE if f == 0 else SCALE
            for at in range(0, ext, 8):
                pick = slice(at, at + 8)
                after, before = halo[0, slot, f, pick, :], halo[1, slot, f, pick, :]
                rings, middle = [], []
                for k, m in zip((first, 2 * p), places):
                    low, high = st[k, f, pick, 0:128], st[k, f, pick, 128:256]
                    beyond = pltpu.roll(jnp.where(lane // 8 == m, after, before), lax.rem(128 - 8 * m, 128), 1)
                    rings.append(jnp.where(lane < 120, low, beyond))
                    rings.append(jnp.where(lane < 8, beyond, high))
                    middle.append(jnp.where(lane < 64, high, low))
                apart = pltpu.roll(middle[1], 64, 1)
                rings.append(jnp.where((lane < 32) | (lane >= 96), middle[0], apart))
                for i in range(5):
                    now[f, i, pick] = cini[f, i, pick] + scale * rings[i]

        @pl.when(p == 0)
        def _():
            cini[...] = now[:3]

        for i in range(5):
            for at in range(0, ext, 8):
                now[3, i, at : at + 8] = now[0, i, at : at + 8] * now[2, i, at : at + 8]

        for step in range(STEPS):
            for i in range(5):
                starts = inner[2 * step]
                along = slopes_x(now, i, starts)
                for j, at in enumerate(starts):
                    put_state(mid, i, at, *forward(now, i, at, along[:, j]))
            for i in range(5):
                starts = inner[2 * step + 1]
                along = slopes_x(mid, i, starts)
                for j, at in enumerate(starts):
                    new = forward(mid, i, at, along[:, j])
                    put_state(now, i, at, *(0.5 * (now[f, i, at : at + 8] + new[f]) for f in range(3)))

        for f in range(3):
            scale = 1.0 / (SCALE * SCALE) if f == 0 else 1.0 / SCALE
            for at in range(0, rows, 8):
                pick, to = slice(HALO + at, HALO + at + 8), slice(at, at + 8)
                z = [scale * (now[f, i, pick] - cfin[f, i, to]) for i in range(5)]
                for s, k in enumerate((first, 2 * p)):
                    both = z[4] if s == 0 else pltpu.roll(z[4], 64, 1)
                    fin[k, f, 0, to, :] = jnp.where(lane < 112, z[2 * s], both)
                    fin[k, f, 1, to, :] = jnp.where(lane < 16, both, z[2 * s + 1])

        @pl.when(p == 0)
        def _():
            cfin[...] = now[:3, :, HALO : HALO + rows]

        @pl.when(p > 0)
        def _():
            bred_out(p).start()

    @pl.loop(0, members // 4)
    def _(a):
        @pl.loop(0, a + 1)
        def _(b):
            total = [[None] * 4 for _ in range(4)]
            for f in range(3):
                for i in range(2):
                    x = [fin[1 + 4 * a + u, f, i] for u in range(4)]
                    y = [fin[1 + 4 * b + u, f, i] for u in range(4)]
                    for u in range(4):
                        for v in range(4):
                            z = jnp.sum((x[u] * y[v]).reshape(rows // 8, 8, 128), axis=0)
                            total[u][v] = z if total[u][v] is None else total[u][v] + z
            for u in range(4):
                for v in range(4):
                    parts[4 * a + u, 4 * b + v] = total[u][v]
                    parts[4 * b + v, 4 * a + u] = total[u][v]

    row_id = lax.broadcasted_iota(jnp.int32, (members, 128), 0)
    col_id = lax.broadcasted_iota(jnp.int32, (members, 128), 1)
    gram = jnp.zeros((members, 128), jnp.float32)
    for m in range(members):
        sums = jnp.sum(jnp.sum(parts[m], axis=1), axis=1, keepdims=True)
        gram = jnp.where(col_id == m, sums, gram)

    def all_sum(value, buf, me, count, peer_of, send, recv):
        buf[me] = value
        copies = []
        for d in range(1, count):
            copies.append(
                pltpu.make_async_remote_copy(
                    buf.at[me], buf.at[me], send.at[d], recv.at[d],
                    device_id=peer_of(lax.rem(me + d, count)), device_id_type=MESH)
            )
        for copy in copies:
            copy.start()
        for copy in copies:
            copy.wait_recv()
        out = buf[0]
        for d in range(1, count):
            out = out + buf[d]
        return out, copies

    packed = jnp.where(lane < members, gram[0:8], pltpu.roll(gram[8:16], members, 1))
    packed, sent1 = all_sum(packed, red1, gx, nx_dev, lambda i: (i, gy), r1_send, r1_recv)
    packed, sent2 = all_sum(packed, red2, gy, ny_dev, lambda i: (gx, i), r2_send, r2_recv)
    for copy in sent1 + sent2:
        copy.wait_send()
    @pl.loop(1, pairs)
    def _(p):
        bred_out(p).wait()

    for copy in x_copies() + control_y():
        copy.wait_send()

    @pl.loop(1, pairs)
    def _(p):
        for copy in pair_y(p):
            copy.wait_send()

    gram = jnp.concatenate([packed, pltpu.roll(packed, 128 - members, 1)], axis=0)

    work = jnp.where(col_id < members, gram, jnp.where(col_id - members == row_id, 1.0, 0.0))
    pivots = jnp.ones((members, 1), jnp.float32)
    for k in range(members):
        column = work[:, k : k + 1]
        pivot = column[k : k + 1]
        work = work - jnp.where(row_id > k, column, 0.0) * (work[k : k + 1] * (1.0 / pivot))
        pivots = jnp.where(row_id[:, :1] == k, pivot, pivots)
    factor_ref[...] = work / jnp.sqrt(pivots)


def apply_kernel(length, members, bred_hbm, factor_hbm, basis_hbm, rfac_hbm, bred, factor, table, out, rout, sem):
    first = pltpu.make_async_copy(factor_hbm, factor, sem.at[4])
    first.start()
    parts = [pltpu.make_async_copy(bred_hbm.at[:, pl.ds(f, 1)], bred.at[:, pl.ds(f, 1)], sem.at[5 + f]) for f in range(3)]
    for copy in parts:
        copy.start()
    first.wait()
    row_id = lax.broadcasted_iota(jnp.int32, (members, members), 0)
    col_id = lax.broadcasted_iota(jnp.int32, (members, members), 1)
    rout[...] = jnp.where(row_id <= col_id, factor[:, :members] * (1.0 / math.sqrt(length)), 0.0)
    small = pltpu.make_async_copy(rout, rfac_hbm, sem.at[3])
    small.start()
    for j in range(members):
        column = factor[:, members + j : members + j + 1] * math.sqrt(length)
        table[j] = jnp.broadcast_to(column, (members, 128))
    copies = []
    for f in range(3):
        parts[f].wait()
        for i in range(2):
            x = [bred[j, f, i] for j in range(members)]
            for m in range(members):
                total = table[0, m : m + 1, :] * x[0]
                for j in range(1, m + 1):
                    total = total + table[j, m : m + 1, :] * x[j]
                out[m, f, :, 128 * i : 128 * (i + 1)] = total
        copies.append(pltpu.make_async_copy(out.at[:, pl.ds(f, 1)], basis_hbm.at[:, pl.ds(f, 1)], sem.at[f]))
        copies[-1].start()
    for copy in copies + [small]:
        copy.wait()


def body(control, perts):
    nx_dev, ny_dev = lax.axis_size("gx"), lax.axis_size("gy")
    members, _, rows, cols = perts.shape
    states, ext = members + 1, rows + 2 * HALO
    f32 = jnp.float32
    dma = pltpu.SemaphoreType.DMA
    vmem, hbm = pl.BlockSpec(memory_space=pltpu.VMEM), pl.BlockSpec(memory_space=pltpu.HBM)
    bred, factor = pl.pallas_call(
        functools.partial(kernel, nx_dev, ny_dev, members, rows, cols),
        out_shape=(
            jax.ShapeDtypeStruct((members, 3, 2, rows, 128), f32),
            jax.ShapeDtypeStruct((members, 128), f32),
        ),
        in_specs=[hbm] * 2,
        out_specs=[hbm, vmem],
        scratch_shapes=[
            pltpu.VMEM((states, 3, ext, cols), f32),
            pltpu.VMEM((2, 2, 3, rows, 128), f32),
            pltpu.VMEM((2, 2, 3, ext, 128), f32),
            pltpu.VMEM((256, 128), jnp.bfloat16),
            pltpu.VMEM((4, 5, ext, 128), f32),
            pltpu.VMEM((4, 5, ext, 128), f32),
            pltpu.VMEM((3, 5, ext, 128), f32),
            pltpu.VMEM((3, 5, rows, 128), f32),
            pltpu.VMEM((ext, 128), f32),
            pltpu.VMEM((states, 3, 2, rows, 128), f32),
            pltpu.VMEM((members, members, 8, 128), f32),
            pltpu.VMEM((nx_dev, 8, 128), f32),
            pltpu.VMEM((ny_dev, 8, 128), f32),
            dma((members // 4 + 1,)),
            dma((members // 2 + 1,)),
            dma((2, members // 2 + 1)),
            dma((2, members // 2 + 1)),
            dma((2, 3)),
            dma((2, 3)),
            dma((nx_dev,)),
            dma((nx_dev,)),
            dma((ny_dev,)),
            dma((ny_dev,)),
        ],
        compiler_params=pltpu.CompilerParams(
            collective_id=0, has_side_effects=True, vmem_limit_bytes=60 * 1024 * 1024
        ),
    )(control, perts)
    length = float(3 * rows * ny_dev * cols * nx_dev)
    return pl.pallas_call(
        functools.partial(apply_kernel, length, members),
        out_shape=(
            jax.ShapeDtypeStruct(perts.shape, f32),
            jax.ShapeDtypeStruct((members, members), f32),
        ),
        in_specs=[hbm] * 2,
        out_specs=[hbm] * 2,
        scratch_shapes=[
            pltpu.VMEM((members, 3, 2, rows, 128), f32),
            pltpu.VMEM((members, 128), f32),
            pltpu.VMEM((members, members, 128), f32),
            pltpu.VMEM((members, 3, rows, cols), f32),
            pltpu.VMEM((members, members), f32),
            dma((8,)),
        ],
        compiler_params=pltpu.CompilerParams(vmem_limit_bytes=60 * 1024 * 1024),
    )(bred, factor)


def solution(mesh):
    in_specs = (P(None, "gy", "gx"), P(None, None, "gy", "gx"))
    out_specs = (P(None, None, "gy", "gx"), P())
    return jax.shard_map(body, mesh=mesh, in_specs=in_specs, out_specs=out_specs, check_vma=False)
```

```python
import functools
import math

import jax
import jax.numpy as jnp
from jax import lax
from jax.experimental import pallas as pl
from jax.experimental.pallas import tpu as pltpu
from jax.sharding import PartitionSpec as P

MESH = pl.DeviceIdType.MESH
HALO = 8
STEPS = 2
ALL_RINGS, CONTROL_RINGS = (0, 1, 2, 3, 4), (0, 1, 4)
SAME_RING = ((0, 2), (1, 3), (4,))
MEAN_DEPTH = 4.0
TIME_STEP = 0.1
SCALE = TIME_STEP * (2.0 / 3.0)


def kernel(
    nx_dev, ny_dev, members, rows, cols,
    ctrl_hbm, perts_hbm, bred_hbm, factor_ref,
    st, pk, halo, band, stages, last, cini, cfin, cor, fin, parts, red1, red2,
    in_sem, out_sem, y_send, y_recv, x_send, x_recv, r1_send, r1_recv, r2_send, r2_recv,
):
    gx, gy = lax.axis_index("gx"), lax.axis_index("gy")
    ext = rows + 2 * HALO
    pairs = members // 2 + 1
    lane = lax.broadcasted_iota(jnp.int32, (8, 128), 1)
    left, right = lax.rem(gx + nx_dev - 1, nx_dev), lax.rem(gx + 1, nx_dev)
    up, down = lax.rem(gy + ny_dev - 1, ny_dev), lax.rem(gy + 1, ny_dev)

    def own_copy(k):
        source = ctrl_hbm if k == 0 else perts_hbm.at[pl.ds((k - 1) * 4, 4)]
        target = st.at[0] if k == 0 else st.at[pl.ds((k - 1) * 4 + 1, 4)]
        if k == 0:
            return pltpu.make_async_copy(source, target.at[:, pl.ds(HALO, rows), :], in_sem.at[k])
        return pltpu.make_async_copy(source, target.at[:, :, pl.ds(HALO, rows), :], in_sem.at[k])

    barrier = pltpu.get_barrier_semaphore()
    greeted = [(a, b) for a in (left, right) for b in (gy, up, down)] + [(gx, up), (gx, down)]
    greeted += [(lax.rem(gx + d, nx_dev), gy) for d in range(2, nx_dev - 1)]
    greeted += [(gx, lax.rem(gy + d, ny_dev)) for d in range(2, ny_dev - 1)]
    for peer in greeted[:8]:
        pl.semaphore_signal(barrier, inc=1, device_id=peer, device_id_type=MESH)
    for k in range(members // 4 + 1):
        own_copy(k).start()
    for peer in greeted[8:]:
        pl.semaphore_signal(barrier, inc=1, device_id=peer, device_id_type=MESH)

    grid_rows = rows * ny_dev
    row = gy * rows - HALO + grid_rows + lax.broadcasted_iota(jnp.int32, (ext, 128), 0)
    row = lax.rem(row, grid_rows).astype(jnp.float32)
    cor[...] = TIME_STEP * 0.5 * (1.0 + 0.5 * jnp.sin(2.0 * math.pi * row / float(grid_rows)))

    for k in range(members // 4 + 1):
        own_copy(k).wait()

    wide = lax.broadcasted_iota(jnp.int32, (rows, 128), 1) // 8

    @pl.loop(0, 3)
    def _(f):
        first = jnp.zeros((rows, 128), jnp.float32)
        last = jnp.zeros((rows, 128), jnp.float32)
        for m in range(members):
            head = st[m + 1, f, HALO : HALO + rows, 0:128]
            tail = st[m + 1, f, HALO : HALO + rows, cols - 128 : cols]
            both = pltpu.roll(jnp.where(wide < 8, head, tail), (8 * m) % 128, 1)
            first = jnp.where(wide == m, both, first)
            last = jnp.where(wide == (m + 15) % 16, both, last)
        pk[0, 0, f] = first
        pk[1, 0, f] = last
        pk[0, 1, f] = st[0, f, HALO : HALO + rows, 0:128]
        pk[1, 1, f] = st[0, f, HALO : HALO + rows, cols - 128 : cols]

    def x_copies(place, tile):
        start, count, to, y_to = ((0, rows, HALO, gy), (0, HALO, HALO + rows, up), (rows - HALO, HALO, 0, down))[place]
        return [
            pltpu.make_async_remote_copy(
                pk.at[side, tile, :, pl.ds(start, count), :],
                halo.at[side, tile, :, pl.ds(to, count), :],
                x_send.at[side, place, tile], x_recv.at[side, place, tile],
                device_id=(x_to, y_to), device_id_type=MESH)
            for side, x_to in ((0, left), (1, right))
        ]

    everything = [(place, tile) for place in range(3) for tile in (1, 0)]
    pl.semaphore_wait(barrier, len(greeted))
    for key in everything:
        for copy in x_copies(*key):
            copy.start()

    def y_copies(p, field_ref, st_ref):
        lead = (slice(None),) * (len(field_ref.shape) - 2)
        return [
            pltpu.make_async_remote_copy(
                field_ref.at[lead + (pl.ds(start, HALO),)],
                st_ref.at[lead + (pl.ds(to, HALO),)],
                y_send.at[way, p], y_recv.at[way, p], device_id=(gx, y_to), device_id_type=MESH)
            for way, (start, to, y_to) in enumerate(((0, HALO + rows, up), (rows - HALO, 0, down)))
        ]

    def control_y():
        return y_copies(0, ctrl_hbm, st.at[0])

    def pair_y(p):
        return y_copies(p, perts_hbm.at[pl.ds(2 * p - 2, 2)], st.at[pl.ds(2 * p - 1, 2)])

    for copy in control_y():
        copy.start()

    @pl.loop(1, pairs)
    def _(p):
        for copy in pair_y(p):
            copy.start()

    k_id = lax.rem(lax.broadcasted_iota(jnp.int32, (256, 128), 0), 128)
    ahead = lax.rem(k_id - lax.broadcasted_iota(jnp.int32, (256, 128), 1) + 128, 128)
    weights = jnp.where(ahead == 1, 1.0, jnp.where(ahead == 127, -1.0, 0.0))
    weights = jnp.where(ahead == 2, -0.125, jnp.where(ahead == 126, 0.125, weights))
    band[...] = weights.astype(jnp.bfloat16)

    def assemble(p, starts):
        control = isinstance(p, int)
        slot, states = (1, (0, 0)) if control else (0, (2 * p - 1, 2 * p))
        for at in starts:
            pick = slice(at, at + 8)
            state = []
            for f in range(3):
                after, before = halo[0, slot, f, pick, :], halo[1, slot, f, pick, :]
                rings, middle = [], []
                for k in states:
                    low, high = st[k, f, pick, 0:128], st[k, f, pick, 128:256]
                    if control:
                        beyond = jnp.where(lane < 8, after, before)
                    else:
                        beyond = pltpu.roll(jnp.where(lane // 8 == k - 1, after, before), lax.rem(136 - 8 * k, 128), 1)
                    rings.append(jnp.where(lane < 120, low, beyond))
                    rings.append(jnp.where(lane < 8, beyond, high))
                    middle.append(jnp.where(lane < 64, high, low))
                apart = pltpu.roll(middle[1], 64, 1)
                rings.append(jnp.where((lane < 32) | (lane >= 96), middle[0], apart))
                scale = SCALE * SCALE if f == 0 else SCALE
                if control:
                    rings = [scale * z + (scale * MEAN_DEPTH if f == 0 else 0.0) for z in rings]
                    for same in SAME_RING:
                        for i in same:
                            cini[f, i, pick] = rings[same[0]]
                else:
                    rings = [cini[f, i, pick] + scale * z for i, z in enumerate(rings)]
                state.append(rings)
            for i in CONTROL_RINGS if control else ALL_RINGS:
                put_state(p, 0, i, at, *(state[f][i] for f in range(3)))

    def put_state(p, stage, i, at, h, e, n):
        for f, z in enumerate((h, e, n, h * n)):
            stages[stage, p, f, i, at : at + 8] = z

    def slopes_x(p, stage, units):
        h, e, n = ([stages[stage, p, f, i, at : at + 8] for i, at in units] for f in range(3))
        z = jnp.concatenate(h + e + n + [u * v for u, v in zip(h, e)], axis=0)
        top = z.astype(jnp.bfloat16)
        rest = (z - top.astype(jnp.float32)).astype(jnp.bfloat16)
        out = jnp.dot(jnp.concatenate([top, rest], axis=1), band[...], preferred_element_type=jnp.float32)
        return out.reshape(4, len(units), 8, 128)

    def slope_y(p, stage, f, i, at):
        z = [stages[stage, p, f, i, at + d : at + d + 8] for d in (-2, -1, 1, 2)]
        return (z[2] - z[1]) - 0.125 * (z[3] - z[0])

    def forward(p, stage, i, at, along):
        h, e, n = (stages[stage, p, f, i, at : at + 8] for f in range(3))
        c = cor[at : at + 8]
        new_h = h - along[3] - slope_y(p, stage, 3, i, at)
        new_e = e - (e * along[1] + n * (slope_y(p, stage, 1, i, at) - c) + along[0])
        new_n = n - (e * (along[2] + c) + n * slope_y(p, stage, 2, i, at) + slope_y(p, stage, 0, i, at))
        return new_h, new_e, new_n

    def evaluate(p, stage, units, u=0):
        along = slopes_x(p, stage, units)
        for j, (i, at) in enumerate(units):
            new = forward(p, stage, i, at, along[:, j])
            if stage % 2 == 1:
                new = [0.5 * (stages[stage - 1, p, f, i, at : at + 8] + new[f]) for f in range(3)]
            if stage < 2 * STEPS - 1:
                put_state(p, stage + 1, i, at, *new)
            else:
                for f in range(3):
                    last[u, f, i, at - HALO : at - HALO + 8] = new[f]

    def finish(p, starts, u=0):
        for f in range(3):
            scale = 1.0 / (SCALE * SCALE) if f == 0 else 1.0 / SCALE
            for at in starts:
                to = slice(at - HALO, at - HALO + 8)
                if isinstance(p, int):
                    for same in SAME_RING:
                        for i in same:
                            cfin[f, i, to] = last[u, f, same[0], to]
                    continue
                z = [scale * (last[u, f, i, to] - cfin[f, i, to]) for i in ALL_RINGS]
                for s, k in enumerate((2 * p - 1, 2 * p)):
                    both = z[4] if s == 0 else pltpu.roll(z[4], 64, 1)
                    fin[k, f, 0, to, :] = jnp.where(lane < 112, z[2 * s], both)
                    fin[k, f, 1, to, :] = jnp.where(lane < 16, both, z[2 * s + 1])

    def inner(chosen):
        for p in chosen:
            assemble(p, range(HALO, HALO + rows, 8))
        for stage in range(2 * STEPS):
            low, high = HALO + 2 * stage + 2, HALO + rows - 2 * stage - 2
            starts = [min(at, high - 8) for at in range(low, high, 8)]
            for u, p in enumerate(chosen):
                for i in CONTROL_RINGS if isinstance(p, int) else ALL_RINGS:
                    evaluate(p, stage, [(i, at) for at in starts], u)
        for u, p in enumerate(chosen):
            finish(p, starts, u)

    def edges(chosen):
        for p in chosen:
            assemble(p, (0, HALO + rows))
        for stage in range(2 * STEPS):
            starts = (2 * stage + 2, rows + 2 * HALO - 2 * stage - 10)
            for u, p in enumerate(chosen):
                for i in CONTROL_RINGS if isinstance(p, int) else ALL_RINGS:
                    evaluate(p, stage, [(i, at) for at in starts], u)
        for u, p in enumerate(chosen):
            finish(p, starts, u)

    def bred_out(p):
        return pltpu.make_async_copy(fin.at[pl.ds(2 * p - 1, 2)], bred_hbm.at[pl.ds(2 * p - 2, 2)], out_sem.at[p])

    for copy in x_copies(0, 1):
        copy.wait_recv()
    inner([0])
    for copy in x_copies(0, 0):
        copy.wait_recv()

    @pl.loop(0, members // 4)
    def _(q):
        inner([2 * q + 1, 2 * q + 2])

    for copy in x_copies(1, 1) + x_copies(2, 1) + control_y():
        copy.wait_recv()
    edges([0])
    for copy in x_copies(1, 0) + x_copies(2, 0):
        copy.wait_recv()

    @pl.loop(0, members // 4)
    def _(q):
        for p in (2 * q + 1, 2 * q + 2):
            for copy in pair_y(p):
                copy.wait_recv()
        edges([2 * q + 1, 2 * q + 2])
        for p in (2 * q + 1, 2 * q + 2):
            bred_out(p).start()

    @pl.loop(0, members // 4)
    def _(a):
        @pl.loop(0, a + 1)
        def _(b):
            total = [[None] * 4 for _ in range(4)]
            for f in range(3):
                for i in range(2):
                    x = [fin[1 + 4 * a + u, f, i] for u in range(4)]
                    y = [fin[1 + 4 * b + u, f, i] for u in range(4)]
                    for u in range(4):
                        for v in range(4):
                            z = jnp.sum((x[u] * y[v]).reshape(rows // 8, 8, 128), axis=0)
                            total[u][v] = z if total[u][v] is None else total[u][v] + z
            for u in range(4):
                for v in range(4):
                    parts[4 * a + u, 4 * b + v] = total[u][v]
                    parts[4 * b + v, 4 * a + u] = total[u][v]

    row_id = lax.broadcasted_iota(jnp.int32, (members, 128), 0)
    col_id = lax.broadcasted_iota(jnp.int32, (members, 128), 1)
    gram = jnp.zeros((members, 128), jnp.float32)
    for m in range(members):
        sums = jnp.sum(jnp.sum(parts[m], axis=1), axis=1, keepdims=True)
        gram = jnp.where(col_id == m, sums, gram)

    def all_sum(value, buf, me, count, peer_of, send, recv):
        buf[me] = value
        copies = []
        for d in range(1, count):
            copies.append(
                pltpu.make_async_remote_copy(
                    buf.at[me], buf.at[me], send.at[d], recv.at[d],
                    device_id=peer_of(lax.rem(me + d, count)), device_id_type=MESH)
            )
        for copy in copies:
            copy.start()
        for copy in copies:
            copy.wait_recv()
        out = buf[0]
        for d in range(1, count):
            out = out + buf[d]
        return out, copies

    packed = jnp.where(lane < members, gram[0:8], pltpu.roll(gram[8:16], members, 1))
    packed, sent1 = all_sum(packed, red1, gx, nx_dev, lambda i: (i, gy), r1_send, r1_recv)
    packed, sent2 = all_sum(packed, red2, gy, ny_dev, lambda i: (gx, i), r2_send, r2_recv)
    for copy in sent1 + sent2:
        copy.wait_send()
    @pl.loop(1, pairs)
    def _(p):
        bred_out(p).wait()

    for copy in [copy for key in everything for copy in x_copies(*key)] + control_y():
        copy.wait_send()

    @pl.loop(1, pairs)
    def _(p):
        for copy in pair_y(p):
            copy.wait_send()

    gram = jnp.concatenate([packed, pltpu.roll(packed, 128 - members, 1)], axis=0)

    work = jnp.where(col_id < members, gram, jnp.where(col_id - members == row_id, 1.0, 0.0))
    pivots = jnp.ones((members, 1), jnp.float32)
    for k in range(members):
        column = work[:, k : k + 1]
        pivot = column[k : k + 1]
        work = work - jnp.where(row_id > k, column, 0.0) * (work[k : k + 1] * (1.0 / pivot))
        pivots = jnp.where(row_id[:, :1] == k, pivot, pivots)
    factor_ref[...] = work / jnp.sqrt(pivots)


def apply_kernel(length, members, bred_hbm, factor_hbm, basis_hbm, rfac_hbm, bred, factor, table, out, rout, sem):
    first = pltpu.make_async_copy(factor_hbm, factor, sem.at[7])
    first.start()
    parts = [
        pltpu.make_async_copy(bred_hbm.at[:, pl.ds(f, 1), pl.ds(i, 1)], bred.at[:, pl.ds(f, 1), pl.ds(i, 1)], sem.at[8 + 2 * f + i])
        for f in range(3)
        for i in range(2)
    ]
    for copy in parts:
        copy.start()
    first.wait()
    row_id = lax.broadcasted_iota(jnp.int32, (members, members), 0)
    col_id = lax.broadcasted_iota(jnp.int32, (members, members), 1)
    rout[...] = jnp.where(row_id <= col_id, factor[:, :members] * (1.0 / math.sqrt(length)), 0.0)
    small = pltpu.make_async_copy(rout, rfac_hbm, sem.at[6])
    small.start()
    for j in range(members):
        column = factor[:, members + j : members + j + 1] * math.sqrt(length)
        table[j] = jnp.broadcast_to(column, (members, 128))
    copies = []
    for f in range(3):
        for i in range(2):
            parts[2 * f + i].wait()
            x = [bred[j, f, i] for j in range(members)]
            for m in range(members):
                total = table[0, m : m + 1, :] * x[0]
                for j in range(1, m + 1):
                    total = total + table[j, m : m + 1, :] * x[j]
                out[m, f, :, 128 * i : 128 * (i + 1)] = total
            half = (slice(None), pl.ds(f, 1), slice(None), pl.ds(128 * i, 128))
            copies.append(pltpu.make_async_copy(out.at[half], basis_hbm.at[half], sem.at[2 * f + i]))
            copies[-1].start()
    for copy in copies + [small]:
        copy.wait()


def body(control, perts):
    nx_dev, ny_dev = lax.axis_size("gx"), lax.axis_size("gy")
    members, _, rows, cols = perts.shape
    states, ext = members + 1, rows + 2 * HALO
    f32 = jnp.float32
    dma = pltpu.SemaphoreType.DMA
    vmem, hbm = pl.BlockSpec(memory_space=pltpu.VMEM), pl.BlockSpec(memory_space=pltpu.HBM)
    bred, factor = pl.pallas_call(
        functools.partial(kernel, nx_dev, ny_dev, members, rows, cols),
        out_shape=(
            jax.ShapeDtypeStruct((members, 3, 2, rows, 128), f32),
            jax.ShapeDtypeStruct((members, 128), f32),
        ),
        in_specs=[hbm] * 2,
        out_specs=[hbm, vmem],
        scratch_shapes=[
            pltpu.VMEM((states, 3, ext, cols), f32),
            pltpu.VMEM((2, 2, 3, rows, 128), f32),
            pltpu.VMEM((2, 2, 3, ext, 128), f32),
            pltpu.VMEM((256, 128), jnp.bfloat16),
            pltpu.VMEM((2 * STEPS, members // 2 + 1, 4, 5, ext, 128), f32),
            pltpu.VMEM((2, 3, 5, rows, 128), f32),
            pltpu.VMEM((3, 5, ext, 128), f32),
            pltpu.VMEM((3, 5, rows, 128), f32),
            pltpu.VMEM((ext, 128), f32),
            pltpu.VMEM((states, 3, 2, rows, 128), f32),
            pltpu.VMEM((members, members, 8, 128), f32),
            pltpu.VMEM((nx_dev, 8, 128), f32),
            pltpu.VMEM((ny_dev, 8, 128), f32),
            dma((members // 4 + 1,)),
            dma((members // 2 + 1,)),
            dma((2, members // 2 + 1)),
            dma((2, members // 2 + 1)),
            dma((2, 3, 2)),
            dma((2, 3, 2)),
            dma((nx_dev,)),
            dma((nx_dev,)),
            dma((ny_dev,)),
            dma((ny_dev,)),
        ],
        compiler_params=pltpu.CompilerParams(
            collective_id=0, has_side_effects=True, vmem_limit_bytes=60 * 1024 * 1024
        ),
    )(control, perts)
    length = float(3 * rows * ny_dev * cols * nx_dev)
    return pl.pallas_call(
        functools.partial(apply_kernel, length, members),
        out_shape=(
            jax.ShapeDtypeStruct(perts.shape, f32),
            jax.ShapeDtypeStruct((members, members), f32),
        ),
        in_specs=[hbm] * 2,
        out_specs=[hbm] * 2,
        scratch_shapes=[
            pltpu.VMEM((members, 3, 2, rows, 128), f32),
            pltpu.VMEM((members, 128), f32),
            pltpu.VMEM((members, members, 128), f32),
            pltpu.VMEM((members, 3, rows, cols), f32),
            pltpu.VMEM((members, members), f32),
            dma((14,)),
        ],
        compiler_params=pltpu.CompilerParams(vmem_limit_bytes=60 * 1024 * 1024),
    )(bred, factor)


def solution(mesh):
    in_specs = (P(None, "gy", "gx"), P(None, None, "gy", "gx"))
    out_specs = (P(None, None, "gy", "gx"), P())
    return jax.shard_map(body, mesh=mesh, in_specs=in_specs, out_specs=out_specs, check_vma=False)
```

```python
import functools
import math

import jax
import jax.numpy as jnp
from jax import lax
from jax.experimental import pallas as pl
from jax.experimental.pallas import tpu as pltpu
from jax.sharding import PartitionSpec as P

MESH = pl.DeviceIdType.MESH
HALO = 8
STEPS = 2
ALL_RINGS, OUTER_RINGS, MIDDLE_RING = (0, 1, 2, 3, 4), (0, 1, 2, 3), (4,)
SAME_RING = ((0, 2), (1, 3), (4,))
MEAN_DEPTH = 4.0
TIME_STEP = 0.1
SCALE = TIME_STEP * (2.0 / 3.0)


def kernel(
    nx_dev, ny_dev, members, rows, cols,
    ctrl_hbm, perts_hbm, bred_hbm, factor_ref,
    st, pk, halo, band, stages, last, cini, cfin, cor, fin, parts, red1, red2,
    in_sem, out_sem, y_send, y_recv, x_send, x_recv, r1_send, r1_recv, r2_send, r2_recv,
):
    gx, gy = lax.axis_index("gx"), lax.axis_index("gy")
    ext = rows + 2 * HALO
    pairs = members // 2 + 1
    lane = lax.broadcasted_iota(jnp.int32, (8, 128), 1)
    left, right = lax.rem(gx + nx_dev - 1, nx_dev), lax.rem(gx + 1, nx_dev)
    up, down = lax.rem(gy + ny_dev - 1, ny_dev), lax.rem(gy + 1, ny_dev)

    def own_copy(k):
        source = ctrl_hbm if k == 0 else perts_hbm.at[pl.ds((k - 1) * 4, 4)]
        target = st.at[0] if k == 0 else st.at[pl.ds((k - 1) * 4 + 1, 4)]
        if k == 0:
            return pltpu.make_async_copy(source, target.at[:, pl.ds(HALO, rows), :], in_sem.at[k])
        return pltpu.make_async_copy(source, target.at[:, :, pl.ds(HALO, rows), :], in_sem.at[k])

    barrier = pltpu.get_barrier_semaphore()
    greeted = [(a, b) for a in (left, right) for b in (gy, up, down)] + [(gx, up), (gx, down)]
    greeted += [(lax.rem(gx + d, nx_dev), gy) for d in range(2, nx_dev - 1)]
    greeted += [(gx, lax.rem(gy + d, ny_dev)) for d in range(2, ny_dev - 1)]
    for peer in greeted[:8]:
        pl.semaphore_signal(barrier, inc=1, device_id=peer, device_id_type=MESH)
    for k in range(members // 4 + 1):
        own_copy(k).start()
    for peer in greeted[8:]:
        pl.semaphore_signal(barrier, inc=1, device_id=peer, device_id_type=MESH)

    grid_rows = rows * ny_dev
    row = gy * rows - HALO + grid_rows + lax.broadcasted_iota(jnp.int32, (ext, 128), 0)
    row = lax.rem(row, grid_rows).astype(jnp.float32)
    cor[...] = TIME_STEP * 0.5 * (1.0 + 0.5 * jnp.sin(2.0 * math.pi * row / float(grid_rows)))

    for k in range(members // 4 + 1):
        own_copy(k).wait()

    wide = lax.broadcasted_iota(jnp.int32, (rows, 128), 1) // 8

    @pl.loop(0, 3)
    def _(f):
        first = jnp.zeros((rows, 128), jnp.float32)
        last = jnp.zeros((rows, 128), jnp.float32)
        for m in range(members):
            head = st[m + 1, f, HALO : HALO + rows, 0:128]
            tail = st[m + 1, f, HALO : HALO + rows, cols - 128 : cols]
            both = pltpu.roll(jnp.where(wide < 8, head, tail), (8 * m) % 128, 1)
            first = jnp.where(wide == m, both, first)
            last = jnp.where(wide == (m + 15) % 16, both, last)
        pk[0, 0, f] = first
        pk[1, 0, f] = last
        pk[0, 1, f] = st[0, f, HALO : HALO + rows, 0:128]
        pk[1, 1, f] = st[0, f, HALO : HALO + rows, cols - 128 : cols]

    def x_copies(place, tile):
        start, count, to, y_to = ((0, rows, HALO, gy), (0, HALO, HALO + rows, up), (rows - HALO, HALO, 0, down))[place]
        return [
            pltpu.make_async_remote_copy(
                pk.at[side, tile, :, pl.ds(start, count), :],
                halo.at[side, tile, :, pl.ds(to, count), :],
                x_send.at[side, place, tile], x_recv.at[side, place, tile],
                device_id=(x_to, y_to), device_id_type=MESH)
            for side, x_to in ((0, left), (1, right))
        ]

    everything = [(place, tile) for place in range(3) for tile in (1, 0)]
    pl.semaphore_wait(barrier, len(greeted))
    for key in everything:
        for copy in x_copies(*key):
            copy.start()

    def y_copies(p, field_ref, st_ref):
        lead = (slice(None),) * (len(field_ref.shape) - 2)
        return [
            pltpu.make_async_remote_copy(
                field_ref.at[lead + (pl.ds(start, HALO),)],
                st_ref.at[lead + (pl.ds(to, HALO),)],
                y_send.at[way, p], y_recv.at[way, p], device_id=(gx, y_to), device_id_type=MESH)
            for way, (start, to, y_to) in enumerate(((0, HALO + rows, up), (rows - HALO, 0, down)))
        ]

    def control_y():
        return y_copies(0, ctrl_hbm, st.at[0])

    def pair_y(p):
        return y_copies(p, perts_hbm.at[pl.ds(2 * p - 2, 2)], st.at[pl.ds(2 * p - 1, 2)])

    for copy in control_y():
        copy.start()

    @pl.loop(1, 5)
    def _(p):
        for copy in pair_y(p):
            copy.start()

    k_id = lax.rem(lax.broadcasted_iota(jnp.int32, (256, 128), 0), 128)
    ahead = lax.rem(k_id - lax.broadcasted_iota(jnp.int32, (256, 128), 1) + 128, 128)
    weights = jnp.where(ahead == 1, 1.0, jnp.where(ahead == 127, -1.0, 0.0))
    weights = jnp.where(ahead == 2, -0.125, jnp.where(ahead == 126, 0.125, weights))
    band[...] = weights.astype(jnp.bfloat16)

    def of_control(p, rings):
        return [i for i in rings if i in (0, 1, 4)] if isinstance(p, int) else rings

    def assemble(p, starts, rings):
        control = isinstance(p, int)
        slot, states = (1, (0, 0)) if control else (0, (2 * p - 1, 2 * p))
        for at in starts:
            pick = slice(at, at + 8)
            state = []
            for f in range(3):
                tiles = [[st[k, f, pick, 128 * i : 128 * (i + 1)] for i in range(2)] for k in states]
                full = {}
                if 0 in rings:
                    after, before = halo[0, slot, f, pick, :], halo[1, slot, f, pick, :]
                    for s, k in enumerate(states):
                        if control:
                            beyond = jnp.where(lane < 8, after, before)
                        else:
                            beyond = pltpu.roll(jnp.where(lane // 8 == k - 1, after, before), lax.rem(136 - 8 * k, 128), 1)
                        full[2 * s] = jnp.where(lane < 120, tiles[s][0], beyond)
                        full[2 * s + 1] = jnp.where(lane < 8, beyond, tiles[s][1])
                if 4 in rings:
                    middle = [jnp.where(lane < 64, high, low) for low, high in tiles]
                    full[4] = jnp.where((lane < 32) | (lane >= 96), middle[0], pltpu.roll(middle[1], 64, 1))
                scale = SCALE * SCALE if f == 0 else SCALE
                if control:
                    full = {i: scale * z + (scale * MEAN_DEPTH if f == 0 else 0.0) for i, z in full.items()}
                    for same in SAME_RING:
                        if same[0] in full:
                            for i in same:
                                cini[f, i, pick] = full[same[0]]
                else:
                    full = {i: cini[f, i, pick] + scale * z for i, z in full.items()}
                state.append(full)
            for i in of_control(p, rings):
                put_state(p, 0, i, at, *(state[f][i] for f in range(3)))

    def put_state(p, stage, i, at, h, e, n):
        for f, z in enumerate((h, e, n, h * n)):
            stages[stage, p, f, i, at : at + 8] = z

    def slopes_x(p, stage, units):
        h, e, n = ([stages[stage, p, f, i, at : at + 8] for i, at in units] for f in range(3))
        z = jnp.concatenate(h + e + n + [u * v for u, v in zip(h, e)], axis=0)
        top = z.astype(jnp.bfloat16)
        rest = (z - top.astype(jnp.float32)).astype(jnp.bfloat16)
        out = jnp.dot(jnp.concatenate([top, rest], axis=1), band[...], preferred_element_type=jnp.float32)
        return out.reshape(4, len(units), 8, 128)

    def slope_y(p, stage, f, i, at):
        z = [stages[stage, p, f, i, at + d : at + d + 8] for d in (-2, -1, 1, 2)]
        return (z[2] - z[1]) - 0.125 * (z[3] - z[0])

    def forward(p, stage, i, at, along):
        h, e, n = (stages[stage, p, f, i, at : at + 8] for f in range(3))
        c = cor[at : at + 8]
        new_h = h - along[3] - slope_y(p, stage, 3, i, at)
        new_e = e - (e * along[1] + n * (slope_y(p, stage, 1, i, at) - c) + along[0])
        new_n = n - (e * (along[2] + c) + n * slope_y(p, stage, 2, i, at) + slope_y(p, stage, 0, i, at))
        return new_h, new_e, new_n

    def evaluate(p, stage, units):
        along = slopes_x(p, stage, units)
        for j, (i, at) in enumerate(units):
            new = forward(p, stage, i, at, along[:, j])
            if stage % 2 == 1:
                new = [0.5 * (stages[stage - 1, p, f, i, at : at + 8] + new[f]) for f in range(3)]
            if stage < 2 * STEPS - 1:
                put_state(p, stage + 1, i, at, *new)
            else:
                for f in range(3):
                    last[p, f, i, at - HALO : at - HALO + 8] = new[f]

    def finish(p, starts):
        for f in range(3):
            scale = 1.0 / (SCALE * SCALE) if f == 0 else 1.0 / SCALE
            for at in starts:
                to = slice(at - HALO, at - HALO + 8)
                if isinstance(p, int):
                    for same in SAME_RING:
                        for i in same:
                            cfin[f, i, to] = last[p, f, same[0], to]
                    continue
                z = [scale * (last[p, f, i, to] - cfin[f, i, to]) for i in ALL_RINGS]
                for s, k in enumerate((2 * p - 1, 2 * p)):
                    both = z[4] if s == 0 else pltpu.roll(z[4], 64, 1)
                    fin[k, f, 0, to, :] = jnp.where(lane < 112, z[2 * s], both)
                    fin[k, f, 1, to, :] = jnp.where(lane < 16, both, z[2 * s + 1])

    def inner(chosen, rings):
        for p in chosen:
            assemble(p, range(HALO, HALO + rows, 8), rings)
        for stage in range(2 * STEPS):
            low, high = HALO + 2 * stage + 2, HALO + rows - 2 * stage - 2
            starts = [min(at, high - 8) for at in range(low, high, 8)]
            for p in chosen:
                for i in of_control(p, rings):
                    evaluate(p, stage, [(i, at) for at in starts])
        if 0 in rings:
            for p in chosen:
                finish(p, starts)

    def edges(chosen):
        for p in chosen:
            assemble(p, (0, HALO + rows), ALL_RINGS)
        for stage in range(2 * STEPS):
            starts = (2 * stage + 2, rows + 2 * HALO - 2 * stage - 10)
            for p in chosen:
                for i in of_control(p, ALL_RINGS):
                    evaluate(p, stage, [(i, at) for at in starts])
        for p in chosen:
            finish(p, starts)

    def bred_out(p):
        return pltpu.make_async_copy(fin.at[pl.ds(2 * p - 1, 2)], bred_hbm.at[pl.ds(2 * p - 2, 2)], out_sem.at[p])

    inner([0], MIDDLE_RING)

    @pl.loop(0, members // 8)
    def _(q):
        inner([4 * q + j for j in range(1, 5)], MIDDLE_RING)

    for copy in x_copies(0, 1):
        copy.wait_recv()
    inner([0], OUTER_RINGS)
    for copy in x_copies(0, 0):
        copy.wait_recv()

    @pl.loop(0, members // 4)
    def _(q):
        @pl.when(q < members // 4 - 2)
        def _():
            for p in (2 * q + 5, 2 * q + 6):
                for copy in pair_y(p):
                    copy.start()

        inner([2 * q + 1, 2 * q + 2], OUTER_RINGS)

    for copy in x_copies(1, 1) + x_copies(2, 1) + control_y():
        copy.wait_recv()
    edges([0])
    for copy in x_copies(1, 0) + x_copies(2, 0):
        copy.wait_recv()

    @pl.loop(0, members // 4)
    def _(q):
        for p in (2 * q + 1, 2 * q + 2):
            for copy in pair_y(p):
                copy.wait_recv()
        edges([2 * q + 1, 2 * q + 2])
        for p in (2 * q + 1, 2 * q + 2):
            bred_out(p).start()

    @pl.loop(0, members // 4)
    def _(a):
        @pl.loop(0, a + 1)
        def _(b):
            total = [[None] * 4 for _ in range(4)]
            for f in range(3):
                for i in range(2):
                    x = [fin[1 + 4 * a + u, f, i] for u in range(4)]
                    y = [fin[1 + 4 * b + u, f, i] for u in range(4)]
                    for u in range(4):
                        for v in range(4):
                            z = jnp.sum((x[u] * y[v]).reshape(rows // 8, 8, 128), axis=0)
                            total[u][v] = z if total[u][v] is None else total[u][v] + z
            for u in range(4):
                for v in range(4):
                    parts[4 * a + u, 4 * b + v] = total[u][v]
                    parts[4 * b + v, 4 * a + u] = total[u][v]

    row_id = lax.broadcasted_iota(jnp.int32, (members, 128), 0)
    col_id = lax.broadcasted_iota(jnp.int32, (members, 128), 1)
    gram = jnp.zeros((members, 128), jnp.float32)
    for m in range(members):
        sums = jnp.sum(jnp.sum(parts[m], axis=1), axis=1, keepdims=True)
        gram = jnp.where(col_id == m, sums, gram)

    def all_sum(value, buf, me, count, peer_of, send, recv):
        buf[me] = value
        copies = []
        for d in range(1, count):
            copies.append(
                pltpu.make_async_remote_copy(
                    buf.at[me], buf.at[me], send.at[d], recv.at[d],
                    device_id=peer_of(lax.rem(me + d, count)), device_id_type=MESH)
            )
        for copy in copies:
            copy.start()
        for copy in copies:
            copy.wait_recv()
        out = buf[0]
        for d in range(1, count):
            out = out + buf[d]
        return out, copies

    packed = jnp.where(lane < members, gram[0:8], pltpu.roll(gram[8:16], members, 1))
    packed, sent1 = all_sum(packed, red1, gx, nx_dev, lambda i: (i, gy), r1_send, r1_recv)
    packed, sent2 = all_sum(packed, red2, gy, ny_dev, lambda i: (gx, i), r2_send, r2_recv)
    for copy in sent1 + sent2:
        copy.wait_send()
    @pl.loop(1, pairs)
    def _(p):
        bred_out(p).wait()

    for copy in [copy for key in everything for copy in x_copies(*key)] + control_y():
        copy.wait_send()

    @pl.loop(1, pairs)
    def _(p):
        for copy in pair_y(p):
            copy.wait_send()

    gram = jnp.concatenate([packed, pltpu.roll(packed, 128 - members, 1)], axis=0)

    work = jnp.where(col_id < members, gram, jnp.where(col_id - members == row_id, 1.0, 0.0))
    pivots = jnp.ones((members, 1), jnp.float32)
    for k in range(members):
        column = work[:, k : k + 1]
        pivot = column[k : k + 1]
        work = work - jnp.where(row_id > k, column, 0.0) * (work[k : k + 1] * (1.0 / pivot))
        pivots = jnp.where(row_id[:, :1] == k, pivot, pivots)
    factor_ref[...] = work / jnp.sqrt(pivots)


def apply_kernel(length, members, bred_hbm, factor_hbm, basis_hbm, rfac_hbm, bred, factor, table, out, rout, sem):
    first = pltpu.make_async_copy(factor_hbm, factor, sem.at[7])
    first.start()
    parts = [
        pltpu.make_async_copy(bred_hbm.at[:, pl.ds(f, 1), pl.ds(i, 1)], bred.at[:, pl.ds(f, 1), pl.ds(i, 1)], sem.at[8 + 2 * f + i])
        for f in range(3)
        for i in range(2)
    ]
    for copy in parts:
        copy.start()
    first.wait()
    row_id = lax.broadcasted_iota(jnp.int32, (members, members), 0)
    col_id = lax.broadcasted_iota(jnp.int32, (members, members), 1)
    rout[...] = jnp.where(row_id <= col_id, factor[:, :members] * (1.0 / math.sqrt(length)), 0.0)
    small = pltpu.make_async_copy(rout, rfac_hbm, sem.at[6])
    small.start()
    for j in range(members):
        column = factor[:, members + j : members + j + 1] * math.sqrt(length)
        table[j] = jnp.broadcast_to(column, (members, 128))
    copies = []
    for f in range(3):
        for i in range(2):
            parts[2 * f + i].wait()
            x = [bred[j, f, i] for j in range(members)]
            for m in range(members):
                total = table[0, m : m + 1, :] * x[0]
                for j in range(1, m + 1):
                    total = total + table[j, m : m + 1, :] * x[j]
                out[m, f, :, 128 * i : 128 * (i + 1)] = total
            half = (slice(None), pl.ds(f, 1), slice(None), pl.ds(128 * i, 128))
            copies.append(pltpu.make_async_copy(out.at[half], basis_hbm.at[half], sem.at[2 * f + i]))
            copies[-1].start()
    for copy in copies + [small]:
        copy.wait()


def body(control, perts):
    nx_dev, ny_dev = lax.axis_size("gx"), lax.axis_size("gy")
    members, _, rows, cols = perts.shape
    states, ext = members + 1, rows + 2 * HALO
    f32 = jnp.float32
    dma = pltpu.SemaphoreType.DMA
    vmem, hbm = pl.BlockSpec(memory_space=pltpu.VMEM), pl.BlockSpec(memory_space=pltpu.HBM)
    bred, factor = pl.pallas_call(
        functools.partial(kernel, nx_dev, ny_dev, members, rows, cols),
        out_shape=(
            jax.ShapeDtypeStruct((members, 3, 2, rows, 128), f32),
            jax.ShapeDtypeStruct((members, 128), f32),
        ),
        in_specs=[hbm] * 2,
        out_specs=[hbm, vmem],
        scratch_shapes=[
            pltpu.VMEM((states, 3, ext, cols), f32),
            pltpu.VMEM((2, 2, 3, rows, 128), f32),
            pltpu.VMEM((2, 2, 3, ext, 128), f32),
            pltpu.VMEM((256, 128), jnp.bfloat16),
            pltpu.VMEM((2 * STEPS, members // 2 + 1, 4, 5, ext, 128), f32),
            pltpu.VMEM((members // 2 + 1, 3, 5, rows, 128), f32),
            pltpu.VMEM((3, 5, ext, 128), f32),
            pltpu.VMEM((3, 5, rows, 128), f32),
            pltpu.VMEM((ext, 128), f32),
            pltpu.VMEM((states, 3, 2, rows, 128), f32),
            pltpu.VMEM((members, members, 8, 128), f32),
            pltpu.VMEM((nx_dev, 8, 128), f32),
            pltpu.VMEM((ny_dev, 8, 128), f32),
            dma((members // 4 + 1,)),
            dma((members // 2 + 1,)),
            dma((2, members // 2 + 1)),
            dma((2, members // 2 + 1)),
            dma((2, 3, 2)),
            dma((2, 3, 2)),
            dma((nx_dev,)),
            dma((nx_dev,)),
            dma((ny_dev,)),
            dma((ny_dev,)),
        ],
        compiler_params=pltpu.CompilerParams(
            collective_id=0, has_side_effects=True, vmem_limit_bytes=60 * 1024 * 1024
        ),
    )(control, perts)
    length = float(3 * rows * ny_dev * cols * nx_dev)
    return pl.pallas_call(
        functools.partial(apply_kernel, length, members),
        out_shape=(
            jax.ShapeDtypeStruct(perts.shape, f32),
            jax.ShapeDtypeStruct((members, members), f32),
        ),
        in_specs=[hbm] * 2,
        out_specs=[hbm] * 2,
        scratch_shapes=[
            pltpu.VMEM((members, 3, 2, rows, 128), f32),
            pltpu.VMEM((members, 128), f32),
            pltpu.VMEM((members, members, 128), f32),
            pltpu.VMEM((members, 3, rows, cols), f32),
            pltpu.VMEM((members, members), f32),
            dma((14,)),
        ],
        compiler_params=pltpu.CompilerParams(vmem_limit_bytes=60 * 1024 * 1024),
    )(bred, factor)


def solution(mesh):
    in_specs = (P(None, "gy", "gx"), P(None, None, "gy", "gx"))
    out_specs = (P(None, None, "gy", "gx"), P())
    return jax.shard_map(body, mesh=mesh, in_specs=in_specs, out_specs=out_specs, check_vma=False)
```

```python
import functools
import math

import jax
import jax.numpy as jnp
from jax import lax
from jax.experimental import pallas as pl
from jax.experimental.pallas import tpu as pltpu
from jax.sharding import PartitionSpec as P

MESH = pl.DeviceIdType.MESH
HALO = 8
STEPS = 2
ALL_RINGS, OUTER_RINGS, MIDDLE_RING = (0, 1, 2, 3, 4), (0, 1, 2, 3), (4,)
SAME_RING = ((0, 2), (1, 3), (4,))
MEAN_DEPTH = 4.0
TIME_STEP = 0.1
SCALE = TIME_STEP * (2.0 / 3.0)


def kernel(
    nx_dev, ny_dev, members, rows, cols,
    ctrl_hbm, perts_hbm, bred_hbm, factor_ref,
    st, pk, halo, pk1, halo1, band, stages, last, cini, cfin, cor, fin, parts, red1, red2,
    in_sem, out_sem, y_send, y_recv, x_send, x_recv, r1_send, r1_recv, r2_send, r2_recv,
):
    gx, gy = lax.axis_index("gx"), lax.axis_index("gy")
    ext = rows + 2 * HALO
    pairs = members // 2 + 1
    lane = lax.broadcasted_iota(jnp.int32, (8, 128), 1)
    left, right = lax.rem(gx + nx_dev - 1, nx_dev), lax.rem(gx + 1, nx_dev)
    up, down = lax.rem(gy + ny_dev - 1, ny_dev), lax.rem(gy + 1, ny_dev)

    def own_copy(k):
        source = ctrl_hbm if k == 0 else perts_hbm.at[pl.ds((k - 1) * 4, 4)]
        target = st.at[0] if k == 0 else st.at[pl.ds((k - 1) * 4 + 1, 4)]
        if k == 0:
            return pltpu.make_async_copy(source, target.at[:, pl.ds(HALO, rows), :], in_sem.at[k])
        return pltpu.make_async_copy(source, target.at[:, :, pl.ds(HALO, rows), :], in_sem.at[k])

    barrier = pltpu.get_barrier_semaphore()
    greeted = [(a, b) for a in (left, right) for b in (gy, up, down)] + [(gx, up), (gx, down)]
    greeted += [(lax.rem(gx + d, nx_dev), gy) for d in range(2, nx_dev - 1)]
    greeted += [(gx, lax.rem(gy + d, ny_dev)) for d in range(2, ny_dev - 1)]
    for peer in greeted[:8]:
        pl.semaphore_signal(barrier, inc=1, device_id=peer, device_id_type=MESH)
    for k in range(members // 4 + 1):
        own_copy(k).start()
    for peer in greeted[8:]:
        pl.semaphore_signal(barrier, inc=1, device_id=peer, device_id_type=MESH)

    pl.semaphore_wait(barrier, len(greeted))

    def y_copies(p, field_ref, st_ref):
        lead = (slice(None),) * (len(field_ref.shape) - 2)
        return [
            pltpu.make_async_remote_copy(
                field_ref.at[lead + (pl.ds(start, HALO),)],
                st_ref.at[lead + (pl.ds(to, HALO),)],
                y_send.at[way, p], y_recv.at[way, p], device_id=(gx, y_to), device_id_type=MESH)
            for way, (start, to, y_to) in enumerate(((0, HALO + rows, up), (rows - HALO, 0, down)))
        ]

    def control_y():
        return y_copies(0, ctrl_hbm, st.at[0])

    def pair_y(p):
        return y_copies(p, perts_hbm.at[pl.ds(2 * p - 2, 2)], st.at[pl.ds(2 * p - 1, 2)])

    for copy in control_y():
        copy.start()

    @pl.loop(1, 3)
    def _(p):
        for copy in pair_y(p):
            copy.start()

    for k in range(members // 4 + 1):
        own_copy(k).wait()

    wide = lax.broadcasted_iota(jnp.int32, (rows, 128), 1) // 8

    @pl.loop(0, 3)
    def _(f):
        first = jnp.zeros((rows, 128), jnp.float32)
        last = jnp.zeros((rows, 128), jnp.float32)
        for m in range(members):
            head = st[m + 1, f, HALO : HALO + rows, 0:128]
            tail = st[m + 1, f, HALO : HALO + rows, cols - 128 : cols]
            both = pltpu.roll(jnp.where(wide < 8, head, tail), (8 * m) % 128, 1)
            first = jnp.where(wide == m, both, first)
            last = jnp.where(wide == (m + 15) % 16, both, last)
        pk[0, f] = first
        pk[1, f] = last

    for side in range(2):
        both = jnp.zeros((rows, 128), jnp.float32)
        for f in range(3):
            tile = st[0, f, HALO : HALO + rows, 128 * side : 128 * (side + 1)]
            both = jnp.where(wide == f, pltpu.roll(tile, 8 * (f + side), 1), both)
        pk1[side] = both

    def x_copies(place, tile):
        start, count, to, y_to = ((0, rows, HALO, gy), (0, HALO, HALO + rows, up), (rows - HALO, HALO, 0, down))[place]
        source, target, lead = ((pk, halo, (slice(None),)), (pk1, halo1, ()))[tile]
        return [
            pltpu.make_async_remote_copy(
                source.at[(side,) + lead + (pl.ds(start, count),)],
                target.at[(side,) + lead + (pl.ds(to, count),)],
                x_send.at[side, place, tile], x_recv.at[side, place, tile],
                device_id=(x_to, y_to), device_id_type=MESH)
            for side, x_to in ((0, left), (1, right))
        ]

    everything = [(place, tile) for place in range(3) for tile in (1, 0)]
    for key in everything:
        for copy in x_copies(*key):
            copy.start()

    @pl.loop(3, pairs)
    def _(p):
        for copy in pair_y(p):
            copy.start()

    grid_rows = rows * ny_dev
    row = gy * rows - HALO + grid_rows + lax.broadcasted_iota(jnp.int32, (ext, 128), 0)
    row = lax.rem(row, grid_rows).astype(jnp.float32)
    cor[...] = TIME_STEP * 0.5 * (1.0 + 0.5 * jnp.sin(2.0 * math.pi * row / float(grid_rows)))

    k_id = lax.rem(lax.broadcasted_iota(jnp.int32, (256, 128), 0), 128)
    ahead = lax.rem(k_id - lax.broadcasted_iota(jnp.int32, (256, 128), 1) + 128, 128)
    weights = jnp.where(ahead == 1, 1.0, jnp.where(ahead == 127, -1.0, 0.0))
    weights = jnp.where(ahead == 2, -0.125, jnp.where(ahead == 126, 0.125, weights))
    band[...] = weights.astype(jnp.bfloat16)

    def of_control(p, rings):
        return [i for i in rings if i in (0, 1, 4)] if isinstance(p, int) else rings

    def assemble(p, starts, rings):
        control = isinstance(p, int)
        states = (0, 0) if control else (2 * p - 1, 2 * p)
        for at in starts:
            pick = slice(at, at + 8)
            state = []
            for f in range(3):
                tiles = [[st[k, f, pick, 128 * i : 128 * (i + 1)] for i in range(2)] for k in states]
                full = {}
                if 0 in rings:
                    for s, k in enumerate(states):
                        if control:
                            ends = (halo1[0, pick, :], halo1[1, pick, :])
                            beyond = jnp.where(lane < 8, pltpu.roll(ends[0], (128 - 8 * f) % 128, 1), pltpu.roll(ends[1], 120 - 8 * f, 1))
                        else:
                            ends = (halo[0, f, pick, :], halo[1, f, pick, :])
                            beyond = pltpu.roll(jnp.where(lane // 8 == k - 1, *ends), lax.rem(136 - 8 * k, 128), 1)
                        full[2 * s] = jnp.where(lane < 120, tiles[s][0], beyond)
                        full[2 * s + 1] = jnp.where(lane < 8, beyond, tiles[s][1])
                if 4 in rings:
                    middle = [jnp.where(lane < 64, high, low) for low, high in tiles]
                    full[4] = jnp.where((lane < 32) | (lane >= 96), middle[0], pltpu.roll(middle[1], 64, 1))
                scale = SCALE * SCALE if f == 0 else SCALE
                if control:
                    full = {i: scale * z + (scale * MEAN_DEPTH if f == 0 else 0.0) for i, z in full.items()}
                    for same in SAME_RING:
                        if same[0] in full:
                            for i in same:
                                cini[f, i, pick] = full[same[0]]
                else:
                    full = {i: cini[f, i, pick] + scale * z for i, z in full.items()}
                state.append(full)
            for i in of_control(p, rings):
                put_state(p, 0, i, at, *(state[f][i] for f in range(3)))

    def put_state(p, stage, i, at, h, e, n):
        for f, z in enumerate((h, e, n, h * n)):
            stages[stage, p, f, i, at : at + 8] = z

    def slopes_x(p, stage, units):
        h, e, n = ([stages[stage, p, f, i, at : at + 8] for i, at in units] for f in range(3))
        z = jnp.concatenate(h + e + n + [u * v for u, v in zip(h, e)], axis=0)
        top = z.astype(jnp.bfloat16)
        rest = (z - top.astype(jnp.float32)).astype(jnp.bfloat16)
        out = jnp.dot(jnp.concatenate([top, rest], axis=1), band[...], preferred_element_type=jnp.float32)
        return out.reshape(4, len(units), 8, 128)

    def slope_y(p, stage, f, i, at):
        z = [stages[stage, p, f, i, at + d : at + d + 8] for d in (-2, -1, 1, 2)]
        return (z[2] - z[1]) - 0.125 * (z[3] - z[0])

    def forward(p, stage, i, at, along):
        h, e, n = (stages[stage, p, f, i, at : at + 8] for f in range(3))
        c = cor[at : at + 8]
        new_h = h - along[3] - slope_y(p, stage, 3, i, at)
        new_e = e - (e * along[1] + n * (slope_y(p, stage, 1, i, at) - c) + along[0])
        new_n = n - (e * (along[2] + c) + n * slope_y(p, stage, 2, i, at) + slope_y(p, stage, 0, i, at))
        return new_h, new_e, new_n

    def evaluate(p, stage, units):
        along = slopes_x(p, stage, units)
        for j, (i, at) in enumerate(units):
            new = forward(p, stage, i, at, along[:, j])
            if stage % 2 == 1:
                new = [0.5 * (stages[stage - 1, p, f, i, at : at + 8] + new[f]) for f in range(3)]
            if stage < 2 * STEPS - 1:
                put_state(p, stage + 1, i, at, *new)
            else:
                for f in range(3):
                    last[p, f, i, at - HALO : at - HALO + 8] = new[f]

    def finish(p, starts):
        for f in range(3):
            scale = 1.0 / (SCALE * SCALE) if f == 0 else 1.0 / SCALE
            for at in starts:
                to = slice(at - HALO, at - HALO + 8)
                if isinstance(p, int):
                    for same in SAME_RING:
                        for i in same:
                            cfin[f, i, to] = last[p, f, same[0], to]
                    continue
                z = [scale * (last[p, f, i, to] - cfin[f, i, to]) for i in ALL_RINGS]
                for s, k in enumerate((2 * p - 1, 2 * p)):
                    both = z[4] if s == 0 else pltpu.roll(z[4], 64, 1)
                    fin[k, f, 0, to, :] = jnp.where(lane < 112, z[2 * s], both)
                    fin[k, f, 1, to, :] = jnp.where(lane < 16, both, z[2 * s + 1])

    def inner(chosen, rings):
        for p in chosen:
            assemble(p, range(HALO, HALO + rows, 8), rings)
        for stage in range(2 * STEPS):
            low, high = HALO + 2 * stage + 2, HALO + rows - 2 * stage - 2
            starts = [min(at, high - 8) for at in range(low, high, 8)]
            for p in chosen:
                for i in of_control(p, rings):
                    evaluate(p, stage, [(i, at) for at in starts])
        if 0 in rings:
            for p in chosen:
                finish(p, starts)

    def edges(chosen):
        for p in chosen:
            assemble(p, (0, HALO + rows), ALL_RINGS)
        for stage in range(2 * STEPS):
            starts = (2 * stage + 2, rows + 2 * HALO - 2 * stage - 10)
            for p in chosen:
                for i in of_control(p, ALL_RINGS):
                    evaluate(p, stage, [(i, at) for at in starts])
        for p in chosen:
            finish(p, starts)

    def bred_out(p):
        return pltpu.make_async_copy(fin.at[pl.ds(2 * p - 1, 2)], bred_hbm.at[pl.ds(2 * p - 2, 2)], out_sem.at[p])

    inner([0], MIDDLE_RING)

    @pl.loop(0, members // 8)
    def _(q):
        inner([4 * q + j for j in range(1, 5)], MIDDLE_RING)

    for copy in x_copies(0, 1):
        copy.wait_recv()
    inner([0], OUTER_RINGS)
    for copy in x_copies(0, 0):
        copy.wait_recv()

    @pl.loop(0, members // 4)
    def _(q):
        inner([2 * q + 1, 2 * q + 2], OUTER_RINGS)

    def products(a, b, cuts, fresh):
        total = [[None] * 4 for _ in range(4)]
        for f in range(3):
            for i in range(2):
                for cut in cuts:
                    x = [fin[1 + 4 * a + u, f, i, cut] for u in range(4)]
                    y = [fin[1 + 4 * b + u, f, i, cut] for u in range(4)]
                    for u in range(4):
                        for v in range(4):
                            z = x[u] * y[v]
                            total[u][v] = z if total[u][v] is None else total[u][v] + z
        if not fresh:
            total = [[parts[4 * a + u, 4 * b + v] + total[u][v] for v in range(4)] for u in range(4)]
        for u in range(4):
            for v in range(4):
                parts[4 * a + u, 4 * b + v] = total[u][v]
                if not fresh:
                    parts[4 * b + v, 4 * a + u] = total[u][v]

    @pl.loop(0, members // 4)
    def _(a):
        @pl.loop(0, a + 1)
        def _(b):
            products(a, b, [slice(at, at + 8) for at in range(8, rows - 8, 8)], True)

    for copy in x_copies(1, 1) + x_copies(2, 1) + control_y():
        copy.wait_recv()
    edges([0])
    for copy in x_copies(1, 0) + x_copies(2, 0):
        copy.wait_recv()

    @pl.loop(1, pairs)
    def _(p):
        for copy in pair_y(p):
            copy.wait_recv()
        edges([p])
        bred_out(p).start()

        @pl.when(p % 2 == 0)
        def _():
            @pl.loop(0, p // 2)
            def _(b):
                products(p // 2 - 1, b, [slice(0, 8), slice(rows - 8, rows)], False)

    row_id = lax.broadcasted_iota(jnp.int32, (members, 128), 0)
    col_id = lax.broadcasted_iota(jnp.int32, (members, 128), 1)
    gram = jnp.zeros((members, 128), jnp.float32)
    for m in range(members):
        sums = jnp.sum(jnp.sum(parts[m], axis=1), axis=1, keepdims=True)
        gram = jnp.where(col_id == m, sums, gram)

    def all_sum(value, buf, me, count, peer_of, send, recv):
        buf[me] = value
        copies = []
        for d in range(1, count):
            copies.append(
                pltpu.make_async_remote_copy(
                    buf.at[me], buf.at[me], send.at[d], recv.at[d],
                    device_id=peer_of(lax.rem(me + d, count)), device_id_type=MESH)
            )
        for copy in copies:
            copy.start()
        for copy in copies:
            copy.wait_recv()
        out = buf[0]
        for d in range(1, count):
            out = out + buf[d]
        return out, copies

    packed = jnp.where(lane < members, gram[0:8], pltpu.roll(gram[8:16], members, 1))
    packed, sent1 = all_sum(packed, red1, gx, nx_dev, lambda i: (i, gy), r1_send, r1_recv)
    packed, sent2 = all_sum(packed, red2, gy, ny_dev, lambda i: (gx, i), r2_send, r2_recv)
    for copy in sent1 + sent2:
        copy.wait_send()
    @pl.loop(1, pairs)
    def _(p):
        bred_out(p).wait()

    for copy in [copy for key in everything for copy in x_copies(*key)] + control_y():
        copy.wait_send()

    @pl.loop(1, pairs)
    def _(p):
        for copy in pair_y(p):
            copy.wait_send()

    gram = jnp.concatenate([packed, pltpu.roll(packed, 128 - members, 1)], axis=0)

    work = jnp.where(col_id < members, gram, jnp.where(col_id - members == row_id, 1.0, 0.0))
    pivots = jnp.ones((members, 1), jnp.float32)
    for k in range(members):
        column = work[:, k : k + 1]
        pivot = column[k : k + 1]
        work = work - jnp.where(row_id > k, column, 0.0) * (work[k : k + 1] * (1.0 / pivot))
        pivots = jnp.where(row_id[:, :1] == k, pivot, pivots)
    factor_ref[...] = work / jnp.sqrt(pivots)


def apply_kernel(length, members, bred_hbm, factor_hbm, basis_hbm, rfac_hbm, bred, factor, table, out, rout, sem):
    first = pltpu.make_async_copy(factor_hbm, factor, sem.at[7])
    first.start()
    parts = [
        pltpu.make_async_copy(bred_hbm.at[:, pl.ds(f, 1), pl.ds(i, 1)], bred.at[:, pl.ds(f, 1), pl.ds(i, 1)], sem.at[8 + 2 * f + i])
        for f in range(3)
        for i in range(2)
    ]
    for copy in parts:
        copy.start()
    first.wait()
    row_id = lax.broadcasted_iota(jnp.int32, (members, members), 0)
    col_id = lax.broadcasted_iota(jnp.int32, (members, members), 1)
    rout[...] = jnp.where(row_id <= col_id, factor[:, :members] * (1.0 / math.sqrt(length)), 0.0)
    small = pltpu.make_async_copy(rout, rfac_hbm, sem.at[6])
    small.start()
    for j in range(members):
        column = factor[:, members + j : members + j + 1] * math.sqrt(length)
        table[j] = jnp.broadcast_to(column, (members, 128))
    copies = []
    for f in range(3):
        for i in range(2):
            parts[2 * f + i].wait()
            x = [bred[j, f, i] for j in range(members)]
            for m in range(members):
                total = table[0, m : m + 1, :] * x[0]
                for j in range(1, m + 1):
                    total = total + table[j, m : m + 1, :] * x[j]
                out[m, f, :, 128 * i : 128 * (i + 1)] = total
            half = (slice(None), pl.ds(f, 1), slice(None), pl.ds(128 * i, 128))
            copies.append(pltpu.make_async_copy(out.at[half], basis_hbm.at[half], sem.at[2 * f + i]))
            copies[-1].start()
    for copy in copies + [small]:
        copy.wait()


def body(control, perts):
    nx_dev, ny_dev = lax.axis_size("gx"), lax.axis_size("gy")
    members, _, rows, cols = perts.shape
    states, ext = members + 1, rows + 2 * HALO
    f32 = jnp.float32
    dma = pltpu.SemaphoreType.DMA
    vmem, hbm = pl.BlockSpec(memory_space=pltpu.VMEM), pl.BlockSpec(memory_space=pltpu.HBM)
    bred, factor = pl.pallas_call(
        functools.partial(kernel, nx_dev, ny_dev, members, rows, cols),
        out_shape=(
            jax.ShapeDtypeStruct((members, 3, 2, rows, 128), f32),
            jax.ShapeDtypeStruct((members, 128), f32),
        ),
        in_specs=[hbm] * 2,
        out_specs=[hbm, vmem],
        scratch_shapes=[
            pltpu.VMEM((states, 3, ext, cols), f32),
            pltpu.VMEM((2, 3, rows, 128), f32),
            pltpu.VMEM((2, 3, ext, 128), f32),
            pltpu.VMEM((2, rows, 128), f32),
            pltpu.VMEM((2, ext, 128), f32),
            pltpu.VMEM((256, 128), jnp.bfloat16),
            pltpu.VMEM((2 * STEPS, members // 2 + 1, 4, 5, ext, 128), f32),
            pltpu.VMEM((members // 2 + 1, 3, 5, rows, 128), f32),
            pltpu.VMEM((3, 5, ext, 128), f32),
            pltpu.VMEM((3, 5, rows, 128), f32),
            pltpu.VMEM((ext, 128), f32),
            pltpu.VMEM((states, 3, 2, rows, 128), f32),
            pltpu.VMEM((members, members, 8, 128), f32),
            pltpu.VMEM((nx_dev, 8, 128), f32),
            pltpu.VMEM((ny_dev, 8, 128), f32),
            dma((members // 4 + 1,)),
            dma((members // 2 + 1,)),
            dma((2, members // 2 + 1)),
            dma((2, members // 2 + 1)),
            dma((2, 3, 2)),
            dma((2, 3, 2)),
            dma((nx_dev,)),
            dma((nx_dev,)),
            dma((ny_dev,)),
            dma((ny_dev,)),
        ],
        compiler_params=pltpu.CompilerParams(
            collective_id=0, has_side_effects=True, vmem_limit_bytes=60 * 1024 * 1024
        ),
    )(control, perts)
    length = float(3 * rows * ny_dev * cols * nx_dev)
    return pl.pallas_call(
        functools.partial(apply_kernel, length, members),
        out_shape=(
            jax.ShapeDtypeStruct(perts.shape, f32),
            jax.ShapeDtypeStruct((members, members), f32),
        ),
        in_specs=[hbm] * 2,
        out_specs=[hbm] * 2,
        scratch_shapes=[
            pltpu.VMEM((members, 3, 2, rows, 128), f32),
            pltpu.VMEM((members, 128), f32),
            pltpu.VMEM((members, members, 128), f32),
            pltpu.VMEM((members, 3, rows, cols), f32),
            pltpu.VMEM((members, members), f32),
            dma((14,)),
        ],
        compiler_params=pltpu.CompilerParams(vmem_limit_bytes=60 * 1024 * 1024),
    )(bred, factor)


def solution(mesh):
    in_specs = (P(None, "gy", "gx"), P(None, None, "gy", "gx"))
    out_specs = (P(None, None, "gy", "gx"), P())
    return jax.shard_map(body, mesh=mesh, in_specs=in_specs, out_specs=out_specs, check_vma=False)
```

```python
import functools
import math

import jax
import jax.numpy as jnp
from jax import lax
from jax.experimental import pallas as pl
from jax.experimental.pallas import tpu as pltpu
from jax.sharding import PartitionSpec as P

MESH = pl.DeviceIdType.MESH
HALO = 8
STEPS = 2
ALL_RINGS, OUTER_RINGS, MIDDLE_RING = (0, 1, 2, 3, 4), (0, 1, 2, 3), (4,)
SAME_RING = ((0, 2), (1, 3), (4,))
MEAN_DEPTH = 4.0
TIME_STEP = 0.1
SCALE = TIME_STEP * (2.0 / 3.0)


def kernel(
    nx_dev, ny_dev, members, rows, cols,
    ctrl_hbm, perts_hbm, bred_hbm, factor_ref,
    st, pk, halo, pk1, halo1, band, stages, last, cini, cfin, cor, fin, parts, red1, red2,
    in_sem, out_sem, y_send, y_recv, x_send, x_recv, r1_send, r1_recv, r2_send, r2_recv,
):
    gx, gy = lax.axis_index("gx"), lax.axis_index("gy")
    ext = rows + 2 * HALO
    pairs = members // 2 + 1
    lane = lax.broadcasted_iota(jnp.int32, (8, 128), 1)
    left, right = lax.rem(gx + nx_dev - 1, nx_dev), lax.rem(gx + 1, nx_dev)
    up, down = lax.rem(gy + ny_dev - 1, ny_dev), lax.rem(gy + 1, ny_dev)

    def own_copy(k):
        source = ctrl_hbm if k == 0 else perts_hbm.at[pl.ds((k - 1) * 4, 4)]
        target = st.at[0] if k == 0 else st.at[pl.ds((k - 1) * 4 + 1, 4)]
        if k == 0:
            return pltpu.make_async_copy(source, target.at[:, pl.ds(HALO, rows), :], in_sem.at[k])
        return pltpu.make_async_copy(source, target.at[:, :, pl.ds(HALO, rows), :], in_sem.at[k])

    barrier = pltpu.get_barrier_semaphore()
    greeted = [(a, b) for a in (left, right) for b in (gy, up, down)] + [(gx, up), (gx, down)]
    greeted += [(lax.rem(gx + d, nx_dev), gy) for d in range(2, nx_dev - 1)]
    greeted += [(gx, lax.rem(gy + d, ny_dev)) for d in range(2, ny_dev - 1)]
    for peer in greeted[:8]:
        pl.semaphore_signal(barrier, inc=1, device_id=peer, device_id_type=MESH)
    for k in range(members // 4 + 1):
        own_copy(k).start()
    for peer in greeted[8:]:
        pl.semaphore_signal(barrier, inc=1, device_id=peer, device_id_type=MESH)

    def y_copies(p, field_ref, st_ref):
        lead = (slice(None),) * (len(field_ref.shape) - 2)
        return [
            pltpu.make_async_remote_copy(
                field_ref.at[lead + (pl.ds(start, HALO),)],
                st_ref.at[lead + (pl.ds(to, HALO),)],
                y_send.at[way, p], y_recv.at[way, p], device_id=(gx, y_to), device_id_type=MESH)
            for way, (start, to, y_to) in enumerate(((0, HALO + rows, up), (rows - HALO, 0, down)))
        ]

    def control_y():
        return y_copies(0, ctrl_hbm, st.at[0])

    def pair_y(p):
        return y_copies(p, perts_hbm.at[pl.ds(2 * p - 2, 2)], st.at[pl.ds(2 * p - 1, 2)])

    for k in range(members // 4 + 1):
        own_copy(k).wait()

    wide = lax.broadcasted_iota(jnp.int32, (rows, 128), 1) // 8

    @pl.loop(0, 3)
    def _(f):
        first = jnp.zeros((rows, 128), jnp.float32)
        last = jnp.zeros((rows, 128), jnp.float32)
        for m in range(members):
            head = st[m + 1, f, HALO : HALO + rows, 0:128]
            tail = st[m + 1, f, HALO : HALO + rows, cols - 128 : cols]
            both = pltpu.roll(jnp.where(wide < 8, head, tail), (8 * m) % 128, 1)
            first = jnp.where(wide == m, both, first)
            last = jnp.where(wide == (m + 15) % 16, both, last)
        pk[0, f] = first
        pk[1, f] = last

    for side in range(2):
        both = jnp.zeros((rows, 128), jnp.float32)
        for f in range(3):
            tile = st[0, f, HALO : HALO + rows, 128 * side : 128 * (side + 1)]
            both = jnp.where(wide == f, pltpu.roll(tile, 8 * (f + side), 1), both)
        pk1[side] = both

    def x_copies(place, tile):
        start, count, to, y_to = ((0, rows, HALO, gy), (0, HALO, HALO + rows, up), (rows - HALO, HALO, 0, down))[place]
        source, target, lead = ((pk, halo, (slice(None),)), (pk1, halo1, ()))[tile]
        return [
            pltpu.make_async_remote_copy(
                source.at[(side,) + lead + (pl.ds(start, count),)],
                target.at[(side,) + lead + (pl.ds(to, count),)],
                x_send.at[side, place, tile], x_recv.at[side, place, tile],
                device_id=(x_to, y_to), device_id_type=MESH)
            for side, x_to in ((0, left), (1, right))
        ]

    everything = [(place, tile) for place in range(3) for tile in (1, 0)]
    pl.semaphore_wait(barrier, len(greeted))

    for key in everything:
        for copy in x_copies(*key):
            copy.start()

    for copy in control_y():
        copy.start()

    @pl.loop(1, pairs)
    def _(p):
        for copy in pair_y(p):
            copy.start()

    grid_rows = rows * ny_dev
    row = gy * rows - HALO + grid_rows + lax.broadcasted_iota(jnp.int32, (ext, 128), 0)
    row = lax.rem(row, grid_rows).astype(jnp.float32)
    cor[...] = TIME_STEP * 0.5 * (1.0 + 0.5 * jnp.sin(2.0 * math.pi * row / float(grid_rows)))

    k_id = lax.rem(lax.broadcasted_iota(jnp.int32, (256, 128), 0), 128)
    ahead = lax.rem(k_id - lax.broadcasted_iota(jnp.int32, (256, 128), 1) + 128, 128)
    weights = jnp.where(ahead == 1, 1.0, jnp.where(ahead == 127, -1.0, 0.0))
    weights = jnp.where(ahead == 2, -0.125, jnp.where(ahead == 126, 0.125, weights))
    band[...] = weights.astype(jnp.bfloat16)

    def of_control(p, rings):
        return [i for i in rings if i in (0, 1, 4)] if isinstance(p, int) else rings

    def assemble(p, starts, rings):
        control = isinstance(p, int)
        states = (0, 0) if control else (2 * p - 1, 2 * p)
        for at in starts:
            pick = slice(at, at + 8)
            state = []
            for f in range(3):
                tiles = [[st[k, f, pick, 128 * i : 128 * (i + 1)] for i in range(2)] for k in states]
                full = {}
                if 0 in rings:
                    for s, k in enumerate(states):
                        if control:
                            ends = (halo1[0, pick, :], halo1[1, pick, :])
                            beyond = jnp.where(lane < 8, pltpu.roll(ends[0], (128 - 8 * f) % 128, 1), pltpu.roll(ends[1], 120 - 8 * f, 1))
                        else:
                            ends = (halo[0, f, pick, :], halo[1, f, pick, :])
                            beyond = pltpu.roll(jnp.where(lane // 8 == k - 1, *ends), lax.rem(136 - 8 * k, 128), 1)
                        full[2 * s] = jnp.where(lane < 120, tiles[s][0], beyond)
                        full[2 * s + 1] = jnp.where(lane < 8, beyond, tiles[s][1])
                if 4 in rings:
                    middle = [jnp.where(lane < 64, high, low) for low, high in tiles]
                    full[4] = jnp.where((lane < 32) | (lane >= 96), middle[0], pltpu.roll(middle[1], 64, 1))
                scale = SCALE * SCALE if f == 0 else SCALE
                if control:
                    full = {i: scale * z + (scale * MEAN_DEPTH if f == 0 else 0.0) for i, z in full.items()}
                    for same in SAME_RING:
                        if same[0] in full:
                            for i in same:
                                cini[f, i, pick] = full[same[0]]
                else:
                    full = {i: cini[f, i, pick] + scale * z for i, z in full.items()}
                state.append(full)
            for i in of_control(p, rings):
                put_state(p, 0, i, at, *(state[f][i] for f in range(3)))

    def put_state(p, stage, i, at, h, e, n):
        for f, z in enumerate((h, e, n, h * n)):
            stages[stage, p, f, i, at : at + 8] = z

    def slopes_x(p, stage, units):
        h, e, n = ([stages[stage, p, f, i, at : at + 8] for i, at in units] for f in range(3))
        z = jnp.concatenate(h + e + n + [u * v for u, v in zip(h, e)], axis=0)
        top = z.astype(jnp.bfloat16)
        rest = (z - top.astype(jnp.float32)).astype(jnp.bfloat16)
        out = jnp.dot(jnp.concatenate([top, rest], axis=1), band[...], preferred_element_type=jnp.float32)
        return out.reshape(4, len(units), 8, 128)

    def slope_y(p, stage, f, i, at):
        z = [stages[stage, p, f, i, at + d : at + d + 8] for d in (-2, -1, 1, 2)]
        return (z[2] - z[1]) - 0.125 * (z[3] - z[0])

    def forward(p, stage, i, at, along):
        h, e, n = (stages[stage, p, f, i, at : at + 8] for f in range(3))
        c = cor[at : at + 8]
        new_h = h - along[3] - slope_y(p, stage, 3, i, at)
        new_e = e - (e * along[1] + n * (slope_y(p, stage, 1, i, at) - c) + along[0])
        new_n = n - (e * (along[2] + c) + n * slope_y(p, stage, 2, i, at) + slope_y(p, stage, 0, i, at))
        return new_h, new_e, new_n

    def evaluate(p, stage, units):
        along = slopes_x(p, stage, units)
        for j, (i, at) in enumerate(units):
            new = forward(p, stage, i, at, along[:, j])
            if stage % 2 == 1:
                new = [0.5 * (stages[stage - 1, p, f, i, at : at + 8] + new[f]) for f in range(3)]
            if stage < 2 * STEPS - 1:
                put_state(p, stage + 1, i, at, *new)
            else:
                for f in range(3):
                    last[p, f, i, at - HALO : at - HALO + 8] = new[f]

    def finish(p, starts):
        for f in range(3):
            scale = 1.0 / (SCALE * SCALE) if f == 0 else 1.0 / SCALE
            for at in starts:
                to = slice(at - HALO, at - HALO + 8)
                if isinstance(p, int):
                    for same in SAME_RING:
                        for i in same:
                            cfin[f, i, to] = last[p, f, same[0], to]
                    continue
                z = [scale * (last[p, f, i, to] - cfin[f, i, to]) for i in ALL_RINGS]
                for s, k in enumerate((2 * p - 1, 2 * p)):
                    both = z[4] if s == 0 else pltpu.roll(z[4], 64, 1)
                    fin[k, f, 0, to, :] = jnp.where(lane < 112, z[2 * s], both)
                    fin[k, f, 1, to, :] = jnp.where(lane < 16, both, z[2 * s + 1])

    def inner(chosen, rings):
        for p in chosen:
            assemble(p, range(HALO, HALO + rows, 8), rings)
        for stage in range(2 * STEPS):
            low, high = HALO + 2 * stage + 2, HALO + rows - 2 * stage - 2
            starts = [min(at, high - 8) for at in range(low, high, 8)]
            for p in chosen:
                for i in of_control(p, rings):
                    evaluate(p, stage, [(i, at) for at in starts])
        if 0 in rings:
            for p in chosen:
                finish(p, starts)

    def edges(chosen):
        for p in chosen:
            assemble(p, (0, HALO + rows), ALL_RINGS)
        for stage in range(2 * STEPS):
            starts = (2 * stage + 2, rows + 2 * HALO - 2 * stage - 10)
            for p in chosen:
                for i in of_control(p, ALL_RINGS):
                    evaluate(p, stage, [(i, at) for at in starts])
        for p in chosen:
            finish(p, starts)

    def bred_out(p):
        return pltpu.make_async_copy(fin.at[pl.ds(2 * p - 1, 2)], bred_hbm.at[pl.ds(2 * p - 2, 2)], out_sem.at[p])

    inner([0], MIDDLE_RING)

    @pl.loop(0, members // 8)
    def _(q):
        inner([4 * q + j for j in range(1, 5)], MIDDLE_RING)

    for copy in x_copies(0, 1):
        copy.wait_recv()
    inner([0], OUTER_RINGS)
    for copy in x_copies(0, 0):
        copy.wait_recv()

    @pl.loop(0, members // 4)
    def _(q):
        inner([2 * q + 1, 2 * q + 2], OUTER_RINGS)

    def products(a, b, cuts, fresh):
        total = [[None] * 4 for _ in range(4)]
        for f in range(3):
            for i in range(2):
                for cut in cuts:
                    x = [fin[1 + 4 * a + u, f, i, cut] for u in range(4)]
                    y = [fin[1 + 4 * b + u, f, i, cut] for u in range(4)]
                    for u in range(4):
                        for v in range(4):
                            z = x[u] * y[v]
                            total[u][v] = z if total[u][v] is None else total[u][v] + z
        if not fresh:
            total = [[parts[4 * a + u, 4 * b + v] + total[u][v] for v in range(4)] for u in range(4)]
        for u in range(4):
            for v in range(4):
                parts[4 * a + u, 4 * b + v] = total[u][v]
                if not fresh:
                    parts[4 * b + v, 4 * a + u] = total[u][v]

    @pl.loop(0, members // 4)
    def _(a):
        @pl.loop(0, a + 1)
        def _(b):
            products(a, b, [slice(at, at + 8) for at in range(8, rows - 8, 8)], True)

    for copy in x_copies(1, 1) + x_copies(2, 1) + control_y():
        copy.wait_recv()
    edges([0])
    for copy in x_copies(1, 0) + x_copies(2, 0):
        copy.wait_recv()

    @pl.loop(0, members // 4)
    def _(q):
        for p in (2 * q + 1, 2 * q + 2):
            for copy in pair_y(p):
                copy.wait_recv()
        edges([2 * q + 1, 2 * q + 2])
        for p in (2 * q + 1, 2 * q + 2):
            bred_out(p).start()

    @pl.loop(0, members // 4)
    def _(a):
        @pl.loop(0, a + 1)
        def _(b):
            products(a, b, [slice(0, 8), slice(rows - 8, rows)], False)

    row_id = lax.broadcasted_iota(jnp.int32, (members, 128), 0)
    col_id = lax.broadcasted_iota(jnp.int32, (members, 128), 1)
    gram = jnp.zeros((members, 128), jnp.float32)
    for m in range(members):
        sums = jnp.sum(jnp.sum(parts[m], axis=1), axis=1, keepdims=True)
        gram = jnp.where(col_id == m, sums, gram)

    def all_sum(value, buf, me, count, peer_of, send, recv):
        buf[me] = value
        copies = []
        for d in range(1, count):
            copies.append(
                pltpu.make_async_remote_copy(
                    buf.at[me], buf.at[me], send.at[d], recv.at[d],
                    device_id=peer_of(lax.rem(me + d, count)), device_id_type=MESH)
            )
        for copy in copies:
            copy.start()
        for copy in copies:
            copy.wait_recv()
        out = buf[0]
        for d in range(1, count):
            out = out + buf[d]
        return out, copies

    packed = jnp.where(lane < members, gram[0:8], pltpu.roll(gram[8:16], members, 1))
    packed, sent1 = all_sum(packed, red1, gx, nx_dev, lambda i: (i, gy), r1_send, r1_recv)
    packed, sent2 = all_sum(packed, red2, gy, ny_dev, lambda i: (gx, i), r2_send, r2_recv)
    for copy in sent1 + sent2:
        copy.wait_send()
    @pl.loop(1, pairs)
    def _(p):
        bred_out(p).wait()

    for copy in [copy for key in everything for copy in x_copies(*key)] + control_y():
        copy.wait_send()

    @pl.loop(1, pairs)
    def _(p):
        for copy in pair_y(p):
            copy.wait_send()

    gram = jnp.concatenate([packed, pltpu.roll(packed, 128 - members, 1)], axis=0)

    work = jnp.where(col_id < members, gram, jnp.where(col_id - members == row_id, 1.0, 0.0))
    pivots = jnp.ones((members, 1), jnp.float32)
    for k in range(members):
        column = work[:, k : k + 1]
        pivot = column[k : k + 1]
        work = work - jnp.where(row_id > k, column, 0.0) * (work[k : k + 1] * (1.0 / pivot))
        pivots = jnp.where(row_id[:, :1] == k, pivot, pivots)
    factor_ref[...] = work / jnp.sqrt(pivots)


def apply_kernel(length, members, bred_hbm, factor_hbm, basis_hbm, rfac_hbm, bred, factor, table, out, rout, sem):
    first = pltpu.make_async_copy(factor_hbm, factor, sem.at[7])
    first.start()
    parts = [
        pltpu.make_async_copy(bred_hbm.at[:, pl.ds(f, 1), pl.ds(i, 1)], bred.at[:, pl.ds(f, 1), pl.ds(i, 1)], sem.at[8 + 2 * f + i])
        for f in range(3)
        for i in range(2)
    ]
    for copy in parts:
        copy.start()
    first.wait()
    row_id = lax.broadcasted_iota(jnp.int32, (members, members), 0)
    col_id = lax.broadcasted_iota(jnp.int32, (members, members), 1)
    rout[...] = jnp.where(row_id <= col_id, factor[:, :members] * (1.0 / math.sqrt(length)), 0.0)
    small = pltpu.make_async_copy(rout, rfac_hbm, sem.at[6])
    small.start()
    for j in range(members):
        column = factor[:, members + j : members + j + 1] * math.sqrt(length)
        table[j] = jnp.broadcast_to(column, (members, 128))
    copies = []
    for f in range(3):
        for i in range(2):
            parts[2 * f + i].wait()
            x = [bred[j, f, i] for j in range(members)]
            for m in range(members):
                total = table[0, m : m + 1, :] * x[0]
                for j in range(1, m + 1):
                    total = total + table[j, m : m + 1, :] * x[j]
                out[m, f, :, 128 * i : 128 * (i + 1)] = total
            half = (slice(None), pl.ds(f, 1), slice(None), pl.ds(128 * i, 128))
            copies.append(pltpu.make_async_copy(out.at[half], basis_hbm.at[half], sem.at[2 * f + i]))
            copies[-1].start()
    for copy in copies + [small]:
        copy.wait()


def body(control, perts):
    nx_dev, ny_dev = lax.axis_size("gx"), lax.axis_size("gy")
    members, _, rows, cols = perts.shape
    states, ext = members + 1, rows + 2 * HALO
    f32 = jnp.float32
    dma = pltpu.SemaphoreType.DMA
    vmem, hbm = pl.BlockSpec(memory_space=pltpu.VMEM), pl.BlockSpec(memory_space=pltpu.HBM)
    bred, factor = pl.pallas_call(
        functools.partial(kernel, nx_dev, ny_dev, members, rows, cols),
        out_shape=(
            jax.ShapeDtypeStruct((members, 3, 2, rows, 128), f32),
            jax.ShapeDtypeStruct((members, 128), f32),
        ),
        in_specs=[hbm] * 2,
        out_specs=[hbm, vmem],
        scratch_shapes=[
            pltpu.VMEM((states, 3, ext, cols), f32),
            pltpu.VMEM((2, 3, rows, 128), f32),
            pltpu.VMEM((2, 3, ext, 128), f32),
            pltpu.VMEM((2, rows, 128), f32),
            pltpu.VMEM((2, ext, 128), f32),
            pltpu.VMEM((256, 128), jnp.bfloat16),
            pltpu.VMEM((2 * STEPS, members // 2 + 1, 4, 5, ext, 128), f32),
            pltpu.VMEM((members // 2 + 1, 3, 5, rows, 128), f32),
            pltpu.VMEM((3, 5, ext, 128), f32),
            pltpu.VMEM((3, 5, rows, 128), f32),
            pltpu.VMEM((ext, 128), f32),
            pltpu.VMEM((states, 3, 2, rows, 128), f32),
            pltpu.VMEM((members, members, 8, 128), f32),
            pltpu.VMEM((nx_dev, 8, 128), f32),
            pltpu.VMEM((ny_dev, 8, 128), f32),
            dma((members // 4 + 1,)),
            dma((members // 2 + 1,)),
            dma((2, members // 2 + 1)),
            dma((2, members // 2 + 1)),
            dma((2, 3, 2)),
            dma((2, 3, 2)),
            dma((nx_dev,)),
            dma((nx_dev,)),
            dma((ny_dev,)),
            dma((ny_dev,)),
        ],
        compiler_params=pltpu.CompilerParams(
            collective_id=0, has_side_effects=True, vmem_limit_bytes=60 * 1024 * 1024
        ),
    )(control, perts)
    length = float(3 * rows * ny_dev * cols * nx_dev)
    return pl.pallas_call(
        functools.partial(apply_kernel, length, members),
        out_shape=(
            jax.ShapeDtypeStruct(perts.shape, f32),
            jax.ShapeDtypeStruct((members, members), f32),
        ),
        in_specs=[hbm] * 2,
        out_specs=[hbm] * 2,
        scratch_shapes=[
            pltpu.VMEM((members, 3, 2, rows, 128), f32),
            pltpu.VMEM((members, 128), f32),
            pltpu.VMEM((members, members, 128), f32),
            pltpu.VMEM((members, 3, rows, cols), f32),
            pltpu.VMEM((members, members), f32),
            dma((14,)),
        ],
        compiler_params=pltpu.CompilerParams(vmem_limit_bytes=60 * 1024 * 1024),
    )(bred, factor)


def solution(mesh):
    in_specs = (P(None, "gy", "gx"), P(None, None, "gy", "gx"))
    out_specs = (P(None, None, "gy", "gx"), P())
    return jax.shard_map(body, mesh=mesh, in_specs=in_specs, out_specs=out_specs, check_vma=False)
```

```python
import functools
import math

import jax
import jax.numpy as jnp
from jax import lax
from jax.experimental import pallas as pl
from jax.experimental.pallas import tpu as pltpu
from jax.sharding import PartitionSpec as P

MESH = pl.DeviceIdType.MESH
HALO = 8
STEPS = 2
ALL_RINGS, OUTER_RINGS, MIDDLE_RING = (0, 1, 2, 3, 4), (0, 1, 2, 3), (4,)
SAME_RING = ((0, 2), (1, 3), (4,))
MEAN_DEPTH = 4.0
TIME_STEP = 0.1
SCALE = TIME_STEP * (2.0 / 3.0)


def kernel(
    nx_dev, ny_dev, members, rows, cols,
    ctrl_hbm, perts_hbm, bred_hbm, factor_ref,
    st, pk, halo, pk1, halo1, band, stages, last, cini, cfin, cor, fin, parts, red1, red2,
    in_sem, out_sem, y_send, y_recv, x_send, x_recv, r1_send, r1_recv, r2_send, r2_recv,
):
    gx, gy = lax.axis_index("gx"), lax.axis_index("gy")
    ext = rows + 2 * HALO
    pairs = members // 2 + 1
    lane = lax.broadcasted_iota(jnp.int32, (8, 128), 1)
    left, right = lax.rem(gx + nx_dev - 1, nx_dev), lax.rem(gx + 1, nx_dev)
    up, down = lax.rem(gy + ny_dev - 1, ny_dev), lax.rem(gy + 1, ny_dev)

    def own_copy(k):
        source = ctrl_hbm if k == 0 else perts_hbm.at[pl.ds((k - 1) * 4, 4)]
        target = st.at[0] if k == 0 else st.at[pl.ds((k - 1) * 4 + 1, 4)]
        if k == 0:
            return pltpu.make_async_copy(source, target.at[:, pl.ds(HALO, rows), :], in_sem.at[k])
        return pltpu.make_async_copy(source, target.at[:, :, pl.ds(HALO, rows), :], in_sem.at[k])

    barrier = pltpu.get_barrier_semaphore()
    greeted = [(a, b) for a in (left, right) for b in (gy, up, down)] + [(gx, up), (gx, down)]
    greeted += [(lax.rem(gx + d, nx_dev), gy) for d in range(2, nx_dev - 1)]
    greeted += [(gx, lax.rem(gy + d, ny_dev)) for d in range(2, ny_dev - 1)]
    for peer in greeted[:8]:
        pl.semaphore_signal(barrier, inc=1, device_id=peer, device_id_type=MESH)
    for k in range(members // 4 + 1):
        own_copy(k).start()
    for peer in greeted[8:]:
        pl.semaphore_signal(barrier, inc=1, device_id=peer, device_id_type=MESH)

    def y_copies(p, field_ref, st_ref):
        lead = (slice(None),) * (len(field_ref.shape) - 2)
        return [
            pltpu.make_async_remote_copy(
                field_ref.at[lead + (pl.ds(start, HALO),)],
                st_ref.at[lead + (pl.ds(to, HALO),)],
                y_send.at[way, p], y_recv.at[way, p], device_id=(gx, y_to), device_id_type=MESH)
            for way, (start, to, y_to) in enumerate(((0, HALO + rows, up), (rows - HALO, 0, down)))
        ]

    def control_y():
        return y_copies(0, ctrl_hbm, st.at[0])

    def pair_y(p):
        return y_copies(p, perts_hbm.at[pl.ds(2 * p - 2, 2)], st.at[pl.ds(2 * p - 1, 2)])

    for k in range(members // 4 + 1):
        own_copy(k).wait()

    wide = lax.broadcasted_iota(jnp.int32, (rows, 128), 1) // 8

    @pl.loop(0, 3)
    def _(f):
        first = jnp.zeros((rows, 128), jnp.float32)
        last = jnp.zeros((rows, 128), jnp.float32)
        for m in range(members):
            head = st[m + 1, f, HALO : HALO + rows, 0:128]
            tail = st[m + 1, f, HALO : HALO + rows, cols - 128 : cols]
            both = pltpu.roll(jnp.where(wide < 8, head, tail), (8 * m) % 128, 1)
            first = jnp.where(wide == m, both, first)
            last = jnp.where(wide == (m + 15) % 16, both, last)
        pk[0, f] = first
        pk[1, f] = last

    for side in range(2):
        both = jnp.zeros((rows, 128), jnp.float32)
        for f in range(3):
            tile = st[0, f, HALO : HALO + rows, 128 * side : 128 * (side + 1)]
            both = jnp.where(wide == f, pltpu.roll(tile, 8 * (f + side), 1), both)
        pk1[side] = both

    def x_copies(place, tile):
        start, count, to, y_to = ((0, rows, HALO, gy), (0, HALO, HALO + rows, up), (rows - HALO, HALO, 0, down))[place]
        source, target, lead = ((pk, halo, (slice(None),)), (pk1, halo1, ()))[tile]
        return [
            pltpu.make_async_remote_copy(
                source.at[(side,) + lead + (pl.ds(start, count),)],
                target.at[(side,) + lead + (pl.ds(to, count),)],
                x_send.at[side, place, tile], x_recv.at[side, place, tile],
                device_id=(x_to, y_to), device_id_type=MESH)
            for side, x_to in ((0, left), (1, right))
        ]

    everything = [(place, tile) for place in range(3) for tile in (1, 0)]
    pl.semaphore_wait(barrier, len(greeted))

    for key in everything:
        for copy in x_copies(*key):
            copy.start()

    for copy in control_y():
        copy.start()

    @pl.loop(1, pairs)
    def _(p):
        for copy in pair_y(p):
            copy.start()

    grid_rows = rows * ny_dev
    row = gy * rows - HALO + grid_rows + lax.broadcasted_iota(jnp.int32, (ext, 128), 0)
    row = lax.rem(row, grid_rows).astype(jnp.float32)
    cor[...] = TIME_STEP * 0.5 * (1.0 + 0.5 * jnp.sin(2.0 * math.pi * row / float(grid_rows)))

    k_id = lax.rem(lax.broadcasted_iota(jnp.int32, (256, 128), 0), 128)
    ahead = lax.rem(k_id - lax.broadcasted_iota(jnp.int32, (256, 128), 1) + 128, 128)
    weights = jnp.where(ahead == 1, 1.0, jnp.where(ahead == 127, -1.0, 0.0))
    weights = jnp.where(ahead == 2, -0.125, jnp.where(ahead == 126, 0.125, weights))
    band[...] = weights.astype(jnp.bfloat16)

    def of_control(p, rings):
        return [i for i in rings if i in (0, 1, 4)] if isinstance(p, int) else rings

    def assemble(p, starts, rings):
        control = isinstance(p, int)
        states = (0, 0) if control else (2 * p - 1, 2 * p)
        for at in starts:
            pick = slice(at, at + 8)
            state = []
            for f in range(3):
                tiles = [[st[k, f, pick, 128 * i : 128 * (i + 1)] for i in range(2)] for k in states]
                full = {}
                if 0 in rings:
                    for s, k in enumerate(states):
                        if control:
                            ends = (halo1[0, pick, :], halo1[1, pick, :])
                            beyond = jnp.where(lane < 8, pltpu.roll(ends[0], (128 - 8 * f) % 128, 1), pltpu.roll(ends[1], 120 - 8 * f, 1))
                        else:
                            ends = (halo[0, f, pick, :], halo[1, f, pick, :])
                            beyond = pltpu.roll(jnp.where(lane // 8 == k - 1, *ends), lax.rem(136 - 8 * k, 128), 1)
                        full[2 * s] = jnp.where(lane < 120, tiles[s][0], beyond)
                        full[2 * s + 1] = jnp.where(lane < 8, beyond, tiles[s][1])
                if 4 in rings:
                    middle = [jnp.where(lane < 64, high, low) for low, high in tiles]
                    full[4] = jnp.where((lane < 32) | (lane >= 96), middle[0], pltpu.roll(middle[1], 64, 1))
                scale = SCALE * SCALE if f == 0 else SCALE
                if control:
                    full = {i: scale * z + (scale * MEAN_DEPTH if f == 0 else 0.0) for i, z in full.items()}
                    for same in SAME_RING:
                        if same[0] in full:
                            for i in same:
                                cini[f, i, pick] = full[same[0]]
                else:
                    full = {i: cini[f, i, pick] + scale * z for i, z in full.items()}
                state.append(full)
            for i in of_control(p, rings):
                put_state(p, 0, i, at, *(state[f][i] for f in range(3)))

    def put_state(p, stage, i, at, h, e, n):
        for f, z in enumerate((h, e, n, h * n)):
            stages[stage, p, f, i, at : at + 8] = z

    def slopes_x(p, stage, units):
        h, e, n = ([stages[stage, p, f, i, at : at + 8] for i, at in units] for f in range(3))
        z = jnp.concatenate(h + e + n + [u * v for u, v in zip(h, e)], axis=0)
        top = z.astype(jnp.bfloat16)
        rest = (z - top.astype(jnp.float32)).astype(jnp.bfloat16)
        out = jnp.dot(jnp.concatenate([top, rest], axis=1), band[...], preferred_element_type=jnp.float32)
        return out.reshape(4, len(units), 8, 128)

    def slope_y(p, stage, f, i, at):
        z = [stages[stage, p, f, i, at + d : at + d + 8] for d in (-2, -1, 1, 2)]
        return (z[2] - z[1]) - 0.125 * (z[3] - z[0])

    def forward(p, stage, i, at, along):
        h, e, n = (stages[stage, p, f, i, at : at + 8] for f in range(3))
        c = cor[at : at + 8]
        new_h = h - along[3] - slope_y(p, stage, 3, i, at)
        new_e = e - (e * along[1] + n * (slope_y(p, stage, 1, i, at) - c) + along[0])
        new_n = n - (e * (along[2] + c) + n * slope_y(p, stage, 2, i, at) + slope_y(p, stage, 0, i, at))
        return new_h, new_e, new_n

    def evaluate(p, stage, units):
        along = slopes_x(p, stage, units)
        for j, (i, at) in enumerate(units):
            new = forward(p, stage, i, at, along[:, j])
            if stage % 2 == 1:
                new = [0.5 * (stages[stage - 1, p, f, i, at : at + 8] + new[f]) for f in range(3)]
            if stage < 2 * STEPS - 1:
                put_state(p, stage + 1, i, at, *new)
            else:
                for f in range(3):
                    last[p, f, i, at - HALO : at - HALO + 8] = new[f]

    def finish(p, starts):
        for f in range(3):
            scale = 1.0 / (SCALE * SCALE) if f == 0 else 1.0 / SCALE
            for at in starts:
                to = slice(at - HALO, at - HALO + 8)
                if isinstance(p, int):
                    for same in SAME_RING:
                        for i in same:
                            cfin[f, i, to] = last[p, f, same[0], to]
                    continue
                z = [scale * (last[p, f, i, to] - cfin[f, i, to]) for i in ALL_RINGS]
                for s, k in enumerate((2 * p - 1, 2 * p)):
                    both = z[4] if s == 0 else pltpu.roll(z[4], 64, 1)
                    fin[k, f, 0, to, :] = jnp.where(lane < 112, z[2 * s], both)
                    fin[k, f, 1, to, :] = jnp.where(lane < 16, both, z[2 * s + 1])

    def inner(chosen, rings):
        for p in chosen:
            assemble(p, range(HALO, HALO + rows, 8), rings)
        for stage in range(2 * STEPS):
            low, high = HALO + 2 * stage + 2, HALO + rows - 2 * stage - 2
            starts = [min(at, high - 8) for at in range(low, high, 8)]
            for p in chosen:
                for i in of_control(p, rings):
                    evaluate(p, stage, [(i, at) for at in starts])
        if 0 in rings:
            for p in chosen:
                finish(p, starts)

    def edges(chosen):
        for p in chosen:
            assemble(p, (0, HALO + rows), ALL_RINGS)
        for stage in range(2 * STEPS):
            starts = (2 * stage + 2, rows + 2 * HALO - 2 * stage - 10)
            for p in chosen:
                for i in of_control(p, ALL_RINGS):
                    evaluate(p, stage, [(i, at) for at in starts])
        for p in chosen:
            finish(p, starts)

    def bred_out(p):
        return pltpu.make_async_copy(fin.at[pl.ds(2 * p - 1, 2)], bred_hbm.at[pl.ds(2 * p - 2, 2)], out_sem.at[p])

    inner([0], MIDDLE_RING)

    @pl.loop(0, members // 8)
    def _(q):
        inner([4 * q + j for j in range(1, 5)], MIDDLE_RING)

    for copy in x_copies(0, 1):
        copy.wait_recv()
    inner([0], OUTER_RINGS)
    for copy in x_copies(0, 0):
        copy.wait_recv()

    @pl.loop(0, members // 4)
    def _(q):
        inner([2 * q + 1, 2 * q + 2], OUTER_RINGS)

    def products(a, b, cuts, fresh):
        total = [[None] * 4 for _ in range(4)]
        for f in range(3):
            for i in range(2):
                for cut in cuts:
                    x = [fin[1 + 4 * a + u, f, i, cut] for u in range(4)]
                    y = [fin[1 + 4 * b + u, f, i, cut] for u in range(4)]
                    for u in range(4):
                        for v in range(4):
                            z = x[u] * y[v]
                            total[u][v] = z if total[u][v] is None else total[u][v] + z
        if not fresh:
            total = [[parts[4 * a + u, 4 * b + v] + total[u][v] for v in range(4)] for u in range(4)]
        for u in range(4):
            for v in range(4):
                parts[4 * a + u, 4 * b + v] = total[u][v]
                if not fresh:
                    parts[4 * b + v, 4 * a + u] = total[u][v]

    @pl.loop(0, members // 4)
    def _(a):
        @pl.loop(0, a + 1)
        def _(b):
            products(a, b, [slice(at, at + 8) for at in range(8, rows - 8, 8)], True)

    for copy in x_copies(1, 1) + x_copies(2, 1) + control_y():
        copy.wait_recv()
    edges([0])
    for copy in x_copies(1, 0) + x_copies(2, 0):
        copy.wait_recv()

    def edge_products(a):
        @pl.loop(0, a + 1)
        def _(b):
            products(a, b, [slice(0, 8), slice(rows - 8, rows)], False)

    @pl.loop(0, members // 4 - 1)
    def _(q):
        for p in (2 * q + 1, 2 * q + 2):
            for copy in pair_y(p):
                copy.wait_recv()
        edges([2 * q + 1, 2 * q + 2])
        for p in (2 * q + 1, 2 * q + 2):
            bred_out(p).start()

    @pl.loop(0, members // 4 - 1)
    def _(a):
        edge_products(a)

    @pl.loop(pairs - 2, pairs)
    def _(p):
        for copy in pair_y(p):
            copy.wait_recv()
        edges([p])
        bred_out(p).start()

    edge_products(members // 4 - 1)

    row_id = lax.broadcasted_iota(jnp.int32, (members, 128), 0)
    col_id = lax.broadcasted_iota(jnp.int32, (members, 128), 1)
    gram = jnp.zeros((members, 128), jnp.float32)
    for m in range(members):
        sums = jnp.sum(jnp.sum(parts[m], axis=1), axis=1, keepdims=True)
        gram = jnp.where(col_id == m, sums, gram)

    def all_sum(value, buf, me, count, peer_of, send, recv):
        buf[me] = value
        copies = []
        for d in range(1, count):
            copies.append(
                pltpu.make_async_remote_copy(
                    buf.at[me], buf.at[me], send.at[d], recv.at[d],
                    device_id=peer_of(lax.rem(me + d, count)), device_id_type=MESH)
            )
        for copy in copies:
            copy.start()
        for copy in copies:
            copy.wait_recv()
        out = buf[0]
        for d in range(1, count):
            out = out + buf[d]
        return out, copies

    packed = jnp.where(lane < members, gram[0:8], pltpu.roll(gram[8:16], members, 1))
    packed, sent1 = all_sum(packed, red1, gx, nx_dev, lambda i: (i, gy), r1_send, r1_recv)
    packed, sent2 = all_sum(packed, red2, gy, ny_dev, lambda i: (gx, i), r2_send, r2_recv)
    for copy in sent1 + sent2:
        copy.wait_send()
    @pl.loop(1, pairs)
    def _(p):
        bred_out(p).wait()

    for copy in [copy for key in everything for copy in x_copies(*key)] + control_y():
        copy.wait_send()

    @pl.loop(1, pairs)
    def _(p):
        for copy in pair_y(p):
            copy.wait_send()

    gram = jnp.concatenate([packed, pltpu.roll(packed, 128 - members, 1)], axis=0)

    work = jnp.where(col_id < members, gram, jnp.where(col_id - members == row_id, 1.0, 0.0))
    pivots = jnp.ones((members, 1), jnp.float32)
    for k in range(members):
        column = work[:, k : k + 1]
        pivot = column[k : k + 1]
        work = work - jnp.where(row_id > k, column, 0.0) * (work[k : k + 1] * (1.0 / pivot))
        pivots = jnp.where(row_id[:, :1] == k, pivot, pivots)
    factor_ref[...] = work / jnp.sqrt(pivots)


def apply_kernel(length, members, bred_hbm, factor_hbm, basis_hbm, rfac_hbm, bred, factor, table, out, rout, sem):
    first = pltpu.make_async_copy(factor_hbm, factor, sem.at[7])
    first.start()
    parts = [
        pltpu.make_async_copy(bred_hbm.at[:, pl.ds(f, 1), pl.ds(i, 1)], bred.at[:, pl.ds(f, 1), pl.ds(i, 1)], sem.at[8 + 2 * f + i])
        for f in range(3)
        for i in range(2)
    ]
    for copy in parts:
        copy.start()
    first.wait()
    row_id = lax.broadcasted_iota(jnp.int32, (members, members), 0)
    col_id = lax.broadcasted_iota(jnp.int32, (members, members), 1)
    rout[...] = jnp.where(row_id <= col_id, factor[:, :members] * (1.0 / math.sqrt(length)), 0.0)
    small = pltpu.make_async_copy(rout, rfac_hbm, sem.at[6])
    small.start()
    for j in range(members):
        column = factor[:, members + j : members + j + 1] * math.sqrt(length)
        table[j] = jnp.broadcast_to(column, (members, 128))
    copies = []
    for f in range(3):
        for i in range(2):
            parts[2 * f + i].wait()
            x = [bred[j, f, i] for j in range(members)]
            for m in range(members):
                total = table[0, m : m + 1, :] * x[0]
                for j in range(1, m + 1):
                    total = total + table[j, m : m + 1, :] * x[j]
                out[m, f, :, 128 * i : 128 * (i + 1)] = total
            half = (slice(None), pl.ds(f, 1), slice(None), pl.ds(128 * i, 128))
            copies.append(pltpu.make_async_copy(out.at[half], basis_hbm.at[half], sem.at[2 * f + i]))
            copies[-1].start()
    for copy in copies + [small]:
        copy.wait()


def body(control, perts):
    nx_dev, ny_dev = lax.axis_size("gx"), lax.axis_size("gy")
    members, _, rows, cols = perts.shape
    states, ext = members + 1, rows + 2 * HALO
    f32 = jnp.float32
    dma = pltpu.SemaphoreType.DMA
    vmem, hbm = pl.BlockSpec(memory_space=pltpu.VMEM), pl.BlockSpec(memory_space=pltpu.HBM)
    bred, factor = pl.pallas_call(
        functools.partial(kernel, nx_dev, ny_dev, members, rows, cols),
        out_shape=(
            jax.ShapeDtypeStruct((members, 3, 2, rows, 128), f32),
            jax.ShapeDtypeStruct((members, 128), f32),
        ),
        in_specs=[hbm] * 2,
        out_specs=[hbm, vmem],
        scratch_shapes=[
            pltpu.VMEM((states, 3, ext, cols), f32),
            pltpu.VMEM((2, 3, rows, 128), f32),
            pltpu.VMEM((2, 3, ext, 128), f32),
            pltpu.VMEM((2, rows, 128), f32),
            pltpu.VMEM((2, ext, 128), f32),
            pltpu.VMEM((256, 128), jnp.bfloat16),
            pltpu.VMEM((2 * STEPS, members // 2 + 1, 4, 5, ext, 128), f32),
            pltpu.VMEM((members // 2 + 1, 3, 5, rows, 128), f32),
            pltpu.VMEM((3, 5, ext, 128), f32),
            pltpu.VMEM((3, 5, rows, 128), f32),
            pltpu.VMEM((ext, 128), f32),
            pltpu.VMEM((states, 3, 2, rows, 128), f32),
            pltpu.VMEM((members, members, 8, 128), f32),
            pltpu.VMEM((nx_dev, 8, 128), f32),
            pltpu.VMEM((ny_dev, 8, 128), f32),
            dma((members // 4 + 1,)),
            dma((members // 2 + 1,)),
            dma((2, members // 2 + 1)),
            dma((2, members // 2 + 1)),
            dma((2, 3, 2)),
            dma((2, 3, 2)),
            dma((nx_dev,)),
            dma((nx_dev,)),
            dma((ny_dev,)),
            dma((ny_dev,)),
        ],
        compiler_params=pltpu.CompilerParams(
            collective_id=0, has_side_effects=True, vmem_limit_bytes=60 * 1024 * 1024
        ),
    )(control, perts)
    length = float(3 * rows * ny_dev * cols * nx_dev)
    return pl.pallas_call(
        functools.partial(apply_kernel, length, members),
        out_shape=(
            jax.ShapeDtypeStruct(perts.shape, f32),
            jax.ShapeDtypeStruct((members, members), f32),
        ),
        in_specs=[hbm] * 2,
        out_specs=[hbm] * 2,
        scratch_shapes=[
            pltpu.VMEM((members, 3, 2, rows, 128), f32),
            pltpu.VMEM((members, 128), f32),
            pltpu.VMEM((members, members, 128), f32),
            pltpu.VMEM((members, 3, rows, cols), f32),
            pltpu.VMEM((members, members), f32),
            dma((14,)),
        ],
        compiler_params=pltpu.CompilerParams(vmem_limit_bytes=60 * 1024 * 1024),
    )(bred, factor)


def solution(mesh):
    in_specs = (P(None, "gy", "gx"), P(None, None, "gy", "gx"))
    out_specs = (P(None, None, "gy", "gx"), P())
    return jax.shard_map(body, mesh=mesh, in_specs=in_specs, out_specs=out_specs, check_vma=False)
```

```python
import functools
import math

import jax
import jax.numpy as jnp
from jax import lax
from jax.experimental import pallas as pl
from jax.experimental.pallas import tpu as pltpu
from jax.sharding import PartitionSpec as P

MESH = pl.DeviceIdType.MESH
HALO = 8
STEPS = 2
ALL_RINGS, OUTER_RINGS, MIDDLE_RING = (0, 1, 2, 3, 4), (0, 1, 2, 3), (4,)
SAME_RING = ((0, 2), (1, 3), (4,))
MEAN_DEPTH = 4.0
TIME_STEP = 0.1
SCALE = TIME_STEP * (2.0 / 3.0)


def kernel(
    nx_dev, ny_dev, members, rows, cols,
    ctrl_hbm, perts_hbm, bred_hbm, factor_ref,
    st, pk, halo, pk1, halo1, band, stages, last, cini, cfin, cor, fin, parts, red1, red2,
    in_sem, out_sem, y_send, y_recv, x_send, x_recv, r1_send, r1_recv, r2_send, r2_recv,
):
    gx, gy = lax.axis_index("gx"), lax.axis_index("gy")
    ext = rows + 2 * HALO
    pairs = members // 2 + 1
    lane = lax.broadcasted_iota(jnp.int32, (8, 128), 1)
    left, right = lax.rem(gx + nx_dev - 1, nx_dev), lax.rem(gx + 1, nx_dev)
    up, down = lax.rem(gy + ny_dev - 1, ny_dev), lax.rem(gy + 1, ny_dev)

    def own_copy(k):
        source = ctrl_hbm if k == 0 else perts_hbm.at[pl.ds((k - 1) * 4, 4)]
        target = st.at[0] if k == 0 else st.at[pl.ds((k - 1) * 4 + 1, 4)]
        if k == 0:
            return pltpu.make_async_copy(source, target.at[:, pl.ds(HALO, rows), :], in_sem.at[k])
        return pltpu.make_async_copy(source, target.at[:, :, pl.ds(HALO, rows), :], in_sem.at[k])

    barrier = pltpu.get_barrier_semaphore()
    greeted = [(a, b) for a in (left, right) for b in (gy, up, down)] + [(gx, up), (gx, down)]
    greeted += [(lax.rem(gx + d, nx_dev), gy) for d in range(2, nx_dev - 1)]
    greeted += [(gx, lax.rem(gy + d, ny_dev)) for d in range(2, ny_dev - 1)]
    for peer in greeted[:8]:
        pl.semaphore_signal(barrier, inc=1, device_id=peer, device_id_type=MESH)
    for k in range(members // 4 + 1):
        own_copy(k).start()
    for peer in greeted[8:]:
        pl.semaphore_signal(barrier, inc=1, device_id=peer, device_id_type=MESH)

    def y_copies(p, st_ref):
        lead = (slice(None),) * (len(st_ref.shape) - 2)
        return [
            pltpu.make_async_remote_copy(
                st_ref.at[lead + (pl.ds(HALO + start, HALO),)],
                st_ref.at[lead + (pl.ds(to, HALO),)],
                y_send.at[way, p], y_recv.at[way, p], device_id=(gx, y_to), device_id_type=MESH)
            for way, (start, to, y_to) in enumerate(((0, HALO + rows, up), (rows - HALO, 0, down)))
        ]

    def control_y():
        return y_copies(0, st.at[0])

    def pair_y(p):
        return y_copies(p, st.at[pl.ds(2 * p - 1, 2)])

    for k in range(members // 4 + 1):
        own_copy(k).wait()

    wide = lax.broadcasted_iota(jnp.int32, (rows, 128), 1) // 8

    @pl.loop(0, 3)
    def _(f):
        first = jnp.zeros((rows, 128), jnp.float32)
        last = jnp.zeros((rows, 128), jnp.float32)
        for m in range(members):
            head = st[m + 1, f, HALO : HALO + rows, 0:128]
            tail = st[m + 1, f, HALO : HALO + rows, cols - 128 : cols]
            both = pltpu.roll(jnp.where(wide < 8, head, tail), (8 * m) % 128, 1)
            first = jnp.where(wide == m, both, first)
            last = jnp.where(wide == (m + 15) % 16, both, last)
        pk[0, f] = first
        pk[1, f] = last

    for side in range(2):
        both = jnp.zeros((rows, 128), jnp.float32)
        for f in range(3):
            tile = st[0, f, HALO : HALO + rows, 128 * side : 128 * (side + 1)]
            both = jnp.where(wide == f, pltpu.roll(tile, 8 * (f + side), 1), both)
        pk1[side] = both

    def x_copies(place, tile):
        start, count, to, y_to = ((0, rows, HALO, gy), (0, HALO, HALO + rows, up), (rows - HALO, HALO, 0, down))[place]
        source, target, lead = ((pk, halo, (slice(None),)), (pk1, halo1, ()))[tile]
        return [
            pltpu.make_async_remote_copy(
                source.at[(side,) + lead + (pl.ds(start, count),)],
                target.at[(side,) + lead + (pl.ds(to, count),)],
                x_send.at[side, place, tile], x_recv.at[side, place, tile],
                device_id=(x_to, y_to), device_id_type=MESH)
            for side, x_to in ((0, left), (1, right))
        ]

    everything = [(place, tile) for place in range(3) for tile in (1, 0)]
    pl.semaphore_wait(barrier, len(greeted))

    for key in everything:
        for copy in x_copies(*key):
            copy.start()

    for copy in control_y():
        copy.start()

    @pl.loop(1, pairs)
    def _(p):
        for copy in pair_y(p):
            copy.start()

    grid_rows = rows * ny_dev
    row = gy * rows - HALO + grid_rows + lax.broadcasted_iota(jnp.int32, (ext, 128), 0)
    row = lax.rem(row, grid_rows).astype(jnp.float32)
    cor[...] = TIME_STEP * 0.5 * (1.0 + 0.5 * jnp.sin(2.0 * math.pi * row / float(grid_rows)))

    k_id = lax.rem(lax.broadcasted_iota(jnp.int32, (256, 128), 0), 128)
    ahead = lax.rem(k_id - lax.broadcasted_iota(jnp.int32, (256, 128), 1) + 128, 128)
    weights = jnp.where(ahead == 1, 1.0, jnp.where(ahead == 127, -1.0, 0.0))
    weights = jnp.where(ahead == 2, -0.125, jnp.where(ahead == 126, 0.125, weights))
    band[...] = weights.astype(jnp.bfloat16)

    def of_control(p, rings):
        return [i for i in rings if i in (0, 1, 4)] if isinstance(p, int) else rings

    def assemble(p, starts, rings):
        control = isinstance(p, int)
        states = (0, 0) if control else (2 * p - 1, 2 * p)
        for at in starts:
            pick = slice(at, at + 8)
            state = []
            for f in range(3):
                tiles = [[st[k, f, pick, 128 * i : 128 * (i + 1)] for i in range(2)] for k in states]
                full = {}
                if 0 in rings:
                    for s, k in enumerate(states):
                        if control:
                            ends = (halo1[0, pick, :], halo1[1, pick, :])
                            beyond = jnp.where(lane < 8, pltpu.roll(ends[0], (128 - 8 * f) % 128, 1), pltpu.roll(ends[1], 120 - 8 * f, 1))
                        else:
                            ends = (halo[0, f, pick, :], halo[1, f, pick, :])
                            beyond = pltpu.roll(jnp.where(lane // 8 == k - 1, *ends), lax.rem(136 - 8 * k, 128), 1)
                        full[2 * s] = jnp.where(lane < 120, tiles[s][0], beyond)
                        full[2 * s + 1] = jnp.where(lane < 8, beyond, tiles[s][1])
                if 4 in rings:
                    middle = [jnp.where(lane < 64, high, low) for low, high in tiles]
                    full[4] = jnp.where((lane < 32) | (lane >= 96), middle[0], pltpu.roll(middle[1], 64, 1))
                scale = SCALE * SCALE if f == 0 else SCALE
                if control:
                    full = {i: scale * z + (scale * MEAN_DEPTH if f == 0 else 0.0) for i, z in full.items()}
                    for same in SAME_RING:
                        if same[0] in full:
                            for i in same:
                                cini[f, i, pick] = full[same[0]]
                else:
                    full = {i: cini[f, i, pick] + scale * z for i, z in full.items()}
                state.append(full)
            for i in of_control(p, rings):
                put_state(p, 0, i, at, *(state[f][i] for f in range(3)))

    def put_state(p, stage, i, at, h, e, n):
        for f, z in enumerate((h, e, n, h * n)):
            stages[stage, p, f, i, at : at + 8] = z

    def slopes_x(p, stage, units):
        h, e, n = ([stages[stage, p, f, i, at : at + 8] for i, at in units] for f in range(3))
        z = jnp.concatenate(h + e + n + [u * v for u, v in zip(h, e)], axis=0)
        top = z.astype(jnp.bfloat16)
        rest = (z - top.astype(jnp.float32)).astype(jnp.bfloat16)
        out = jnp.dot(jnp.concatenate([top, rest], axis=1), band[...], preferred_element_type=jnp.float32)
        return out.reshape(4, len(units), 8, 128)

    def slope_y(p, stage, f, i, at):
        z = [stages[stage, p, f, i, at + d : at + d + 8] for d in (-2, -1, 1, 2)]
        return (z[2] - z[1]) - 0.125 * (z[3] - z[0])

    def forward(p, stage, i, at, along):
        h, e, n = (stages[stage, p, f, i, at : at + 8] for f in range(3))
        c = cor[at : at + 8]
        new_h = h - along[3] - slope_y(p, stage, 3, i, at)
        new_e = e - (e * along[1] + n * (slope_y(p, stage, 1, i, at) - c) + along[0])
        new_n = n - (e * (along[2] + c) + n * slope_y(p, stage, 2, i, at) + slope_y(p, stage, 0, i, at))
        return new_h, new_e, new_n

    def evaluate(p, stage, units):
        along = slopes_x(p, stage, units)
        for j, (i, at) in enumerate(units):
            new = forward(p, stage, i, at, along[:, j])
            if stage % 2 == 1:
                new = [0.5 * (stages[stage - 1, p, f, i, at : at + 8] + new[f]) for f in range(3)]
            if stage < 2 * STEPS - 1:
                put_state(p, stage + 1, i, at, *new)
            else:
                for f in range(3):
                    last[p, f, i, at - HALO : at - HALO + 8] = new[f]

    def finish(p, starts):
        for f in range(3):
            scale = 1.0 / (SCALE * SCALE) if f == 0 else 1.0 / SCALE
            for at in starts:
                to = slice(at - HALO, at - HALO + 8)
                if isinstance(p, int):
                    for same in SAME_RING:
                        for i in same:
                            cfin[f, i, to] = last[p, f, same[0], to]
                    continue
                z = [scale * (last[p, f, i, to] - cfin[f, i, to]) for i in ALL_RINGS]
                for s, k in enumerate((2 * p - 1, 2 * p)):
                    both = z[4] if s == 0 else pltpu.roll(z[4], 64, 1)
                    fin[k, f, 0, to, :] = jnp.where(lane < 112, z[2 * s], both)
                    fin[k, f, 1, to, :] = jnp.where(lane < 16, both, z[2 * s + 1])

    def inner(chosen, rings):
        for p in chosen:
            assemble(p, range(HALO, HALO + rows, 8), rings)
        for stage in range(2 * STEPS):
            low, high = HALO + 2 * stage + 2, HALO + rows - 2 * stage - 2
            starts = [min(at, high - 8) for at in range(low, high, 8)]
            for p in chosen:
                for i in of_control(p, rings):
                    evaluate(p, stage, [(i, at) for at in starts])
        if 0 in rings:
            for p in chosen:
                finish(p, starts)

    def edges(chosen):
        for p in chosen:
            assemble(p, (0, HALO + rows), ALL_RINGS)
        for stage in range(2 * STEPS):
            starts = (2 * stage + 2, rows + 2 * HALO - 2 * stage - 10)
            for p in chosen:
                for i in of_control(p, ALL_RINGS):
                    evaluate(p, stage, [(i, at) for at in starts])
        for p in chosen:
            finish(p, starts)

    def bred_out(p):
        return pltpu.make_async_copy(fin.at[pl.ds(2 * p - 1, 2)], bred_hbm.at[pl.ds(2 * p - 2, 2)], out_sem.at[p])

    inner([0], MIDDLE_RING)

    @pl.loop(0, members // 8)
    def _(q):
        inner([4 * q + j for j in range(1, 5)], MIDDLE_RING)

    for copy in x_copies(0, 1):
        copy.wait_recv()
    inner([0], OUTER_RINGS)
    for copy in x_copies(0, 0):
        copy.wait_recv()

    @pl.loop(0, members // 4)
    def _(q):
        inner([2 * q + 1, 2 * q + 2], OUTER_RINGS)

    def products(a, b, cuts, fresh):
        total = [[None] * 4 for _ in range(4)]
        for f in range(3):
            for i in range(2):
                for cut in cuts:
                    x = [fin[1 + 4 * a + u, f, i, cut] for u in range(4)]
                    y = [fin[1 + 4 * b + u, f, i, cut] for u in range(4)]
                    for u in range(4):
                        for v in range(4):
                            z = x[u] * y[v]
                            total[u][v] = z if total[u][v] is None else total[u][v] + z
        if not fresh:
            total = [[parts[4 * a + u, 4 * b + v] + total[u][v] for v in range(4)] for u in range(4)]
        for u in range(4):
            for v in range(4):
                parts[4 * a + u, 4 * b + v] = total[u][v]
                if not fresh:
                    parts[4 * b + v, 4 * a + u] = total[u][v]

    @pl.loop(0, members // 4)
    def _(a):
        @pl.loop(0, a + 1)
        def _(b):
            products(a, b, [slice(at, at + 8) for at in range(8, rows - 8, 8)], True)

    for copy in x_copies(1, 1) + x_copies(2, 1) + control_y():
        copy.wait_recv()
    edges([0])
    for copy in x_copies(1, 0) + x_copies(2, 0):
        copy.wait_recv()

    @pl.loop(0, members // 4)
    def _(q):
        for p in (2 * q + 1, 2 * q + 2):
            for copy in pair_y(p):
                copy.wait_recv()
        edges([2 * q + 1, 2 * q + 2])
        for p in (2 * q + 1, 2 * q + 2):
            bred_out(p).start()

    @pl.loop(0, members // 4)
    def _(a):
        @pl.loop(0, a + 1)
        def _(b):
            products(a, b, [slice(0, 8), slice(rows - 8, rows)], False)

    row_id = lax.broadcasted_iota(jnp.int32, (members, 128), 0)
    col_id = lax.broadcasted_iota(jnp.int32, (members, 128), 1)
    gram = jnp.zeros((members, 128), jnp.float32)
    for m in range(members):
        sums = jnp.sum(jnp.sum(parts[m], axis=1), axis=1, keepdims=True)
        gram = jnp.where(col_id == m, sums, gram)

    def all_sum(value, buf, me, count, peer_of, send, recv):
        buf[me] = value
        copies = []
        for d in range(1, count):
            copies.append(
                pltpu.make_async_remote_copy(
                    buf.at[me], buf.at[me], send.at[d], recv.at[d],
                    device_id=peer_of(lax.rem(me + d, count)), device_id_type=MESH)
            )
        for copy in copies:
            copy.start()
        for copy in copies:
            copy.wait_recv()
        out = buf[0]
        for d in range(1, count):
            out = out + buf[d]
        return out, copies

    packed = jnp.where(lane < members, gram[0:8], pltpu.roll(gram[8:16], members, 1))
    packed, sent1 = all_sum(packed, red1, gx, nx_dev, lambda i: (i, gy), r1_send, r1_recv)
    packed, sent2 = all_sum(packed, red2, gy, ny_dev, lambda i: (gx, i), r2_send, r2_recv)
    for copy in sent1 + sent2:
        copy.wait_send()
    @pl.loop(1, pairs)
    def _(p):
        bred_out(p).wait()

    for copy in [copy for key in everything for copy in x_copies(*key)] + control_y():
        copy.wait_send()

    @pl.loop(1, pairs)
    def _(p):
        for copy in pair_y(p):
            copy.wait_send()

    gram = jnp.concatenate([packed, pltpu.roll(packed, 128 - members, 1)], axis=0)

    work = jnp.where(col_id < members, gram, jnp.where(col_id - members == row_id, 1.0, 0.0))
    pivots = jnp.ones((members, 1), jnp.float32)
    for k in range(members):
        column = work[:, k : k + 1]
        pivot = column[k : k + 1]
        work = work - jnp.where(row_id > k, column, 0.0) * (work[k : k + 1] * (1.0 / pivot))
        pivots = jnp.where(row_id[:, :1] == k, pivot, pivots)
    factor_ref[...] = work / jnp.sqrt(pivots)


def apply_kernel(length, members, bred_hbm, factor_hbm, basis_hbm, rfac_hbm, bred, factor, table, out, rout, sem):
    first = pltpu.make_async_copy(factor_hbm, factor, sem.at[7])
    first.start()
    parts = [
        pltpu.make_async_copy(bred_hbm.at[:, pl.ds(f, 1), pl.ds(i, 1)], bred.at[:, pl.ds(f, 1), pl.ds(i, 1)], sem.at[8 + 2 * f + i])
        for f in range(3)
        for i in range(2)
    ]
    for copy in parts:
        copy.start()
    first.wait()
    row_id = lax.broadcasted_iota(jnp.int32, (members, members), 0)
    col_id = lax.broadcasted_iota(jnp.int32, (members, members), 1)
    rout[...] = jnp.where(row_id <= col_id, factor[:, :members] * (1.0 / math.sqrt(length)), 0.0)
    small = pltpu.make_async_copy(rout, rfac_hbm, sem.at[6])
    small.start()
    for j in range(members):
        column = factor[:, members + j : members + j + 1] * math.sqrt(length)
        table[j] = jnp.broadcast_to(column, (members, 128))
    copies = []
    for f in range(3):
        for i in range(2):
            parts[2 * f + i].wait()
            x = [bred[j, f, i] for j in range(members)]
            for m in range(members):
                total = table[0, m : m + 1, :] * x[0]
                for j in range(1, m + 1):
                    total = total + table[j, m : m + 1, :] * x[j]
                out[m, f, :, 128 * i : 128 * (i + 1)] = total
            half = (slice(None), pl.ds(f, 1), slice(None), pl.ds(128 * i, 128))
            copies.append(pltpu.make_async_copy(out.at[half], basis_hbm.at[half], sem.at[2 * f + i]))
            copies[-1].start()
    for copy in copies + [small]:
        copy.wait()


def body(control, perts):
    nx_dev, ny_dev = lax.axis_size("gx"), lax.axis_size("gy")
    members, _, rows, cols = perts.shape
    states, ext = members + 1, rows + 2 * HALO
    f32 = jnp.float32
    dma = pltpu.SemaphoreType.DMA
    vmem, hbm = pl.BlockSpec(memory_space=pltpu.VMEM), pl.BlockSpec(memory_space=pltpu.HBM)
    bred, factor = pl.pallas_call(
        functools.partial(kernel, nx_dev, ny_dev, members, rows, cols),
        out_shape=(
            jax.ShapeDtypeStruct((members, 3, 2, rows, 128), f32),
            jax.ShapeDtypeStruct((members, 128), f32),
        ),
        in_specs=[hbm] * 2,
        out_specs=[hbm, vmem],
        scratch_shapes=[
            pltpu.VMEM((states, 3, ext, cols), f32),
            pltpu.VMEM((2, 3, rows, 128), f32),
            pltpu.VMEM((2, 3, ext, 128), f32),
            pltpu.VMEM((2, rows, 128), f32),
            pltpu.VMEM((2, ext, 128), f32),
            pltpu.VMEM((256, 128), jnp.bfloat16),
            pltpu.VMEM((2 * STEPS, members // 2 + 1, 4, 5, ext, 128), f32),
            pltpu.VMEM((members // 2 + 1, 3, 5, rows, 128), f32),
            pltpu.VMEM((3, 5, ext, 128), f32),
            pltpu.VMEM((3, 5, rows, 128), f32),
            pltpu.VMEM((ext, 128), f32),
            pltpu.VMEM((states, 3, 2, rows, 128), f32),
            pltpu.VMEM((members, members, 8, 128), f32),
            pltpu.VMEM((nx_dev, 8, 128), f32),
            pltpu.VMEM((ny_dev, 8, 128), f32),
            dma((members // 4 + 1,)),
            dma((members // 2 + 1,)),
            dma((2, members // 2 + 1)),
            dma((2, members // 2 + 1)),
            dma((2, 3, 2)),
            dma((2, 3, 2)),
            dma((nx_dev,)),
            dma((nx_dev,)),
            dma((ny_dev,)),
            dma((ny_dev,)),
        ],
        compiler_params=pltpu.CompilerParams(
            collective_id=0, has_side_effects=True, vmem_limit_bytes=60 * 1024 * 1024
        ),
    )(control, perts)
    length = float(3 * rows * ny_dev * cols * nx_dev)
    return pl.pallas_call(
        functools.partial(apply_kernel, length, members),
        out_shape=(
            jax.ShapeDtypeStruct(perts.shape, f32),
            jax.ShapeDtypeStruct((members, members), f32),
        ),
        in_specs=[hbm] * 2,
        out_specs=[hbm] * 2,
        scratch_shapes=[
            pltpu.VMEM((members, 3, 2, rows, 128), f32),
            pltpu.VMEM((members, 128), f32),
            pltpu.VMEM((members, members, 128), f32),
            pltpu.VMEM((members, 3, rows, cols), f32),
            pltpu.VMEM((members, members), f32),
            dma((14,)),
        ],
        compiler_params=pltpu.CompilerParams(vmem_limit_bytes=60 * 1024 * 1024),
    )(bred, factor)


def solution(mesh):
    in_specs = (P(None, "gy", "gx"), P(None, None, "gy", "gx"))
    out_specs = (P(None, None, "gy", "gx"), P())
    return jax.shard_map(body, mesh=mesh, in_specs=in_specs, out_specs=out_specs, check_vma=False)
```
